32 devices in a mesh: head: 4 (over x, core), ctx: 8 (over z, y).
Axes of the slice: x: 2, y: 2, z: 4, core: 2. Of those that a mesh axis runs over, the one named last changes fastest.
Arguments:
- queries: bfloat16 [8192, 4096], P('ctx', 'head'), may hold values from -108 to 108
- key_states: bfloat16 [8192, 1024], P(('ctx', 'head')), may hold values from -9 to 9
- value_states: bfloat16 [8192, 1024], P(('ctx', 'head')), may hold values from -6 to 6
- block_lists: int32 [128, 8], P('ctx'), may hold values from 0 to 127, as said below
- out_grad: bfloat16 [8192, 4096], P('ctx', 'head'), may hold values from -12 to 12
Outputs:
- attended: bfloat16 [8192, 4096], P('ctx', 'head')
- query_grad: bfloat16 [8192, 4096], P('ctx', 'head')
- key_grad: bfloat16 [8192, 1024], P(('ctx', 'head'))
- value_grad: bfloat16 [8192, 1024], P(('ctx', 'head'))
The draws below stay inside these ranges and needn't reach their ends.
Inputs may be any that keep to these rules, and one draw needn't show every extreme that they name: `block_lists`: row i's first entry is i and every entry is at most i (repeats allowed). The lists of the 16 query blocks of one ctx index c name at most 3 distinct blocks held by any other ctx index (index c holds blocks c * 16 to c * 16 + 15).
All inputs are finite; a program needn't handle non-finite values.
Results may differ from the reference program's by a relative error of at most 0.04.
Values may be sent and summed in bfloat16 or wider, within the bound.
No kernel may reach another device: no remote copies, remote signals or barrier semaphores. Data moves between devices by JAX's collectives and lax.ppermute only.
A program may use at most 128 MiB of HBM per device.

```python
import jax
import jax.numpy as jnp
from jax import lax

HEADS = 32
KV_HEADS = 8
HEAD_DIM = 128
GROUP = 4
BLK = 64
LIST = 8
CAP = 3
QB_DEV = 16
SEQ = 8192
NBLOCKS = 128


def shared_keys(key):
    base = 1.5 * jax.random.normal(jax.random.fold_in(key, 7), (SEQ, KV_HEADS * HEAD_DIM), jnp.float32)
    base = jnp.clip(base, -9.0, 9.0)
    return base


def draw_key_states(key, part):
    return shared_keys(key).astype(jnp.bfloat16)


def draw_queries(key, part):
    drawn = jnp.clip(1.5 * jax.random.normal(jax.random.fold_in(key, 9), (SEQ, HEADS * HEAD_DIM), jnp.float32), -9.0, 9.0)
    return drawn.astype(jnp.bfloat16)


def draw_block_lists(key, part):
    shard_count = NBLOCKS // QB_DEV
    slots = QB_DEV * (LIST - 1)
    pool_size = shard_count * CAP
    keys_all = jax.random.split(key, 6)
    picks = jax.random.randint(keys_all[0], (shard_count, shard_count, QB_DEV), 0, 1 << 20) * QB_DEV + jnp.arange(QB_DEV)
    chosen = jnp.argsort(picks, axis=2)[:, :, :CAP]
    owners = jnp.arange(shard_count)
    pool = (owners[None, :, None] * QB_DEV + chosen).reshape(shard_count, pool_size)
    valid = jnp.broadcast_to(owners[None, :, None] < owners[:, None, None], (shard_count, shard_count, CAP)).reshape(shard_count, pool_size)
    order_score = jnp.where(valid, jax.random.randint(keys_all[1], (shard_count, pool_size), 0, 1 << 20), 1 << 21)
    order_score = order_score * pool_size + jnp.arange(pool_size)
    pool_sorted = jnp.take_along_axis(pool, jnp.argsort(order_score, axis=1), axis=1)
    count = CAP * owners
    slot_ids = jnp.arange(slots)
    random_pick = jax.random.randint(keys_all[2], (shard_count, slots), 0, 1 << 20) % jnp.maximum(count, 1)[:, None]
    pool_index = jnp.where(slot_ids[None, :] < count[:, None], slot_ids[None, :], random_pick)
    remote_blocks = jnp.take_along_axis(pool_sorted, pool_index, axis=1)
    shuffle_score = jax.random.randint(keys_all[3], (shard_count, slots), 0, 1 << 20) * slots + slot_ids
    shuffle = jnp.argsort(shuffle_score, axis=1)
    remote_blocks = jnp.take_along_axis(remote_blocks, shuffle, axis=1)
    covering = jnp.take_along_axis(jnp.broadcast_to(slot_ids[None, :] < count[:, None], (shard_count, slots)), shuffle, axis=1)
    coin = jax.random.randint(keys_all[4], (shard_count, slots), 0, 2) == 0
    use_remote = (count[:, None] > 0) & (covering | coin)
    local_block = jnp.broadcast_to(slot_ids[None, :] // (LIST - 1), (shard_count, slots))
    local_pick = jax.random.randint(keys_all[5], (shard_count, slots), 0, local_block + 1)
    local_ids = owners[:, None] * QB_DEV + local_pick
    others = jnp.where(use_remote, remote_blocks, local_ids).reshape(NBLOCKS, LIST - 1)
    return jnp.concatenate([jnp.arange(NBLOCKS)[:, None], others], axis=1).astype(jnp.int32)


def steps_of(key, shape, cuts, smallest, top_value):
    factor_of, own = 1.0, jax.random.fold_in(key, 6)
    for axis_at, parts in cuts:
        steps = jnp.exp(jax.random.uniform(jax.random.fold_in(own, axis_at), (parts,), jnp.float32, smallest / len(cuts), top_value / len(cuts)))
        factor_of = factor_of * jnp.repeat(steps, shape[axis_at] // parts).reshape([-1 if axis == axis_at else 1 for axis in range(len(shape))])
    return factor_of


def scatter_about(rng, extent, scale, limit, pieces=(), held_as=jnp.bfloat16):
    factor_of = steps_of(rng, extent, pieces, -0.22, 0.18) if pieces else 1.0
    result = jax.random.normal(rng, extent, jnp.float32) * scale * factor_of
    return jnp.minimum(jnp.maximum(result, -limit), limit).astype(held_as)


def setup_inputs(seed: int = 0) -> dict:
    keys = jax.random.split(jax.random.key(seed), 6)
    return {
        "queries": draw_queries(jax.random.fold_in(keys[5], 71), 0),
        "key_states": draw_key_states(jax.random.fold_in(keys[5], 71), 0),
        "value_states": scatter_about(keys[2], (SEQ, KV_HEADS * HEAD_DIM), 1.0, 6.0, ((0, 32),)),
        "block_lists": draw_block_lists(jax.random.fold_in(keys[5], 71), 0),
        "out_grad": scatter_about(keys[4], (SEQ, HEADS * HEAD_DIM), 2.0, 12.0, ((0, 8), (1, 4))),
    }


NEG_FILL = -1.0e30


def round_bf16(values):
    return lax.optimization_barrier(values.astype(jnp.bfloat16)).astype(jnp.float32)


def reference(queries, key_states, value_states, block_lists, out_grad):
    softmax_scale = HEAD_DIM ** -0.5
    query_blocks = queries.astype(jnp.float32).reshape(NBLOCKS, BLK, KV_HEADS, GROUP, HEAD_DIM)
    grad_blocks = out_grad.astype(jnp.float32).reshape(NBLOCKS, BLK, KV_HEADS, GROUP, HEAD_DIM)
    key_blocks = key_states.astype(jnp.float32).reshape(NBLOCKS, BLK, KV_HEADS, HEAD_DIM)
    value_blocks = value_states.astype(jnp.float32).reshape(NBLOCKS, BLK, KV_HEADS, HEAD_DIM)
    offsets = jnp.arange(BLK, dtype=jnp.int32)

    def visit(carry, index):
        key_acc, value_acc = carry
        listed = block_lists[index]
        key_rows = key_blocks[listed].reshape(LIST * BLK, KV_HEADS, HEAD_DIM)
        value_rows = value_blocks[listed].reshape(LIST * BLK, KV_HEADS, HEAD_DIM)
        query_rows = query_blocks[index]
        grad_rows = grad_blocks[index]
        scores = jnp.einsum('tkgd,skd->kgts', query_rows, key_rows) * softmax_scale
        key_pos = (listed[:, None] * BLK + offsets[None, :]).reshape(-1)
        query_pos = index * BLK + offsets
        visible = key_pos[None, :] <= query_pos[:, None]
        scores = jnp.where(visible, scores, NEG_FILL)
        row_peak = jnp.max(scores, axis=-1, keepdims=True)
        expo = jnp.exp(scores - row_peak)
        attn_probs = expo / jnp.sum(expo, axis=-1, keepdims=True)
        probs_low = round_bf16(attn_probs)
        attended = round_bf16(jnp.einsum('kgts,skd->tkgd', probs_low, value_rows))
        row_delta = jnp.transpose(jnp.sum(grad_rows * attended, axis=-1), (1, 2, 0))[..., None]
        dprob = jnp.einsum('tkgd,skd->kgts', grad_rows, value_rows)
        dscore = round_bf16(attn_probs * (dprob - row_delta))
        query_part = jnp.einsum('kgts,skd->tkgd', dscore, key_rows) * softmax_scale
        key_part = jnp.einsum('kgts,tkgd->skd', dscore, query_rows) * softmax_scale
        value_part = jnp.einsum('kgts,tkgd->skd', probs_low, grad_rows)
        key_acc = key_acc.at[listed].add(key_part.reshape(LIST, BLK, KV_HEADS, HEAD_DIM))
        value_acc = value_acc.at[listed].add(value_part.reshape(LIST, BLK, KV_HEADS, HEAD_DIM))
        return (key_acc, value_acc), (attended.astype(jnp.bfloat16), query_part.astype(jnp.bfloat16))

    zeros = jnp.zeros((NBLOCKS, BLK, KV_HEADS, HEAD_DIM), jnp.float32)
    (key_acc, value_acc), (attended, query_grad) = lax.scan(visit, (zeros, zeros), jnp.arange(NBLOCKS, dtype=jnp.int32))
    return (attended.reshape(SEQ, HEADS * HEAD_DIM),
            query_grad.reshape(SEQ, HEADS * HEAD_DIM),
            key_acc.reshape(SEQ, KV_HEADS * HEAD_DIM).astype(jnp.bfloat16),
            value_acc.reshape(SEQ, KV_HEADS * HEAD_DIM).astype(jnp.bfloat16))
```

```python
import functools

import jax
import jax.numpy as jnp
from jax import lax
from jax.experimental import pallas as pl
from jax.experimental.pallas import tpu as pltpu
from jax.sharding import PartitionSpec as P

HEAD_DIM = 128
GROUP = 4
BLK = 64
LIST = 8
CAP = 3
STEP_BLOCKS = 2
NEG_FILL = -1e30
SCALE = HEAD_DIM ** (-0.5)
LOG2E = 1.4426950408889634
VMEM_LIMIT = 50 * 1024 * 1024

NT = (((1,), (1,)), ((), ()))
NN = (((1,), (0,)), ((), ()))
TN = (((0,), (0,)), ((), ()))


def dot(a, b, dims):
    return lax.dot_general(a, b, dims, preferred_element_type=jnp.float32)


def params(**kw):
    return pltpu.CompilerParams(vmem_limit_bytes=VMEM_LIMIT, **kw)


def pick_kernel(asked, own, out):
    per_quarter = own.shape[2] // BLK
    for c in range(out.shape[0]):
        for s in range(CAP):
            block = asked[c * CAP + s]
            quarter = block // per_quarter
            row = pl.multiple_of((block % per_quarter) * BLK, BLK)
            for kv in range(2):
                out[c, kv, s] = own[quarter, kv, pl.ds(row, BLK), :]


def attend_kernel(source, q_ref, g_ref, own, far, *rest):
    o_ref, dq_ref, near_out, far_out, table, total = rest[-6:]
    step = pl.program_id(0)
    heads, _, quarter_rows, _ = own.shape
    per_quarter = quarter_rows // BLK
    blocks_here = heads * per_quarter
    shard_count = far.shape[0]

    @pl.when(step == 0)
    def _():
        for kv in range(2):
            for quarter in range(heads):
                for j in range(per_quarter):
                    table[kv, quarter * per_quarter + j] = own[quarter, kv, j * BLK : (j + 1) * BLK, :]
            for c in range(shard_count):
                for s in range(CAP):
                    table[kv, blocks_here + c * CAP + s] = far[c, kv, s]
        total[...] = jnp.zeros_like(total)

    key_row = lax.broadcasted_iota(jnp.int32, (BLK, GROUP * BLK), 0)
    query_col = lax.broadcasted_iota(jnp.int32, (BLK, GROUP * BLK), 1) % BLK
    hidden = key_row > query_col
    for sub in range(STEP_BLOCKS):
        block = step * STEP_BLOCKS + sub
        rows = slice(sub * BLK, (sub + 1) * BLK)
        listed = [source[block * LIST + e] for e in range(LIST)]
        q = jnp.concatenate([q_ref[rows, g * HEAD_DIM : (g + 1) * HEAD_DIM] for g in range(GROUP)], axis=0)
        g_out = jnp.concatenate([g_ref[rows, g * HEAD_DIM : (g + 1) * HEAD_DIM] for g in range(GROUP)], axis=0)
        keys = jnp.concatenate([table[0, at] for at in listed], axis=0)
        values = jnp.concatenate([table[1, at] for at in listed], axis=0)
        scores = dot(keys, q, NT)
        parts = []
        for e in range(LIST):
            part = scores[e * BLK : (e + 1) * BLK]
            mask = hidden if e == 0 else hidden & (listed[e] == block)
            parts.append(jnp.where(mask, NEG_FILL, part))
        scores = jnp.concatenate(parts, axis=0)
        peak = jnp.max(scores, axis=0, keepdims=True)
        expo = jnp.exp2((scores - peak) * (SCALE * LOG2E))
        probs = expo * (1.0 / jnp.sum(expo, axis=0, keepdims=True))
        probs_low = probs.astype(jnp.bfloat16)
        dprob = dot(values, g_out, NT)
        delta = jnp.sum(probs * dprob, axis=0, keepdims=True)
        dscore = (probs * (dprob - delta)).astype(jnp.bfloat16)
        attended = dot(values, probs_low, TN).T.astype(jnp.bfloat16)
        dq = (dot(keys, dscore, TN) * SCALE).T.astype(jnp.bfloat16)
        for g in range(GROUP):
            cols = slice(g * HEAD_DIM, (g + 1) * HEAD_DIM)
            o_ref[rows, cols] = attended[g * BLK : (g + 1) * BLK]
            dq_ref[rows, cols] = dq[g * BLK : (g + 1) * BLK]
        dk = dot(dscore, q, NN)
        dv = dot(probs_low, g_out, NN)
        for e in range(LIST):
            total[0, listed[e]] += dk[e * BLK : (e + 1) * BLK]
            total[1, listed[e]] += dv[e * BLK : (e + 1) * BLK]

    @pl.when(step == pl.num_programs(0) - 1)
    def _():
        for kv, factor in ((0, SCALE), (1, 1.0)):
            near_out[kv] = total[kv, :blocks_here] * factor
            for c in range(shard_count):
                first = blocks_here + c * CAP
                far_out[c, kv] = (total[kv, first : first + CAP] * factor).astype(jnp.bfloat16)


def gather_sum_kernel(asked, near, back, out, total):
    heads, _, quarter_rows, _ = out.shape
    per_quarter = quarter_rows // BLK
    total[...] = near[...]
    for c in range(back.shape[0]):
        for s in range(CAP):
            block = asked[c * CAP + s]
            for kv in range(2):
                total[kv, block] += back[c, kv, s].astype(jnp.float32)
    for quarter in range(heads):
        for kv in range(2):
            for j in range(per_quarter):
                out[quarter, kv, j * BLK : (j + 1) * BLK, :] = total[kv, quarter * per_quarter + j].astype(jnp.bfloat16)


def whole(shape):
    return pl.BlockSpec(shape, lambda *_: (0,) * len(shape))


def pick(asked, own, shard_count):
    shape = (shard_count, 2, CAP, BLK, HEAD_DIM)
    return pl.pallas_call(
        pick_kernel,
        grid_spec=pltpu.PrefetchScalarGridSpec(
            num_scalar_prefetch=1, grid=(1,), in_specs=[whole(own.shape)], out_specs=whole(shape)
        ),
        out_shape=jax.ShapeDtypeStruct(shape, jnp.bfloat16),
        compiler_params=params(),
        name="pick",
    )(asked, own)


def attend(source, queries, out_grad, own, far, head, earlier):
    tokens_here, width = queries.shape
    blocks_here = tokens_here // BLK
    slots = blocks_here + far.shape[0] * CAP
    tile = pl.BlockSpec((STEP_BLOCKS * BLK, GROUP * HEAD_DIM), lambda i, *_: (i, head))
    near_shape = (2, blocks_here, BLK, HEAD_DIM)
    aliases = {5: 0, 6: 1} if earlier else {}
    return pl.pallas_call(
        attend_kernel,
        grid_spec=pltpu.PrefetchScalarGridSpec(
            num_scalar_prefetch=1,
            grid=(blocks_here // STEP_BLOCKS,),
            in_specs=[tile, tile, whole(own.shape), whole(far.shape)]
            + [pl.BlockSpec(memory_space=pl.ANY)] * len(earlier),
            out_specs=[tile, tile, whole(near_shape), whole(far.shape)],
            scratch_shapes=[
                pltpu.VMEM((2, slots, BLK, HEAD_DIM), jnp.bfloat16),
                pltpu.VMEM((2, slots, BLK, HEAD_DIM), jnp.float32),
            ],
        ),
        out_shape=[
            jax.ShapeDtypeStruct((tokens_here, width), jnp.bfloat16),
            jax.ShapeDtypeStruct((tokens_here, width), jnp.bfloat16),
            jax.ShapeDtypeStruct(near_shape, jnp.float32),
            jax.ShapeDtypeStruct(far.shape, jnp.bfloat16),
        ],
        input_output_aliases=aliases,
        compiler_params=params(),
        cost_estimate=pl.CostEstimate(
            flops=12 * blocks_here * LIST * BLK * GROUP * BLK * HEAD_DIM,
            bytes_accessed=20 * 1024 * 1024,
            transcendentals=blocks_here * LIST * BLK * GROUP * BLK,
        ),
        name="attend",
    )(source, queries, out_grad, own, far, *earlier)


def gather_sum(asked, near, back, shape):
    return pl.pallas_call(
        gather_sum_kernel,
        grid_spec=pltpu.PrefetchScalarGridSpec(
            num_scalar_prefetch=1,
            grid=(1,),
            in_specs=[whole(near.shape), whole(back.shape)],
            out_specs=whole(shape),
            scratch_shapes=[pltpu.VMEM(near.shape, jnp.float32)],
        ),
        out_shape=jax.ShapeDtypeStruct(shape, jnp.bfloat16),
        compiler_params=params(),
        name="gather_sum",
    )(asked, near, back)


def swap(x, axis):
    return lax.all_to_all(x, axis, split_axis=0, concat_axis=0, tiled=True)


def per_device(queries, key_states, value_states, block_lists, out_grad):
    shard_index = lax.axis_index("ctx")
    shard_count = lax.axis_size("ctx")
    heads = lax.axis_size("head")
    tokens_here = queries.shape[0]
    blocks_here = tokens_here // BLK
    quarter = key_states.shape[0]
    head_count = key_states.shape[1] // heads // HEAD_DIM

    flat_ids = block_lists.reshape(-1)
    owner_shard = flat_ids // blocks_here
    inner_index = flat_ids % blocks_here
    every_block = jnp.arange(shard_count * blocks_here, dtype=jnp.int32)
    block_hits = jnp.any(flat_ids[:, None] == every_block[None, :], axis=0).reshape(shard_count, blocks_here)
    needed = block_hits & (jnp.arange(shard_count) != shard_index)[:, None]
    slot_rank = jnp.cumsum(needed.astype(jnp.int32), axis=1) - 1
    slot_pick = needed[:, :, None] & (slot_rank[:, :, None] == jnp.arange(CAP)[None, None, :])
    requests = jnp.sum(jnp.where(slot_pick, jnp.arange(blocks_here, dtype=jnp.int32)[None, :, None], 0), axis=1)
    ref_rank = jnp.sum(
        jnp.where(flat_ids[:, None] == every_block[None, :], slot_rank.reshape(-1)[None, :], 0), axis=1
    )
    source = jnp.where(owner_shard == shard_index, inner_index, blocks_here + owner_shard * CAP + ref_rank)
    asked = swap(requests, "ctx").reshape(-1)

    key_parts = key_states.reshape(quarter, heads, head_count, HEAD_DIM)
    value_parts = value_states.reshape(quarter, heads, head_count, HEAD_DIM)
    both = jnp.stack([key_parts, value_parts])
    own, far = [], []
    for h in range(head_count):
        own.append(swap(jnp.transpose(both[:, :, :, h], (2, 0, 1, 3)), "head"))
    for h in range(head_count):
        far.append(swap(pick(asked, own[h], shard_count), "ctx"))
    earlier, nears, backs = [], [], []
    for h in range(head_count):
        attended, query_grad, near, far_grad = attend(source, queries, out_grad, own[h], far[h], h, earlier)
        earlier = [attended, query_grad]
        nears.append(near)
        backs.append(swap(far_grad, "ctx"))
    done = []
    for h in range(head_count):
        done.append(swap(gather_sum(asked, nears[h], backs[h], own[h].shape), "head"))
    grads = jnp.stack(done)
    key_grad = jnp.transpose(grads[:, :, 0], (2, 1, 0, 3)).reshape(quarter, -1)
    value_grad = jnp.transpose(grads[:, :, 1], (2, 1, 0, 3)).reshape(quarter, -1)
    return attended, query_grad, key_grad, value_grad


def solution(mesh):
    return jax.shard_map(
        per_device,
        mesh=mesh,
        in_specs=(
            P("ctx", "head"),
            P(("ctx", "head"), None),
            P(("ctx", "head"), None),
            P("ctx", None),
            P("ctx", "head"),
        ),
        out_specs=(
            P("ctx", "head"),
            P("ctx", "head"),
            P(("ctx", "head"), None),
            P(("ctx", "head"), None),
        ),
        check_vma=False,
    )
```

```python
import functools

import jax
import jax.numpy as jnp
from jax import lax
from jax.experimental import pallas as pl
from jax.experimental.pallas import tpu as pltpu
from jax.sharding import PartitionSpec as P

HEAD_DIM = 128
GROUP = 4
BLK = 64
LIST = 8
CAP = 3
STEP_BLOCKS = 2
NEG_FILL = -1e30
SCALE = HEAD_DIM ** (-0.5)
LOG2E = 1.4426950408889634
VMEM_LIMIT = 50 * 1024 * 1024

NT = (((1,), (1,)), ((), ()))
NN = (((1,), (0,)), ((), ()))
TN = (((0,), (0,)), ((), ()))


def dot(a, b, dims):
    return lax.dot_general(a, b, dims, preferred_element_type=jnp.float32)


def params(**kw):
    return pltpu.CompilerParams(vmem_limit_bytes=VMEM_LIMIT, **kw)


def split_kernel(place, *refs):
    k_ref, v_ref, *outs = refs
    heads = len(outs)
    me = place[1]
    h = place[2]
    head_count = k_ref.shape[1] // heads // HEAD_DIM
    for r, out in enumerate(outs):
        peer = lax.rem(me + r, heads)
        col = pl.multiple_of((peer * head_count + h) * HEAD_DIM, HEAD_DIM)
        out[0] = k_ref[:, pl.ds(col, HEAD_DIM)]
        out[1] = v_ref[:, pl.ds(col, HEAD_DIM)]


def fill_table(place, own, table):
    heads = len(own)
    per_quarter = own[0].shape[1] // BLK
    for r in range(heads):
        first = lax.rem(place[1] + heads - r, heads) * per_quarter
        for kv in range(2):
            for j in range(per_quarter):
                table[kv, first + j] = own[r][kv, j * BLK : (j + 1) * BLK, :]


def pick_kernel(place, asked, *refs, heads):
    own, (*outs, table) = refs[:heads], refs[heads:]
    fill_table(place, own, table)
    shard_count = len(outs) + 1
    for d, out in enumerate(outs, 1):
        c = lax.rem(place[0] + d, shard_count)
        for s in range(CAP):
            block = asked[c * CAP + s]
            for kv in range(2):
                out[kv, s] = table[kv, block]


def attend_kernel(place, source, q_ref, g_ref, *refs, heads, steps):
    own, far = refs[:heads], refs[heads : heads + steps]
    table, total = refs[-2:]
    far_out = refs[-2 - steps : -2]
    o_ref, dq_ref, near_out = refs[-5 - steps : -2 - steps]
    step = pl.program_id(0)
    blocks_here = near_out.shape[1]

    @pl.when(step == 0)
    def _():
        fill_table(place, own, table)
        for kv in range(2):
            for d in range(steps):
                for s in range(CAP):
                    table[kv, blocks_here + d * CAP + s] = far[d][kv, s]
        total[...] = jnp.zeros_like(total)

    key_row = lax.broadcasted_iota(jnp.int32, (BLK, GROUP * BLK), 0)
    query_col = lax.broadcasted_iota(jnp.int32, (BLK, GROUP * BLK), 1) % BLK
    hidden = key_row > query_col
    for sub in range(STEP_BLOCKS):
        block = step * STEP_BLOCKS + sub
        rows = slice(sub * BLK, (sub + 1) * BLK)
        listed = [source[block * LIST + e] for e in range(LIST)]
        q = jnp.concatenate([q_ref[rows, g * HEAD_DIM : (g + 1) * HEAD_DIM] for g in range(GROUP)], axis=0)
        g_out = jnp.concatenate([g_ref[rows, g * HEAD_DIM : (g + 1) * HEAD_DIM] for g in range(GROUP)], axis=0)
        keys = jnp.concatenate([table[0, at] for at in listed], axis=0)
        values = jnp.concatenate([table[1, at] for at in listed], axis=0)
        scores = dot(keys, q, NT)
        parts = []
        for e in range(LIST):
            part = scores[e * BLK : (e + 1) * BLK]
            mask = hidden if e == 0 else hidden & (listed[e] == block)
            parts.append(jnp.where(mask, NEG_FILL, part))
        scores = jnp.concatenate(parts, axis=0)
        peak = jnp.max(scores, axis=0, keepdims=True)
        expo = jnp.exp2((scores - peak) * (SCALE * LOG2E))
        probs = expo * (1.0 / jnp.sum(expo, axis=0, keepdims=True))
        probs_low = probs.astype(jnp.bfloat16)
        dprob = dot(values, g_out, NT)
        delta = jnp.sum(probs * dprob, axis=0, keepdims=True)
        dscore = (probs * (dprob - delta)).astype(jnp.bfloat16)
        attended = dot(values, probs_low, TN).T.astype(jnp.bfloat16)
        dq = (dot(keys, dscore, TN) * SCALE).T.astype(jnp.bfloat16)
        for g in range(GROUP):
            cols = slice(g * HEAD_DIM, (g + 1) * HEAD_DIM)
            o_ref[rows, cols] = attended[g * BLK : (g + 1) * BLK]
            dq_ref[rows, cols] = dq[g * BLK : (g + 1) * BLK]
        dk = dot(dscore, q, NN)
        dv = dot(probs_low, g_out, NN)
        for e in range(LIST):
            total[0, listed[e]] += dk[e * BLK : (e + 1) * BLK]
            total[1, listed[e]] += dv[e * BLK : (e + 1) * BLK]

    @pl.when(step == pl.num_programs(0) - 1)
    def _():
        for kv, factor in ((0, SCALE), (1, 1.0)):
            near_out[kv] = total[kv, :blocks_here] * factor
            for d in range(steps):
                first = blocks_here + d * CAP
                far_out[d][kv] = (total[kv, first : first + CAP] * factor).astype(jnp.bfloat16)


def gather_sum_kernel(place, asked, near, *refs, steps):
    back, (*outs, total) = refs[:steps], refs[steps:]
    heads = len(outs)
    per_quarter = outs[0].shape[1] // BLK
    total[...] = near[...]
    for d in range(1, steps + 1):
        c = lax.rem(place[0] + d, steps + 1)
        for s in range(CAP):
            block = asked[c * CAP + s]
            for kv in range(2):
                total[kv, block] += back[d - 1][kv, s].astype(jnp.float32)
    for r in range(heads):
        first = lax.rem(place[1] + heads - r, heads) * per_quarter
        for kv in range(2):
            for j in range(per_quarter):
                outs[r][kv, j * BLK : (j + 1) * BLK, :] = total[kv, first + j].astype(jnp.bfloat16)


def join_kernel(place, *refs, heads):
    *pieces, k_ref, v_ref = refs
    head_count = len(pieces) // heads
    for h in range(head_count):
        for r in range(heads):
            peer = lax.rem(place[1] + r, heads)
            col = pl.multiple_of((peer * head_count + h) * HEAD_DIM, HEAD_DIM)
            k_ref[:, pl.ds(col, HEAD_DIM)] = pieces[h * heads + r][0]
            v_ref[:, pl.ds(col, HEAD_DIM)] = pieces[h * heads + r][1]


def whole(shape):
    return pl.BlockSpec(tuple(shape), lambda *_: (0,) * len(shape))


def call(kernel, scalars, arrays, out_shapes, scratch=(), name=None):
    return pl.pallas_call(
        kernel,
        grid_spec=pltpu.PrefetchScalarGridSpec(
            num_scalar_prefetch=len(scalars),
            grid=(1,),
            in_specs=[whole(x.shape) for x in arrays],
            out_specs=[whole(x.shape) for x in out_shapes],
            scratch_shapes=list(scratch),
        ),
        out_shape=list(out_shapes),
        compiler_params=params(),
        name=name,
    )(*scalars, *arrays)


def attend(place, source, queries, out_grad, own, far, head, earlier):
    tokens_here, width = queries.shape
    blocks_here = tokens_here // BLK
    slots = blocks_here + len(far) * CAP
    tile = pl.BlockSpec((STEP_BLOCKS * BLK, GROUP * HEAD_DIM), lambda i, *_: (i, head))
    near_shape = (2, blocks_here, BLK, HEAD_DIM)
    first = 4 + len(own) + len(far)
    aliases = {first: 0, first + 1: 1} if earlier else {}
    arrays = [*own, *far]
    return pl.pallas_call(
        functools.partial(attend_kernel, heads=len(own), steps=len(far)),
        grid_spec=pltpu.PrefetchScalarGridSpec(
            num_scalar_prefetch=2,
            grid=(blocks_here // STEP_BLOCKS,),
            in_specs=[tile, tile]
            + [whole(x.shape) for x in arrays]
            + [pl.BlockSpec(memory_space=pl.ANY)] * len(earlier),
            out_specs=[tile, tile, whole(near_shape)] + [whole(x.shape) for x in far],
            scratch_shapes=[
                pltpu.VMEM((2, slots, BLK, HEAD_DIM), jnp.bfloat16),
                pltpu.VMEM((2, slots, BLK, HEAD_DIM), jnp.float32),
            ],
        ),
        out_shape=[
            jax.ShapeDtypeStruct((tokens_here, width), jnp.bfloat16),
            jax.ShapeDtypeStruct((tokens_here, width), jnp.bfloat16),
            jax.ShapeDtypeStruct(near_shape, jnp.float32),
        ]
        + [jax.ShapeDtypeStruct(x.shape, jnp.bfloat16) for x in far],
        input_output_aliases=aliases,
        compiler_params=params(),
        cost_estimate=pl.CostEstimate(
            flops=12 * blocks_here * LIST * BLK * GROUP * BLK * HEAD_DIM,
            bytes_accessed=20 * 1024 * 1024,
            transcendentals=blocks_here * LIST * BLK * GROUP * BLK,
        ),
        name="attend",
    )(place, source, queries, out_grad, *arrays, *earlier)


def turn(x, axis, count, by):
    return lax.ppermute(x, axis, [(i, (i + by) % count) for i in range(count)])


def up(x, count, by):
    return lax.ppermute(x, "ctx", [(i, i + by) for i in range(count - by)])


def down(x, count, by):
    return lax.ppermute(x, "ctx", [(i + by, i) for i in range(count - by)])


def per_device(queries, key_states, value_states, block_lists, out_grad):
    shard_index = lax.axis_index("ctx")
    shard_count = lax.axis_size("ctx")
    heads = lax.axis_size("head")
    blocks_here = queries.shape[0] // BLK
    quarter = key_states.shape[0]
    head_count = key_states.shape[1] // heads // HEAD_DIM
    head_index = lax.axis_index("head")
    place = jnp.stack([shard_index, head_index]).astype(jnp.int32)

    piece = jax.ShapeDtypeStruct((2, quarter, HEAD_DIM), jnp.bfloat16)
    own = []
    for h in range(head_count):
        here = jnp.concatenate([place, jnp.full((1,), h, jnp.int32)])
        parts = call(split_kernel, [here], [key_states, value_states], [piece] * heads, name="split")
        own.append([parts[0]] + [turn(parts[r], "head", heads, r) for r in range(1, heads)])

    flat_ids = block_lists.reshape(-1)
    owner_shard = flat_ids // blocks_here
    inner_index = flat_ids % blocks_here
    every_block = jnp.arange(shard_count * blocks_here, dtype=jnp.int32)
    hits = flat_ids[:, None] == every_block[None, :]
    block_hits = jnp.any(hits, axis=0).reshape(shard_count, blocks_here)
    needed = block_hits & (jnp.arange(shard_count) != shard_index)[:, None]
    slot_rank = jnp.cumsum(needed.astype(jnp.int32), axis=1) - 1
    slot_pick = needed[:, :, None] & (slot_rank[:, :, None] == jnp.arange(CAP)[None, None, :])
    requests = jnp.sum(jnp.where(slot_pick, jnp.arange(blocks_here, dtype=jnp.int32)[None, :, None], 0), axis=1)
    ref_rank = jnp.sum(jnp.where(hits, slot_rank.reshape(-1)[None, :], 0), axis=1)
    distance = shard_index - owner_shard
    source = jnp.where(distance == 0, inner_index, blocks_here + (distance - 1) * CAP + ref_rank)
    asked = lax.all_to_all(requests, "ctx", split_axis=0, concat_axis=0, tiled=True).reshape(-1)

    slots = jax.ShapeDtypeStruct((2, CAP, BLK, HEAD_DIM), jnp.bfloat16)
    table = pltpu.VMEM((2, blocks_here, BLK, HEAD_DIM), jnp.bfloat16)
    far = []
    for h in range(head_count):
        picked = call(
            functools.partial(pick_kernel, heads=heads), [place, asked], own[h], [slots] * (shard_count - 1), [table], "pick"
        )
        far.append([up(x, shard_count, d) for d, x in enumerate(picked, 1)])
    earlier, nears, backs = [], [], []
    for h in range(head_count):
        attended, query_grad, near, *far_grad = attend(
            place, source, queries, out_grad, own[h], far[h], h, earlier
        )
        earlier = [attended, query_grad]
        nears.append(near)
        backs.append([down(x, shard_count, d) for d, x in enumerate(far_grad, 1)])
    total = pltpu.VMEM((2, blocks_here, BLK, HEAD_DIM), jnp.float32)
    done = []
    for h in range(head_count):
        sums = call(
            functools.partial(gather_sum_kernel, steps=shard_count - 1),
            [place, asked], [nears[h], *backs[h]], [piece] * heads, [total], "gather_sum",
        )
        done.append([sums[0]] + [turn(sums[r], "head", heads, -r) for r in range(1, heads)])
    pieces = [x for group in done for x in group]
    grad = jax.ShapeDtypeStruct(key_states.shape, jnp.bfloat16)
    key_grad, value_grad = call(functools.partial(join_kernel, heads=heads), [place], pieces, [grad, grad], name="join")
    return attended, query_grad, key_grad, value_grad


def solution(mesh):
    return jax.shard_map(
        per_device,
        mesh=mesh,
        in_specs=(
            P("ctx", "head"),
            P(("ctx", "head"), None),
            P(("ctx", "head"), None),
            P("ctx", None),
            P("ctx", "head"),
        ),
        out_specs=(
            P("ctx", "head"),
            P("ctx", "head"),
            P(("ctx", "head"), None),
            P(("ctx", "head"), None),
        ),
        check_vma=False,
    )
```

```python
import functools

import jax
import jax.numpy as jnp
from jax import lax
from jax.experimental import pallas as pl
from jax.experimental.pallas import tpu as pltpu
from jax.sharding import PartitionSpec as P

HEAD_DIM = 128
GROUP = 4
BLK = 64
LIST = 8
CAP = 3
STEP_BLOCKS = 2
NEG_FILL = -1e30
SCALE = HEAD_DIM ** (-0.5)
LOG2E = 1.4426950408889634
VMEM_LIMIT = 50 * 1024 * 1024

NT = (((1,), (1,)), ((), ()))
NN = (((1,), (0,)), ((), ()))
TN = (((0,), (0,)), ((), ()))


def dot(a, b, dims):
    return lax.dot_general(a, b, dims, preferred_element_type=jnp.float32)


def params(**kw):
    return pltpu.CompilerParams(vmem_limit_bytes=VMEM_LIMIT, **kw)


def partner(me, r, count):
    return me ^ r if count & (count - 1) == 0 else (me + r) % count


def origin(me, r, count):
    return me ^ r if count & (count - 1) == 0 else (me + count - r) % count


def split_kernel(place, k_ref, v_ref, *refs, heads):
    *outs, sem = refs
    head_count = len(outs) // heads
    copies = []
    for h in range(head_count):
        for r in range(heads):
            peer = partner(place[1], r, heads)
            col = pl.multiple_of((peer * head_count + h) * HEAD_DIM, HEAD_DIM)
            for kv, ref in enumerate((k_ref, v_ref)):
                at = h * heads + r
                copies.append(
                    pltpu.make_async_copy(ref.at[:, pl.ds(col, HEAD_DIM)], outs[at].at[kv], sem.at[2 * at + kv])
                )
    for copy in copies:
        copy.start()
    for copy in copies:
        copy.wait()


def fill_table(place, own, table):
    heads = len(own)
    per_quarter = own[0].shape[1] // BLK
    for r in range(heads):
        first = origin(place[1], r, heads) * per_quarter
        for kv in range(2):
            for j in range(per_quarter):
                table[kv, first + j] = own[r][kv, j * BLK : (j + 1) * BLK, :]


def pick_kernel(place, asked, *refs, heads):
    own, (*outs, table) = refs[:heads], refs[heads:]
    fill_table(place, own, table)
    for d, out in enumerate(outs):
        for s in range(CAP):
            block = asked[d * CAP + s]
            for kv in range(2):
                out[kv, s] = table[kv, block]


def attend_kernel(place, source, q_ref, g_ref, *refs, heads, steps):
    own, far = refs[:heads], refs[heads : heads + steps]
    table, total = refs[-2:]
    far_out = refs[-2 - steps : -2]
    o_ref, dq_ref, near_out = refs[-5 - steps : -2 - steps]
    step = pl.program_id(0)
    blocks_here = near_out.shape[1]

    @pl.when(step == 0)
    def _():
        fill_table(place, own, table)
        for kv in range(2):
            for d in range(steps):
                for s in range(CAP):
                    table[kv, blocks_here + d * CAP + s] = far[d][kv, s]
        total[...] = jnp.zeros_like(total)

    key_row = lax.broadcasted_iota(jnp.int32, (BLK, GROUP * BLK), 0)
    query_col = lax.broadcasted_iota(jnp.int32, (BLK, GROUP * BLK), 1) % BLK
    hidden = key_row > query_col
    for sub in range(STEP_BLOCKS):
        block = step * STEP_BLOCKS + sub
        rows = slice(sub * BLK, (sub + 1) * BLK)
        listed = [source[block * LIST + e] for e in range(LIST)]
        q = jnp.concatenate([q_ref[rows, g * HEAD_DIM : (g + 1) * HEAD_DIM] for g in range(GROUP)], axis=0)
        g_out = jnp.concatenate([g_ref[rows, g * HEAD_DIM : (g + 1) * HEAD_DIM] for g in range(GROUP)], axis=0)
        keys = jnp.concatenate([table[0, at] for at in listed], axis=0)
        values = jnp.concatenate([table[1, at] for at in listed], axis=0)
        scores = dot(keys, q, NT)
        parts = []
        for e in range(LIST):
            part = scores[e * BLK : (e + 1) * BLK]
            mask = hidden if e == 0 else hidden & (listed[e] == block)
            parts.append(jnp.where(mask, NEG_FILL, part))
        scores = jnp.concatenate(parts, axis=0)
        peak = jnp.max(scores, axis=0, keepdims=True)
        expo = jnp.exp2((scores - peak) * (SCALE * LOG2E))
        probs = expo * (1.0 / jnp.sum(expo, axis=0, keepdims=True))
        probs_low = probs.astype(jnp.bfloat16)
        dprob = dot(values, g_out, NT)
        delta = jnp.sum(probs * dprob, axis=0, keepdims=True)
        dscore = (probs * (dprob - delta)).astype(jnp.bfloat16)
        attended = dot(values, probs_low, TN).T.astype(jnp.bfloat16)
        dq = (dot(keys, dscore, TN) * SCALE).T.astype(jnp.bfloat16)
        for g in range(GROUP):
            cols = slice(g * HEAD_DIM, (g + 1) * HEAD_DIM)
            o_ref[rows, cols] = attended[g * BLK : (g + 1) * BLK]
            dq_ref[rows, cols] = dq[g * BLK : (g + 1) * BLK]
        dk = dot(dscore, q, NN)
        dv = dot(probs_low, g_out, NN)
        for e in range(LIST):
            total[0, listed[e]] += dk[e * BLK : (e + 1) * BLK]
            total[1, listed[e]] += dv[e * BLK : (e + 1) * BLK]

    @pl.when(step == pl.num_programs(0) - 1)
    def _():
        for kv, factor in ((0, SCALE), (1, 1.0)):
            near_out[kv] = total[kv, :blocks_here] * factor
            for d in range(steps):
                first = blocks_here + d * CAP
                far_out[d][kv] = (total[kv, first : first + CAP] * factor).astype(jnp.bfloat16)


def gather_sum_kernel(place, asked, near, *refs, steps):
    back, (*outs, total) = refs[:steps], refs[steps:]
    heads = len(outs)
    per_quarter = outs[0].shape[1] // BLK
    total[...] = near[...]
    for d in range(steps):
        for s in range(CAP):
            block = asked[d * CAP + s]
            for kv in range(2):
                total[kv, block] += back[d][kv, s].astype(jnp.float32)
    for r in range(heads):
        first = origin(place[1], r, heads) * per_quarter
        for kv in range(2):
            for j in range(per_quarter):
                outs[r][kv, j * BLK : (j + 1) * BLK, :] = total[kv, first + j].astype(jnp.bfloat16)


def join_kernel(place, *refs, heads):
    *pieces, k_ref, v_ref = refs
    head_count = len(pieces) // heads
    for h in range(head_count):
        for r in range(heads):
            peer = partner(place[1], r, heads)
            col = pl.multiple_of((peer * head_count + h) * HEAD_DIM, HEAD_DIM)
            k_ref[:, pl.ds(col, HEAD_DIM)] = pieces[h * heads + r][0]
            v_ref[:, pl.ds(col, HEAD_DIM)] = pieces[h * heads + r][1]


def whole(shape):
    return pl.BlockSpec(tuple(shape), lambda *_: (0,) * len(shape))


def call(kernel, scalars, arrays, out_shapes, scratch=(), name=None):
    return pl.pallas_call(
        kernel,
        grid_spec=pltpu.PrefetchScalarGridSpec(
            num_scalar_prefetch=len(scalars),
            grid=(1,),
            in_specs=[whole(x.shape) for x in arrays],
            out_specs=[whole(x.shape) for x in out_shapes],
            scratch_shapes=list(scratch),
        ),
        out_shape=list(out_shapes),
        compiler_params=params(),
        name=name,
    )(*scalars, *arrays)


def attend(place, source, queries, out_grad, own, far, head, earlier):
    tokens_here, width = queries.shape
    blocks_here = tokens_here // BLK
    slots = blocks_here + len(far) * CAP
    tile = pl.BlockSpec((STEP_BLOCKS * BLK, GROUP * HEAD_DIM), lambda i, *_: (i, head))
    near_shape = (2, blocks_here, BLK, HEAD_DIM)
    first = 4 + len(own) + len(far)
    aliases = {first: 0, first + 1: 1} if earlier else {}
    arrays = [*own, *far]
    return pl.pallas_call(
        functools.partial(attend_kernel, heads=len(own), steps=len(far)),
        grid_spec=pltpu.PrefetchScalarGridSpec(
            num_scalar_prefetch=2,
            grid=(blocks_here // STEP_BLOCKS,),
            in_specs=[tile, tile]
            + [whole(x.shape) for x in arrays]
            + [pl.BlockSpec(memory_space=pl.ANY)] * len(earlier),
            out_specs=[tile, tile, whole(near_shape)] + [whole(x.shape) for x in far],
            scratch_shapes=[
                pltpu.VMEM((2, slots, BLK, HEAD_DIM), jnp.bfloat16),
                pltpu.VMEM((2, slots, BLK, HEAD_DIM), jnp.float32),
            ],
        ),
        out_shape=[
            jax.ShapeDtypeStruct((tokens_here, width), jnp.bfloat16),
            jax.ShapeDtypeStruct((tokens_here, width), jnp.bfloat16),
            jax.ShapeDtypeStruct(near_shape, jnp.float32),
        ]
        + [jax.ShapeDtypeStruct(x.shape, jnp.bfloat16) for x in far],
        input_output_aliases=aliases,
        compiler_params=params(),
        cost_estimate=pl.CostEstimate(
            flops=12 * blocks_here * LIST * BLK * GROUP * BLK * HEAD_DIM,
            bytes_accessed=20 * 1024 * 1024,
            transcendentals=blocks_here * LIST * BLK * GROUP * BLK,
        ),
        name="attend",
    )(place, source, queries, out_grad, *arrays, *earlier)


def send(x, axis, count, r):
    return lax.ppermute(x, axis, [(i, partner(i, r, count)) for i in range(count)])


def send_back(x, axis, count, r):
    return lax.ppermute(x, axis, [(i, origin(i, r, count)) for i in range(count)])


def rank_of(hits):
    n = hits.shape[-1]
    before = jnp.arange(n)[:, None] < jnp.arange(n)[None, :]
    return jnp.sum((hits[:, :, None] & before[None]).astype(jnp.int32), axis=1)


def per_device(queries, key_states, value_states, block_lists, out_grad):
    shard_index = lax.axis_index("ctx")
    shard_count = lax.axis_size("ctx")
    heads = lax.axis_size("head")
    blocks_here = queries.shape[0] // BLK
    quarter = key_states.shape[0]
    head_count = key_states.shape[1] // heads // HEAD_DIM
    head_index = lax.axis_index("head")
    place = jnp.stack([shard_index, head_index]).astype(jnp.int32)
    inner = jnp.arange(blocks_here, dtype=jnp.int32)

    flat_ids = block_lists.reshape(1, -1)
    others = [send(flat_ids, "ctx", shard_count, d) for d in range(1, shard_count)]

    piece = jax.ShapeDtypeStruct((2, quarter, HEAD_DIM), jnp.bfloat16)
    pieces = pl.pallas_call(
        functools.partial(split_kernel, heads=heads),
        grid_spec=pltpu.PrefetchScalarGridSpec(
            num_scalar_prefetch=1,
            grid=(1,),
            in_specs=[pl.BlockSpec(memory_space=pl.ANY)] * 2,
            out_specs=[pl.BlockSpec(memory_space=pl.ANY)] * (heads * head_count),
            scratch_shapes=[pltpu.SemaphoreType.DMA((2 * heads * head_count,))],
        ),
        out_shape=[piece] * (heads * head_count),
        compiler_params=params(),
        name="split",
    )(place, key_states, value_states)
    own = []
    for h in range(head_count):
        parts = pieces[h * heads : (h + 1) * heads]
        own.append([parts[0]] + [send(parts[r], "head", heads, r) for r in range(1, heads)])

    asked_hits = jnp.any(
        jnp.concatenate(others)[:, :, None] == (shard_index * blocks_here + inner)[None, None, :], axis=1
    )
    asked_rank = rank_of(asked_hits)
    asked = jnp.sum(
        jnp.where(asked_hits[:, None] & (asked_rank[:, None] == jnp.arange(CAP)[None, :, None]), inner[None, None], 0),
        axis=2,
    ).reshape(-1)

    flat_ids = flat_ids.reshape(-1)
    owner = flat_ids // blocks_here
    every_block = jnp.arange(shard_count * blocks_here, dtype=jnp.int32)
    listed = jnp.any(flat_ids[:, None] == every_block[None, :], axis=0)
    same_owner = owner[:, None] == (every_block // blocks_here)[None, :]
    rank = jnp.sum((same_owner & listed[None, :] & (every_block[None, :] < flat_ids[:, None])).astype(jnp.int32), axis=1)
    if shard_count & (shard_count - 1) == 0:
        distance = shard_index ^ owner
    else:
        distance = (shard_index + shard_count - owner) % shard_count
    source = jnp.where(distance == 0, flat_ids % blocks_here, blocks_here + (distance - 1) * CAP + rank)

    slots = jax.ShapeDtypeStruct((2, CAP, BLK, HEAD_DIM), jnp.bfloat16)
    table = pltpu.VMEM((2, blocks_here, BLK, HEAD_DIM), jnp.bfloat16)
    far = []
    for h in range(head_count):
        picked = call(
            functools.partial(pick_kernel, heads=heads), [place, asked], own[h], [slots] * (shard_count - 1), [table], "pick"
        )
        far.append([send(x, "ctx", shard_count, d) for d, x in enumerate(picked, 1)])
    earlier, nears, backs = [], [], []
    for h in range(head_count):
        attended, query_grad, near, *far_grad = attend(
            place, source, queries, out_grad, own[h], far[h], h, earlier
        )
        earlier = [attended, query_grad]
        nears.append(near)
        backs.append([send_back(x, "ctx", shard_count, d) for d, x in enumerate(far_grad, 1)])
    total = pltpu.VMEM((2, blocks_here, BLK, HEAD_DIM), jnp.float32)
    done = []
    for h in range(head_count):
        sums = call(
            functools.partial(gather_sum_kernel, steps=shard_count - 1),
            [place, asked], [nears[h], *backs[h]], [piece] * heads, [total], "gather_sum",
        )
        done.append([sums[0]] + [send_back(sums[r], "head", heads, r) for r in range(1, heads)])
    pieces = [x for group in done for x in group]
    grad = jax.ShapeDtypeStruct(key_states.shape, jnp.bfloat16)
    key_grad, value_grad = call(functools.partial(join_kernel, heads=heads), [place], pieces, [grad, grad], name="join")
    return attended, query_grad, key_grad, value_grad


def solution(mesh):
    return jax.shard_map(
        per_device,
        mesh=mesh,
        in_specs=(
            P("ctx", "head"),
            P(("ctx", "head"), None),
            P(("ctx", "head"), None),
            P("ctx", None),
            P("ctx", "head"),
        ),
        out_specs=(
            P("ctx", "head"),
            P("ctx", "head"),
            P(("ctx", "head"), None),
            P(("ctx", "head"), None),
        ),
        check_vma=False,
    )
```

```python
import functools

import jax
import jax.numpy as jnp
from jax import lax
from jax.experimental import pallas as pl
from jax.experimental.pallas import tpu as pltpu
from jax.sharding import PartitionSpec as P

HEAD_DIM = 128
GROUP = 4
BLK = 64
LIST = 8
CAP = 3
STEP_BLOCKS = 2
NEG_FILL = -1e30
SCALE = HEAD_DIM ** (-0.5)
LOG2E = 1.4426950408889634
VMEM_LIMIT = 40 * 1024 * 1024
VMEM_MOST = 60 * 1024 * 1024

NT = (((1,), (1,)), ((), ()))
NN = (((1,), (0,)), ((), ()))
TN = (((0,), (0,)), ((), ()))


def dot(a, b, dims):
    return lax.dot_general(a, b, dims, preferred_element_type=jnp.float32)


def params(limit=VMEM_LIMIT):
    return pltpu.CompilerParams(vmem_limit_bytes=limit)


def partner(me, r, count):
    return me ^ r if count & (count - 1) == 0 else (me + r) % count


def origin(me, r, count):
    return me ^ r if count & (count - 1) == 0 else (me + count - r) % count


def split_kernel(place, k_ref, v_ref, *refs, heads):
    *outs, sem = refs
    head_count = len(outs) // heads
    copies = []
    for h in range(head_count):
        for r in range(heads):
            at = h * heads + r
            for kv, ref in enumerate((k_ref, v_ref)):
                cols = head_columns(place, r, heads, h, head_count)
                copies.append(pltpu.make_async_copy(ref.at[:, cols], outs[at].at[kv], sem.at[2 * at + kv]))
    run(copies)


def join_kernel(place, *refs, heads):
    *pieces, k_ref, v_ref, sem = refs
    head_count = len(pieces) // heads
    copies = []
    for h in range(head_count):
        for r in range(heads):
            at = h * heads + r
            for kv, ref in enumerate((k_ref, v_ref)):
                cols = head_columns(place, r, heads, h, head_count)
                copies.append(pltpu.make_async_copy(pieces[at].at[kv], ref.at[:, cols], sem.at[2 * at + kv]))
    run(copies)


def head_columns(place, r, heads, h, head_count):
    col = (partner(place[1], r, heads) * head_count + h) * HEAD_DIM
    return pl.ds(pl.multiple_of(col, HEAD_DIM), HEAD_DIM)


def run(copies):
    for copy in copies:
        copy.start()
    for copy in copies:
        copy.wait()


def by_copies(kernel, place, arrays, out_shapes, name, limit):
    here = pl.BlockSpec(memory_space=pl.ANY)
    return pl.pallas_call(
        kernel,
        grid_spec=pltpu.PrefetchScalarGridSpec(
            num_scalar_prefetch=1,
            grid=(1,),
            in_specs=[here] * len(arrays),
            out_specs=[here] * len(out_shapes),
            scratch_shapes=[pltpu.SemaphoreType.DMA((2 * max(len(arrays), len(out_shapes)),))],
        ),
        out_shape=out_shapes,
        compiler_params=params(limit),
        name=name,
    )(place, *arrays)


def fill_table(place, own, table):
    heads = len(own)
    per_quarter = own[0].shape[1] // BLK
    for r in range(heads):
        first = origin(place[1], r, heads) * per_quarter
        for kv in range(2):
            for j in range(per_quarter):
                table[kv, first + j] = own[r][kv, j * BLK : (j + 1) * BLK, :]


def pick_kernel(place, asked, *refs, heads, head_count, first, single):
    own, (*outs, table) = refs[: heads * head_count], refs[heads * head_count :]
    for h in range(head_count):
        fill_table(place, own[h * heads : (h + 1) * heads], table.at[h])
    for d, out in enumerate(outs, first):
        for s in range(CAP):
            block = asked[(d - 1) * CAP + s]
            for kv in range(2):
                if d < single:
                    for h in range(head_count):
                        out[h, kv, s] = table[h, kv, block]
                else:
                    out[kv, s] = table[head_count - 1, kv, block]


def attend_kernel(place, source, q_ref, g_ref, *refs, heads, steps, head):
    own, far = refs[:heads], refs[heads : heads + steps]
    table, total = refs[-2:]
    far_out = refs[-2 - steps : -2]
    o_ref, dq_ref, near_out = refs[-5 - steps : -2 - steps]
    step = pl.program_id(0)
    blocks_here = near_out.shape[1]

    @pl.when(step == 0)
    def _():
        fill_table(place, own, table)
        for kv in range(2):
            for d in range(steps):
                for s in range(CAP):
                    from_there = far[d].at[head] if len(far[d].shape) == 5 else far[d]
                    table[kv, blocks_here + d * CAP + s] = from_there[kv, s]
        total[...] = jnp.zeros_like(total)

    key_row = lax.broadcasted_iota(jnp.int32, (BLK, GROUP * BLK), 0)
    query_col = lax.broadcasted_iota(jnp.int32, (BLK, GROUP * BLK), 1) % BLK
    hidden = key_row > query_col
    for sub in range(STEP_BLOCKS):
        block = step * STEP_BLOCKS + sub
        rows = slice(sub * BLK, (sub + 1) * BLK)
        listed = [source[block * LIST + e] for e in range(LIST)]
        q = jnp.concatenate([q_ref[rows, g * HEAD_DIM : (g + 1) * HEAD_DIM] for g in range(GROUP)], axis=0)
        g_out = jnp.concatenate([g_ref[rows, g * HEAD_DIM : (g + 1) * HEAD_DIM] for g in range(GROUP)], axis=0)
        keys = jnp.concatenate([table[0, at] for at in listed], axis=0)
        values = jnp.concatenate([table[1, at] for at in listed], axis=0)
        scores = dot(keys, q, NT)
        parts = []
        for e in range(LIST):
            part = scores[e * BLK : (e + 1) * BLK]
            mask = hidden if e == 0 else hidden & (listed[e] == block)
            parts.append(jnp.where(mask, NEG_FILL, part))
        scores = jnp.concatenate(parts, axis=0)
        peak = jnp.max(scores, axis=0, keepdims=True)
        expo = jnp.exp2((scores - peak) * (SCALE * LOG2E))
        probs = expo * (1.0 / jnp.sum(expo, axis=0, keepdims=True))
        probs_low = probs.astype(jnp.bfloat16)
        dprob = dot(values, g_out, NT)
        delta = jnp.sum(probs * dprob, axis=0, keepdims=True)
        dscore = (probs * (dprob - delta)).astype(jnp.bfloat16)
        attended = dot(values, probs_low, TN).T.astype(jnp.bfloat16)
        dq = (dot(keys, dscore, TN) * SCALE).T.astype(jnp.bfloat16)
        for g in range(GROUP):
            cols = slice(g * HEAD_DIM, (g + 1) * HEAD_DIM)
            o_ref[rows, cols] = attended[g * BLK : (g + 1) * BLK]
            dq_ref[rows, cols] = dq[g * BLK : (g + 1) * BLK]
        dk = dot(dscore, q, NN)
        dv = dot(probs_low, g_out, NN)
        for e in range(LIST):
            total[0, listed[e]] += dk[e * BLK : (e + 1) * BLK]
            total[1, listed[e]] += dv[e * BLK : (e + 1) * BLK]

    @pl.when(step == pl.num_programs(0) - 1)
    def _():
        for kv, factor in ((0, SCALE), (1, 1.0)):
            near_out[kv] = total[kv, :blocks_here] * factor
            for d in range(steps):
                first = blocks_here + d * CAP
                far_out[d][kv] = (total[kv, first : first + CAP] * factor).astype(jnp.bfloat16)


def gather_sum_kernel(place, asked, near, *refs, steps):
    back, (*outs, total) = refs[:steps], refs[steps:]
    heads = len(outs)
    per_quarter = outs[0].shape[1] // BLK
    total[...] = near[...]
    for d in range(steps):
        for s in range(CAP):
            block = asked[d * CAP + s]
            for kv in range(2):
                total[kv, block] += back[d][kv, s].astype(jnp.float32)
    for r in range(heads):
        first = origin(place[1], r, heads) * per_quarter
        for kv in range(2):
            for j in range(per_quarter):
                outs[r][kv, j * BLK : (j + 1) * BLK, :] = total[kv, first + j].astype(jnp.bfloat16)


def whole(shape):
    return pl.BlockSpec(tuple(shape), lambda *_: (0,) * len(shape))


def call(kernel, scalars, arrays, out_shapes, scratch=(), name=None):
    return pl.pallas_call(
        kernel,
        grid_spec=pltpu.PrefetchScalarGridSpec(
            num_scalar_prefetch=len(scalars),
            grid=(1,),
            in_specs=[whole(x.shape) for x in arrays],
            out_specs=[whole(x.shape) for x in out_shapes],
            scratch_shapes=list(scratch),
        ),
        out_shape=list(out_shapes),
        compiler_params=params(),
        name=name,
    )(*scalars, *arrays)


def attend(place, source, queries, out_grad, own, far, head, earlier):
    tokens_here, width = queries.shape
    blocks_here = tokens_here // BLK
    slots = blocks_here + len(far) * CAP
    tile = pl.BlockSpec((STEP_BLOCKS * BLK, GROUP * HEAD_DIM), lambda i, *_: (i, head))
    near_shape = (2, blocks_here, BLK, HEAD_DIM)
    first = 4 + len(own) + len(far)
    aliases = {first: 0, first + 1: 1} if earlier else {}
    arrays = [*own, *far]
    return pl.pallas_call(
        functools.partial(attend_kernel, heads=len(own), steps=len(far), head=head),
        grid_spec=pltpu.PrefetchScalarGridSpec(
            num_scalar_prefetch=2,
            grid=(blocks_here // STEP_BLOCKS,),
            in_specs=[tile, tile]
            + [whole(x.shape) for x in arrays]
            + [pl.BlockSpec(memory_space=pl.ANY)] * len(earlier),
            out_specs=[tile, tile, whole(near_shape)] + [whole(x.shape[-4:]) for x in far],
            scratch_shapes=[
                pltpu.VMEM((2, slots, BLK, HEAD_DIM), jnp.bfloat16),
                pltpu.VMEM((2, slots, BLK, HEAD_DIM), jnp.float32),
            ],
        ),
        out_shape=[
            jax.ShapeDtypeStruct((tokens_here, width), jnp.bfloat16),
            jax.ShapeDtypeStruct((tokens_here, width), jnp.bfloat16),
            jax.ShapeDtypeStruct(near_shape, jnp.float32),
        ]
        + [jax.ShapeDtypeStruct(x.shape[-4:], jnp.bfloat16) for x in far],
        input_output_aliases=aliases,
        compiler_params=params(),
        cost_estimate=pl.CostEstimate(
            flops=12 * blocks_here * LIST * BLK * GROUP * BLK * HEAD_DIM,
            bytes_accessed=20 * 1024 * 1024,
            transcendentals=blocks_here * LIST * BLK * GROUP * BLK,
        ),
        name="attend",
    )(place, source, queries, out_grad, *arrays, *earlier)


def send(x, axis, count, r):
    return lax.ppermute(x, axis, [(i, partner(i, r, count)) for i in range(count)])


def send_back(x, axis, count, r):
    return lax.ppermute(x, axis, [(i, origin(i, r, count)) for i in range(count)])


def lists_of_others(block_lists, count):
    if count & (count - 1):
        return jnp.stack([send_back(block_lists, "ctx", count, d) for d in range(1, count)])
    known = block_lists[None]
    while known.shape[0] < count:
        known = jnp.concatenate([known, send(known, "ctx", count, known.shape[0])])
    return known[1:]


def rank_of(hits):
    n = hits.shape[-1]
    before = jnp.arange(n)[:, None] < jnp.arange(n)[None, :]
    return jnp.sum((hits[:, :, None] & before[None]).astype(jnp.int32), axis=1)


def per_device(queries, key_states, value_states, block_lists, out_grad):
    shard_index = lax.axis_index("ctx")
    shard_count = lax.axis_size("ctx")
    heads = lax.axis_size("head")
    blocks_here = queries.shape[0] // BLK
    quarter = key_states.shape[0]
    head_count = key_states.shape[1] // heads // HEAD_DIM
    head_index = lax.axis_index("head")
    place = jnp.stack([shard_index, head_index]).astype(jnp.int32)
    inner = jnp.arange(blocks_here, dtype=jnp.int32)

    piece = jax.ShapeDtypeStruct((2, quarter, HEAD_DIM), jnp.bfloat16)
    pieces = by_copies(
        functools.partial(split_kernel, heads=heads), place, [key_states, value_states], [piece] * (heads * head_count), "split", VMEM_MOST
    )
    own = []
    for h in range(head_count):
        parts = pieces[h * heads : (h + 1) * heads]
        own.append([parts[0]] + [send(parts[r], "head", heads, r) for r in range(1, heads)])

    lists, _ = lax.optimization_barrier((block_lists, pieces[0]))
    asked_hits = jnp.any(
        lists_of_others(lists, shard_count)[:, :, :, None] == (shard_index * blocks_here + inner)[None, None, None, :],
        axis=(1, 2),
    )
    asked_rank = rank_of(asked_hits)
    asked = jnp.sum(
        jnp.where(asked_hits[:, None] & (asked_rank[:, None] == jnp.arange(CAP)[None, :, None]), inner[None, None], 0),
        axis=2,
    ).reshape(-1)

    flat_ids = block_lists.reshape(-1)
    owner = flat_ids // blocks_here
    every_block = jnp.arange(shard_count * blocks_here, dtype=jnp.int32)
    listed = jnp.any(flat_ids[:, None] == every_block[None, :], axis=0)
    same_owner = owner[:, None] == (every_block // blocks_here)[None, :]
    rank = jnp.sum((same_owner & listed[None, :] & (every_block[None, :] < flat_ids[:, None])).astype(jnp.int32), axis=1)
    if shard_count & (shard_count - 1) == 0:
        distance = shard_index ^ owner
    else:
        distance = (shard_index + shard_count - owner) % shard_count
    source = jnp.where(distance == 0, flat_ids % blocks_here, blocks_here + (distance - 1) * CAP + rank)

    wide = max(1, shard_count // 2)
    one = (2, CAP, BLK, HEAD_DIM)
    far = [[] for _ in range(head_count)]
    near_shape = jax.ShapeDtypeStruct((head_count, *one), jnp.bfloat16)
    for h in range(head_count):
        last = h == head_count - 1
        first = 1 if last else wide
        picked = call(
            functools.partial(pick_kernel, heads=heads, head_count=h + 1, first=first, single=wide),
            [place, asked],
            [x for group in own[: h + 1] for x in group],
            [near_shape] * (wide - 1) * last + [jax.ShapeDtypeStruct(one, jnp.bfloat16)] * (shard_count - wide),
            [pltpu.VMEM((h + 1, 2, blocks_here, BLK, HEAD_DIM), jnp.bfloat16)],
            "pick",
        )
        sent = {d: send(x, "ctx", shard_count, d) for d, x in enumerate(picked, first)}
        far[h] = [sent[d] for d in range(wide, shard_count)]
    near = [sent[d] for d in range(1, wide)]
    far = [near + group for group in far]
    earlier, nears, backs = [], [], []
    for h in range(head_count):
        attended, query_grad, near, *far_grad = attend(
            place, source, queries, out_grad, own[h], far[h], h, earlier
        )
        earlier = [attended, query_grad]
        nears.append(near)
        backs.append([send_back(x, "ctx", shard_count, d) for d, x in enumerate(far_grad, 1)])
    total = pltpu.VMEM((2, blocks_here, BLK, HEAD_DIM), jnp.float32)
    done = []
    for h in range(head_count):
        sums = call(
            functools.partial(gather_sum_kernel, steps=shard_count - 1),
            [place, asked], [nears[h], *backs[h]], [piece] * heads, [total], "gather_sum",
        )
        done.append([sums[0]] + [send_back(sums[r], "head", heads, r) for r in range(1, heads)])
    grad = jax.ShapeDtypeStruct(key_states.shape, jnp.bfloat16)
    key_grad, value_grad = by_copies(
        functools.partial(join_kernel, heads=heads), place, [x for group in done for x in group], [grad, grad], "join", VMEM_LIMIT
    )
    return attended, query_grad, key_grad, value_grad


def solution(mesh):
    return jax.shard_map(
        per_device,
        mesh=mesh,
        in_specs=(
            P("ctx", "head"),
            P(("ctx", "head"), None),
            P(("ctx", "head"), None),
            P("ctx", None),
            P("ctx", "head"),
        ),
        out_specs=(
            P("ctx", "head"),
            P("ctx", "head"),
            P(("ctx", "head"), None),
            P(("ctx", "head"), None),
        ),
        check_vma=False,
    )
```

```python
import functools

import jax
import jax.numpy as jnp
from jax import lax
from jax.experimental import pallas as pl
from jax.experimental.pallas import tpu as pltpu
from jax.sharding import PartitionSpec as P

HEAD_DIM = 128
GROUP = 4
BLK = 64
LIST = 8
CAP = 3
STEP_BLOCKS = 2
NEG_FILL = -1e30
SCALE = HEAD_DIM ** (-0.5)
LOG2E = 1.4426950408889634
VMEM_LIMIT = 50 * 1024 * 1024
VMEM_MOST = 60 * 1024 * 1024

NT = (((1,), (1,)), ((), ()))
NN = (((1,), (0,)), ((), ()))
TN = (((0,), (0,)), ((), ()))


def dot(a, b, dims):
    return lax.dot_general(a, b, dims, preferred_element_type=jnp.float32)


def params(limit=VMEM_LIMIT):
    return pltpu.CompilerParams(vmem_limit_bytes=limit)


def partner(me, r, count):
    return me ^ r if count & (count - 1) == 0 else (me + r) % count


def origin(me, r, count):
    return me ^ r if count & (count - 1) == 0 else (me + count - r) % count


def head_columns(place, r, heads, h, head_count):
    col = (partner(place[1], r, heads) * head_count + h) * HEAD_DIM
    return pl.ds(pl.multiple_of(col, HEAD_DIM), HEAD_DIM)


def split_kernel(place, k_ref, v_ref, *refs):
    *outs, sem = refs
    heads, head_count = len(outs), outs[0].shape[0]
    copies = []
    for r, out in enumerate(outs):
        for h in range(head_count):
            cols = head_columns(place, r, heads, h, head_count)
            for kv, ref in enumerate((k_ref, v_ref)):
                at = (r * head_count + h) * 2 + kv
                copies.append(pltpu.make_async_copy(ref.at[:, cols], out.at[h, kv], sem.at[at]))
    for copy in copies:
        copy.start()
    for copy in copies:
        copy.wait()


def join_kernel(place, *refs, heads):
    *pieces, k_ref, v_ref, sem = refs
    head_count = len(pieces) // heads
    copies = []
    for at, piece in enumerate(pieces):
        cols = head_columns(place, at % heads, heads, at // heads, head_count)
        for kv, ref in enumerate((k_ref, v_ref)):
            copies.append(pltpu.make_async_copy(piece.at[kv], ref.at[:, cols], sem.at[2 * at + kv]))
    for copy in copies:
        copy.start()
    for copy in copies:
        copy.wait()


def fill_table(place, own, h, table):
    heads = len(own)
    per_quarter = own[0].shape[2] // BLK
    for r in range(heads):
        first = origin(place[1], r, heads) * per_quarter
        for kv in range(2):
            for j in range(per_quarter):
                table[kv, first + j] = own[r][h, kv, j * BLK : (j + 1) * BLK, :]


def parts_of(refs, place, at, shard_count):
    if len(refs) == 1 and len(refs[0].shape) == 5:
        return [(refs[0].at[c], c) for c in range(shard_count)]
    return [(ref, at(place[0], r, shard_count)) for r, ref in enumerate(refs, 1)]


def pick_kernel(place, asked, *refs, heads, head_count, shard_count):
    own, outs, table = refs[:heads], refs[heads:-1], refs[-1]
    for h in range(head_count):
        fill_table(place, own, h, table)
        steps = shard_count - 1
        mine = outs[:steps] if h == 0 else outs[steps + h - 1 : steps + h]
        for out, c in parts_of(mine, place, partner, shard_count):
            for s in range(CAP):
                block = asked[c, s]
                for kv in range(2):
                    out[kv, s] = table[kv, block]


def attend_kernel(place, source, q_ref, g_ref, *refs, heads, fars, outs, head, shard_count):
    own, far = refs[:heads], refs[heads : heads + fars]
    table, total = refs[-2:]
    far_out = refs[-2 - outs : -2]
    o_ref, dq_ref, near_out = refs[-5 - outs : -2 - outs]
    step = pl.program_id(0)
    blocks_here = near_out.shape[1]

    @pl.when(step == 0)
    def _():
        fill_table(place, own, head, table)
        for part, c in parts_of(far, place, origin, shard_count):
            for kv in range(2):
                for s in range(CAP):
                    table[kv, blocks_here + c * CAP + s] = part[kv, s]
        total[...] = jnp.zeros_like(total)

    key_row = lax.broadcasted_iota(jnp.int32, (BLK, GROUP * BLK), 0)
    query_col = lax.broadcasted_iota(jnp.int32, (BLK, GROUP * BLK), 1) % BLK
    hidden = key_row > query_col
    for sub in range(STEP_BLOCKS):
        block = step * STEP_BLOCKS + sub
        rows = slice(sub * BLK, (sub + 1) * BLK)
        listed = [source[block * LIST + e] for e in range(LIST)]
        q = jnp.concatenate([q_ref[rows, g * HEAD_DIM : (g + 1) * HEAD_DIM] for g in range(GROUP)], axis=0)
        g_out = jnp.concatenate([g_ref[rows, g * HEAD_DIM : (g + 1) * HEAD_DIM] for g in range(GROUP)], axis=0)
        keys = jnp.concatenate([table[0, at] for at in listed], axis=0)
        values = jnp.concatenate([table[1, at] for at in listed], axis=0)
        scores = dot(keys, q, NT)
        parts = []
        for e in range(LIST):
            part = scores[e * BLK : (e + 1) * BLK]
            mask = hidden if e == 0 else hidden & (listed[e] == block)
            parts.append(jnp.where(mask, NEG_FILL, part))
        scores = jnp.concatenate(parts, axis=0)
        peak = jnp.max(scores, axis=0, keepdims=True)
        expo = jnp.exp2((scores - peak) * (SCALE * LOG2E))
        probs = expo * (1.0 / jnp.sum(expo, axis=0, keepdims=True))
        probs_low = probs.astype(jnp.bfloat16)
        dprob = dot(values, g_out, NT)
        delta = jnp.sum(probs * dprob, axis=0, keepdims=True)
        dscore = (probs * (dprob - delta)).astype(jnp.bfloat16)
        attended = dot(values, probs_low, TN).T.astype(jnp.bfloat16)
        dq = (dot(keys, dscore, TN) * SCALE).T.astype(jnp.bfloat16)
        for g in range(GROUP):
            cols = slice(g * HEAD_DIM, (g + 1) * HEAD_DIM)
            o_ref[rows, cols] = attended[g * BLK : (g + 1) * BLK]
            dq_ref[rows, cols] = dq[g * BLK : (g + 1) * BLK]
        dk = dot(dscore, q, NN)
        dv = dot(probs_low, g_out, NN)
        for e in range(LIST):
            total[0, listed[e]] += dk[e * BLK : (e + 1) * BLK]
            total[1, listed[e]] += dv[e * BLK : (e + 1) * BLK]

    @pl.when(step == pl.num_programs(0) - 1)
    def _():
        for kv, factor in ((0, SCALE), (1, 1.0)):
            near_out[kv] = total[kv, :blocks_here] * factor
            for out, c in parts_of(far_out, place, origin, shard_count):
                for s in range(CAP):
                    out[kv, s] = (total[kv, blocks_here + c * CAP + s] * factor).astype(jnp.bfloat16)


def gather_sum_kernel(place, asked, near, *refs, heads, shard_count):
    back, outs, total = refs[: -heads - 1], refs[-heads - 1 : -1], refs[-1]
    per_quarter = outs[0].shape[1] // BLK
    total[...] = near[...]
    for part, c in parts_of(back, place, partner, shard_count):
        for s in range(CAP):
            block = asked[c, s]
            for kv in range(2):
                total[kv, block] += part[kv, s].astype(jnp.float32)
    for r in range(heads):
        first = origin(place[1], r, heads) * per_quarter
        for kv in range(2):
            for j in range(per_quarter):
                outs[r][kv, j * BLK : (j + 1) * BLK, :] = total[kv, first + j].astype(jnp.bfloat16)


def whole(shape):
    return pl.BlockSpec(tuple(shape), lambda *_: (0,) * len(shape))


ANYWHERE = pl.BlockSpec(memory_space=pl.ANY)


def bf16(*shape):
    return jax.ShapeDtypeStruct(shape, jnp.bfloat16)


def call(kernel, scalars, arrays, out_shapes, scratch, name, any_in=False, any_out=False, limit=VMEM_LIMIT):
    return pl.pallas_call(
        kernel,
        grid_spec=pltpu.PrefetchScalarGridSpec(
            num_scalar_prefetch=len(scalars),
            grid=(1,),
            in_specs=[ANYWHERE if any_in else whole(x.shape) for x in arrays],
            out_specs=[ANYWHERE if any_out else whole(x.shape) for x in out_shapes],
            scratch_shapes=scratch,
        ),
        out_shape=out_shapes,
        compiler_params=params(limit),
        name=name,
    )(*scalars, *arrays)


def attend(place, source, queries, out_grad, own, far, out_shapes, head, earlier, shard_count):
    tokens_here, width = queries.shape
    blocks_here = tokens_here // BLK
    slots = blocks_here + shard_count * CAP
    tile = pl.BlockSpec((STEP_BLOCKS * BLK, GROUP * HEAD_DIM), lambda i, *_: (i, head))
    near_shape = (2, blocks_here, BLK, HEAD_DIM)
    arrays = [*own, *far]
    first = 4 + len(arrays)
    return pl.pallas_call(
        functools.partial(
            attend_kernel, heads=len(own), fars=len(far), outs=len(out_shapes), head=head, shard_count=shard_count
        ),
        grid_spec=pltpu.PrefetchScalarGridSpec(
            num_scalar_prefetch=2,
            grid=(blocks_here // STEP_BLOCKS,),
            in_specs=[tile, tile] + [whole(x.shape) for x in arrays] + [ANYWHERE] * len(earlier),
            out_specs=[tile, tile, whole(near_shape)] + [whole(x.shape) for x in out_shapes],
            scratch_shapes=[
                pltpu.VMEM((2, slots, BLK, HEAD_DIM), jnp.bfloat16),
                pltpu.VMEM((2, slots, BLK, HEAD_DIM), jnp.float32),
            ],
        ),
        out_shape=[bf16(tokens_here, width), bf16(tokens_here, width), jax.ShapeDtypeStruct(near_shape, jnp.float32)]
        + out_shapes,
        input_output_aliases={first: 0, first + 1: 1} if earlier else {},
        compiler_params=params(),
        cost_estimate=pl.CostEstimate(
            flops=12 * blocks_here * LIST * BLK * GROUP * BLK * HEAD_DIM,
            bytes_accessed=20 * 1024 * 1024,
            transcendentals=blocks_here * LIST * BLK * GROUP * BLK,
        ),
        name="attend",
    )(place, source, queries, out_grad, *arrays, *earlier)


def send(x, axis, count, r):
    return lax.ppermute(x, axis, [(i, partner(i, r, count)) for i in range(count)])


def send_back(x, axis, count, r):
    return lax.ppermute(x, axis, [(i, origin(i, r, count)) for i in range(count)])


def swap(x):
    return lax.all_to_all(x, "ctx", split_axis=0, concat_axis=0, tiled=True)


def requests_of(flat_ids, blocks_here, shard_index, shard_count):
    owner = flat_ids // blocks_here
    shards = jnp.arange(shard_count, dtype=jnp.int32)
    inner = jnp.arange(blocks_here, dtype=jnp.int32)
    every_block = jnp.arange(shard_count * blocks_here, dtype=jnp.int32)
    listed = jnp.any(flat_ids[:, None] == every_block[None, :], axis=0)
    grid = listed.reshape(shard_count, blocks_here) & (shards != shard_index)[:, None]
    rank = jnp.sum((grid[:, :, None] & (inner[:, None] < inner[None, :])[None]).astype(jnp.int32), axis=1)
    hit = grid[:, None] & (rank[:, None] == jnp.arange(128, dtype=jnp.int32)[None, :, None])
    requests = jnp.sum(jnp.where(hit, inner[None, None], 0), axis=2)
    same_owner = owner[:, None] == (every_block // blocks_here)[None, :]
    place_of = jnp.sum((same_owner & listed[None, :] & (every_block[None, :] < flat_ids[:, None])).astype(jnp.int32), axis=1)
    source = jnp.where(owner == shard_index, flat_ids % blocks_here, blocks_here + owner * CAP + place_of)
    return requests, source


def per_device(queries, key_states, value_states, block_lists, out_grad):
    shard_index = lax.axis_index("ctx")
    shard_count = lax.axis_size("ctx")
    heads = lax.axis_size("head")
    blocks_here = queries.shape[0] // BLK
    quarter = key_states.shape[0]
    head_count = key_states.shape[1] // heads // HEAD_DIM
    place = jnp.stack([shard_index, lax.axis_index("head")]).astype(jnp.int32)

    pieces = call(
        split_kernel,
        [place],
        [key_states, value_states],
        [bf16(head_count, 2, quarter, HEAD_DIM)] * heads,
        [pltpu.SemaphoreType.DMA((2 * heads * head_count,))],
        "split",
        any_in=True,
        limit=VMEM_MOST,
    )
    own = [pieces[0]] + [send(pieces[r], "head", heads, r) for r in range(1, heads)]

    requests, source = requests_of(block_lists.reshape(-1), blocks_here, shard_index, shard_count)
    asked = swap(requests)

    one = (2, CAP, BLK, HEAD_DIM)
    by_step = [bf16(*one)] * (shard_count - 1)
    at_once = [bf16(shard_count, *one)]
    picked = call(
        functools.partial(pick_kernel, heads=heads, head_count=head_count, shard_count=shard_count),
        [place, asked],
        own,
        by_step + at_once * (head_count - 1),
        [pltpu.VMEM((2, blocks_here, BLK, HEAD_DIM), jnp.bfloat16)],
        "pick",
    )
    far = [[send(picked[r - 1], "ctx", shard_count, r) for r in range(1, shard_count)]]
    far += [[swap(x)] for x in picked[shard_count - 1 :]]
    earlier, nears, backs = [], [], []
    for h in range(head_count):
        last = h == head_count - 1
        attended, query_grad, near, *far_grad = attend(
            place, source, queries, out_grad, own, far[h], by_step if last else at_once, h, earlier, shard_count
        )
        earlier = [attended, query_grad]
        nears.append(near)
        if last:
            backs.append([send_back(x, "ctx", shard_count, r) for r, x in enumerate(far_grad, 1)])
        else:
            backs.append([swap(far_grad[0])])
    done = []
    for h in range(head_count):
        sums = call(
            functools.partial(gather_sum_kernel, heads=heads, shard_count=shard_count),
            [place, asked],
            [nears[h], *backs[h]],
            [bf16(2, quarter, HEAD_DIM)] * heads,
            [pltpu.VMEM((2, blocks_here, BLK, HEAD_DIM), jnp.float32)],
            "gather_sum",
        )
        done += [sums[0]] + [send_back(sums[r], "head", heads, r) for r in range(1, heads)]
    key_grad, value_grad = call(
        functools.partial(join_kernel, heads=heads),
        [place],
        done,
        [bf16(*key_states.shape)] * 2,
        [pltpu.SemaphoreType.DMA((2 * heads * head_count,))],
        "join",
        any_in=True,
        any_out=True,
    )
    return attended, query_grad, key_grad, value_grad


def solution(mesh):
    return jax.shard_map(
        per_device,
        mesh=mesh,
        in_specs=(
            P("ctx", "head"),
            P(("ctx", "head"), None),
            P(("ctx", "head"), None),
            P("ctx", None),
            P("ctx", "head"),
        ),
        out_specs=(
            P("ctx", "head"),
            P("ctx", "head"),
            P(("ctx", "head"), None),
            P(("ctx", "head"), None),
        ),
        check_vma=False,
    )
```

```python
import functools

import jax
import jax.numpy as jnp
from jax import lax
from jax.experimental import pallas as pl
from jax.experimental.pallas import tpu as pltpu
from jax.sharding import PartitionSpec as P

HEAD_DIM = 128
GROUP = 4
BLK = 64
LIST = 8
CAP = 3
STEP_BLOCKS = 2
NEG_FILL = -1e30
SCALE = HEAD_DIM ** (-0.5)
LOG2E = 1.4426950408889634
VMEM_LIMIT = 50 * 1024 * 1024
VMEM_MOST = 60 * 1024 * 1024

NT = (((1,), (1,)), ((), ()))
NN = (((1,), (0,)), ((), ()))
TN = (((0,), (0,)), ((), ()))


def dot(a, b, dims):
    return lax.dot_general(a, b, dims, preferred_element_type=jnp.float32)


def params(limit=VMEM_LIMIT):
    return pltpu.CompilerParams(vmem_limit_bytes=limit)


def partner(me, r, count):
    return me ^ r if count & (count - 1) == 0 else (me + r) % count


def origin(me, r, count):
    return me ^ r if count & (count - 1) == 0 else (me + count - r) % count


def step_to(me, there, count):
    return me ^ there if count & (count - 1) == 0 else (there + count - me) % count


def head_columns(place, r, heads, h, head_count):
    col = (partner(place[1], r, heads) * head_count + h) * HEAD_DIM
    return pl.ds(pl.multiple_of(col, HEAD_DIM), HEAD_DIM)


def split_kernel(place, k_ref, v_ref, *outs, heads):
    for at, out in enumerate(outs):
        cols = head_columns(place, at % heads, heads, at // heads, len(outs) // heads)
        out[0] = k_ref[:, cols]
        out[1] = v_ref[:, cols]


def join_kernel(place, *refs, heads):
    *pieces, k_ref, v_ref, sem = refs
    head_count = len(pieces) // heads
    copies = []
    for at, piece in enumerate(pieces):
        cols = head_columns(place, at % heads, heads, at // heads, head_count)
        for kv, ref in enumerate((k_ref, v_ref)):
            copies.append(pltpu.make_async_copy(piece.at[kv], ref.at[:, cols], sem.at[2 * at + kv]))
    for copy in copies:
        copy.start()
    for copy in copies:
        copy.wait()


def fill_table(place, own, table):
    heads = len(own)
    per_quarter = own[0].shape[1] // BLK
    for r in range(heads):
        first = origin(place[1], r, heads) * per_quarter
        for kv in range(2):
            for j in range(per_quarter):
                table[kv, first + j] = own[r][kv, j * BLK : (j + 1) * BLK, :]


def parts_of(refs, place, at, shard_count):
    if len(refs) == 1 and len(refs[0].shape) == 5:
        return [(refs[0].at[c], c, step_to(place[0], c, shard_count)) for c in range(shard_count)]
    return [(ref, at(place[0], r, shard_count), r) for r, ref in enumerate(refs, 1)]


def pick_kernel(place, asked, *refs, heads, shard_count):
    own, outs, table = refs[:heads], refs[heads:-1], refs[-1]
    fill_table(place, own, table)
    for out, _, r in parts_of(outs, place, partner, shard_count):
        for s in range(CAP):
            block = asked[r * CAP + s]
            for kv in range(2):
                out[kv, s] = table[kv, block]


def attend_kernel(place, source, q_ref, g_ref, *refs, heads, fars, outs, shard_count):
    own, far = refs[:heads], refs[heads : heads + fars]
    table, total = refs[-2:]
    far_out = refs[-2 - outs : -2]
    o_ref, dq_ref, near_out = refs[-5 - outs : -2 - outs]
    step = pl.program_id(0)
    blocks_here = near_out.shape[1]

    @pl.when(step == 0)
    def _():
        fill_table(place, own, table)
        for part, c, _ in parts_of(far, place, origin, shard_count):
            for kv in range(2):
                for s in range(CAP):
                    table[kv, blocks_here + c * CAP + s] = part[kv, s]
        total[...] = jnp.zeros_like(total)

    key_row = lax.broadcasted_iota(jnp.int32, (BLK, GROUP * BLK), 0)
    query_col = lax.broadcasted_iota(jnp.int32, (BLK, GROUP * BLK), 1) % BLK
    hidden = key_row > query_col
    for sub in range(STEP_BLOCKS):
        block = step * STEP_BLOCKS + sub
        rows = slice(sub * BLK, (sub + 1) * BLK)
        listed = [source[block * LIST + e] for e in range(LIST)]
        q = jnp.concatenate([q_ref[rows, g * HEAD_DIM : (g + 1) * HEAD_DIM] for g in range(GROUP)], axis=0)
        g_out = jnp.concatenate([g_ref[rows, g * HEAD_DIM : (g + 1) * HEAD_DIM] for g in range(GROUP)], axis=0)
        keys = jnp.concatenate([table[0, at] for at in listed], axis=0)
        values = jnp.concatenate([table[1, at] for at in listed], axis=0)
        scores = dot(keys, q, NT)
        parts = []
        for e in range(LIST):
            part = scores[e * BLK : (e + 1) * BLK]
            mask = hidden if e == 0 else hidden & (listed[e] == block)
            parts.append(jnp.where(mask, NEG_FILL, part))
        scores = jnp.concatenate(parts, axis=0)
        peak = jnp.max(scores, axis=0, keepdims=True)
        expo = jnp.exp2((scores - peak) * (SCALE * LOG2E))
        probs = expo * (1.0 / jnp.sum(expo, axis=0, keepdims=True))
        probs_low = probs.astype(jnp.bfloat16)
        dprob = dot(values, g_out, NT)
        delta = jnp.sum(probs * dprob, axis=0, keepdims=True)
        dscore = (probs * (dprob - delta)).astype(jnp.bfloat16)
        attended = dot(values, probs_low, TN).T.astype(jnp.bfloat16)
        dq = (dot(keys, dscore, TN) * SCALE).T.astype(jnp.bfloat16)
        for g in range(GROUP):
            cols = slice(g * HEAD_DIM, (g + 1) * HEAD_DIM)
            o_ref[rows, cols] = attended[g * BLK : (g + 1) * BLK]
            dq_ref[rows, cols] = dq[g * BLK : (g + 1) * BLK]
        dk = dot(dscore, q, NN)
        dv = dot(probs_low, g_out, NN)
        for e in range(LIST):
            total[0, listed[e]] += dk[e * BLK : (e + 1) * BLK]
            total[1, listed[e]] += dv[e * BLK : (e + 1) * BLK]

    @pl.when(step == pl.num_programs(0) - 1)
    def _():
        for kv, factor in ((0, SCALE), (1, 1.0)):
            near_out[kv] = total[kv, :blocks_here] * factor
            for out, c, _ in parts_of(far_out, place, origin, shard_count):
                for s in range(CAP):
                    out[kv, s] = (total[kv, blocks_here + c * CAP + s] * factor).astype(jnp.bfloat16)


def gather_sum_kernel(place, asked, near, *refs, heads, shard_count):
    back, outs, total = refs[: -heads - 1], refs[-heads - 1 : -1], refs[-1]
    per_quarter = outs[0].shape[1] // BLK
    total[...] = near[...]
    for part, _, r in parts_of(back, place, partner, shard_count):
        for s in range(CAP):
            block = asked[r * CAP + s]
            for kv in range(2):
                total[kv, block] += part[kv, s].astype(jnp.float32)
    for r in range(heads):
        first = origin(place[1], r, heads) * per_quarter
        for kv in range(2):
            for j in range(per_quarter):
                outs[r][kv, j * BLK : (j + 1) * BLK, :] = total[kv, first + j].astype(jnp.bfloat16)


def whole(shape):
    return pl.BlockSpec(tuple(shape), lambda *_: (0,) * len(shape))


ANYWHERE = pl.BlockSpec(memory_space=pl.ANY)


def bf16(*shape):
    return jax.ShapeDtypeStruct(shape, jnp.bfloat16)


def call(kernel, scalars, arrays, out_shapes, scratch, name, any_in=False, any_out=False, limit=VMEM_LIMIT):
    return pl.pallas_call(
        kernel,
        grid_spec=pltpu.PrefetchScalarGridSpec(
            num_scalar_prefetch=len(scalars),
            grid=(1,),
            in_specs=[ANYWHERE if any_in else whole(x.shape) for x in arrays],
            out_specs=[ANYWHERE if any_out else whole(x.shape) for x in out_shapes],
            scratch_shapes=scratch,
        ),
        out_shape=out_shapes,
        compiler_params=params(limit),
        name=name,
    )(*scalars, *arrays)


def attend(place, source, queries, out_grad, own, far, out_shapes, head, earlier, shard_count):
    tokens_here, width = queries.shape
    blocks_here = tokens_here // BLK
    slots = blocks_here + shard_count * CAP
    tile = pl.BlockSpec((STEP_BLOCKS * BLK, GROUP * HEAD_DIM), lambda i, *_: (i, head))
    near_shape = (2, blocks_here, BLK, HEAD_DIM)
    arrays = [*own, *far]
    first = 4 + len(arrays)
    return pl.pallas_call(
        functools.partial(
            attend_kernel, heads=len(own), fars=len(far), outs=len(out_shapes), shard_count=shard_count
        ),
        grid_spec=pltpu.PrefetchScalarGridSpec(
            num_scalar_prefetch=2,
            grid=(blocks_here // STEP_BLOCKS,),
            in_specs=[tile, tile] + [whole(x.shape) for x in arrays] + [ANYWHERE] * len(earlier),
            out_specs=[tile, tile, whole(near_shape)] + [whole(x.shape) for x in out_shapes],
            scratch_shapes=[
                pltpu.VMEM((2, slots, BLK, HEAD_DIM), jnp.bfloat16),
                pltpu.VMEM((2, slots, BLK, HEAD_DIM), jnp.float32),
            ],
        ),
        out_shape=[bf16(tokens_here, width), bf16(tokens_here, width), jax.ShapeDtypeStruct(near_shape, jnp.float32)]
        + out_shapes,
        input_output_aliases={first: 0, first + 1: 1} if earlier else {},
        compiler_params=params(),
        cost_estimate=pl.CostEstimate(
            flops=12 * blocks_here * LIST * BLK * GROUP * BLK * HEAD_DIM,
            bytes_accessed=20 * 1024 * 1024,
            transcendentals=blocks_here * LIST * BLK * GROUP * BLK,
        ),
        name="attend",
    )(place, source, queries, out_grad, *arrays, *earlier)


def send(x, axis, count, r):
    return lax.ppermute(x, axis, [(i, partner(i, r, count)) for i in range(count)])


def send_back(x, axis, count, r):
    return lax.ppermute(x, axis, [(i, origin(i, r, count)) for i in range(count)])


def swap(x):
    return lax.all_to_all(x, "ctx", split_axis=0, concat_axis=0, tiled=True)


def asked_of(lists, blocks_here, shard_index):
    inner = jnp.arange(blocks_here, dtype=jnp.int32)
    hits = jnp.any(lists[:, :, :, None] == (shard_index * blocks_here + inner)[None, None, None, :], axis=(1, 2))
    rank = jnp.sum((hits[:, :, None] & (inner[:, None] < inner[None, :])[None]).astype(jnp.int32), axis=1)
    slot = hits[:, None] & (rank[:, None] == jnp.arange(CAP, dtype=jnp.int32)[None, :, None])
    blocks = jnp.sum(jnp.where(slot, inner[None, None], 0), axis=2)
    return jnp.pad(blocks.reshape(-1), (CAP, 0))


def source_of(flat_ids, blocks_here, shard_index, shard_count):
    owner = flat_ids // blocks_here
    every_block = jnp.arange(shard_count * blocks_here, dtype=jnp.int32)
    listed = jnp.any(flat_ids[:, None] == every_block[None, :], axis=0)
    same_owner = owner[:, None] == (every_block // blocks_here)[None, :]
    rank = jnp.sum((same_owner & listed[None, :] & (every_block[None, :] < flat_ids[:, None])).astype(jnp.int32), axis=1)
    return jnp.where(owner == shard_index, flat_ids % blocks_here, blocks_here + owner * CAP + rank)


def after(x, *others):
    return lax.optimization_barrier((x, *others))[0]


def per_device(queries, key_states, value_states, block_lists, out_grad):
    shard_index = lax.axis_index("ctx")
    shard_count = lax.axis_size("ctx")
    heads = lax.axis_size("head")
    blocks_here = queries.shape[0] // BLK
    quarter = key_states.shape[0]
    head_count = key_states.shape[1] // heads // HEAD_DIM
    place = jnp.stack([shard_index, lax.axis_index("head")]).astype(jnp.int32)

    pieces = call(
        functools.partial(split_kernel, heads=heads),
        [place],
        [key_states, value_states],
        [bf16(2, quarter, HEAD_DIM)] * (heads * head_count),
        [],
        "split",
        limit=VMEM_MOST,
    )
    own, lists = [], []
    for h in range(head_count):
        parts = pieces[h * heads : (h + 1) * heads]
        if h:
            parts = [after(x, lists[0]) for x in parts]
        own.append([parts[0]] + [send(parts[r], "head", heads, r) for r in range(1, heads)])
        if not h:
            lists_here = after(block_lists, *own[0][:2])
            lists = [send_back(lists_here, "ctx", shard_count, r) for r in range(1, shard_count)]
    asked = asked_of(jnp.stack(lists), blocks_here, shard_index)
    source = source_of(block_lists.reshape(-1), blocks_here, shard_index, shard_count)

    one = (2, CAP, BLK, HEAD_DIM)
    by_step = [bf16(*one)] * (shard_count - 1)
    at_once = [bf16(shard_count, *one)]
    far = []
    for h in range(head_count):
        picked = call(
            functools.partial(pick_kernel, heads=heads, shard_count=shard_count),
            [place, asked],
            own[h],
            at_once if h else by_step,
            [pltpu.VMEM((2, blocks_here, BLK, HEAD_DIM), jnp.bfloat16)],
            "pick",
        )
        if h:
            far.append([swap(after(picked[0], far[0][-2]))])
        else:
            far.append([send(x, "ctx", shard_count, r) for r, x in enumerate(picked, 1)])
    earlier, nears, backs = [], [], []
    for h in range(head_count):
        last = h == head_count - 1
        attended, query_grad, near, *far_grad = attend(
            place, source, queries, out_grad, own[h], far[h], by_step if last else at_once, h, earlier, shard_count
        )
        earlier = [attended, query_grad]
        nears.append(near)
        if last:
            backs.append([send_back(x, "ctx", shard_count, r) for r, x in enumerate(far_grad, 1)])
        else:
            backs.append([swap(after(far_grad[0], *far[h + 1]))])
    done = []
    for h in range(head_count):
        sums = call(
            functools.partial(gather_sum_kernel, heads=heads, shard_count=shard_count),
            [place, asked],
            [after(nears[h], *done[-1:]), *backs[h]],
            [bf16(2, quarter, HEAD_DIM)] * heads,
            [pltpu.VMEM((2, blocks_here, BLK, HEAD_DIM), jnp.float32)],
            "gather_sum",
        )
        done += [sums[0]] + [send_back(sums[r], "head", heads, r) for r in range(1, heads)]
    key_grad, value_grad = call(
        functools.partial(join_kernel, heads=heads),
        [place],
        done,
        [bf16(*key_states.shape)] * 2,
        [pltpu.SemaphoreType.DMA((2 * heads * head_count,))],
        "join",
        any_in=True,
        any_out=True,
    )
    return attended, query_grad, key_grad, value_grad


def solution(mesh):
    return jax.shard_map(
        per_device,
        mesh=mesh,
        in_specs=(
            P("ctx", "head"),
            P(("ctx", "head"), None),
            P(("ctx", "head"), None),
            P("ctx", None),
            P("ctx", "head"),
        ),
        out_specs=(
            P("ctx", "head"),
            P("ctx", "head"),
            P(("ctx", "head"), None),
            P(("ctx", "head"), None),
        ),
        check_vma=False,
    )
```

```python
import functools

import jax
import jax.numpy as jnp
from jax import lax
from jax.experimental import pallas as pl
from jax.experimental.pallas import tpu as pltpu
from jax.sharding import PartitionSpec as P

HEAD_DIM = 128
GROUP = 4
BLK = 64
LIST = 8
CAP = 3
STEP_BLOCKS = 2
NEG_FILL = -1e30
SCALE = HEAD_DIM ** (-0.5)
LOG2E = 1.4426950408889634
VMEM_LIMIT = 50 * 1024 * 1024
VMEM_MOST = 60 * 1024 * 1024

NT = (((1,), (1,)), ((), ()))
NN = (((1,), (0,)), ((), ()))
TN = (((0,), (0,)), ((), ()))


def dot(a, b, dims):
    return lax.dot_general(a, b, dims, preferred_element_type=jnp.float32)


def params(limit=VMEM_LIMIT):
    return pltpu.CompilerParams(vmem_limit_bytes=limit)


def partner(me, r, count):
    return me ^ r if count & (count - 1) == 0 else (me + r) % count


def origin(me, r, count):
    return me ^ r if count & (count - 1) == 0 else (me + count - r) % count


def head_columns(place, r, heads, h, head_count):
    col = (partner(place[1], r, heads) * head_count + h) * HEAD_DIM
    return pl.ds(pl.multiple_of(col, HEAD_DIM), HEAD_DIM)


def split_kernel(place, k_ref, v_ref, *refs):
    *outs, sem = refs
    heads, head_count = len(outs), outs[0].shape[0]
    copies = []
    for r, out in enumerate(outs):
        for h in range(head_count):
            cols = head_columns(place, r, heads, h, head_count)
            for kv, ref in enumerate((k_ref, v_ref)):
                at = (r * head_count + h) * 2 + kv
                copies.append(pltpu.make_async_copy(ref.at[:, cols], out.at[h, kv], sem.at[at]))
    for copy in copies:
        copy.start()
    for copy in copies:
        copy.wait()


def join_kernel(place, *refs, heads):
    *pieces, k_ref, v_ref, sem = refs
    head_count = len(pieces) // heads
    copies = []
    for at, piece in enumerate(pieces):
        cols = head_columns(place, at % heads, heads, at // heads, head_count)
        for kv, ref in enumerate((k_ref, v_ref)):
            copies.append(pltpu.make_async_copy(piece.at[kv], ref.at[:, cols], sem.at[2 * at + kv]))
    for copy in copies:
        copy.start()
    for copy in copies:
        copy.wait()


def fill_table(place, own, h, table):
    heads = len(own)
    per_quarter = own[0].shape[2] // BLK
    for r in range(heads):
        first = origin(place[1], r, heads) * per_quarter
        for kv in range(2):
            for j in range(per_quarter):
                table[kv, first + j] = own[r][h, kv, j * BLK : (j + 1) * BLK, :]


def parts_of(refs, place, at, shard_count):
    if len(refs) == 1 and len(refs[0].shape) == 5:
        return [(refs[0].at[c], c) for c in range(shard_count)]
    return [(ref, at(place[0], r, shard_count)) for r, ref in enumerate(refs, 1)]


def pick_kernel(place, asked, *refs, heads, head_count, shard_count):
    own, outs, table = refs[:heads], refs[heads:-1], refs[-1]
    for h in range(head_count):
        fill_table(place, own, h, table)
        steps = shard_count - 1
        mine = outs[:steps] if h == 0 else outs[steps + h - 1 : steps + h]
        for out, c in parts_of(mine, place, partner, shard_count):
            for s in range(CAP):
                block = asked[c, s]
                for kv in range(2):
                    out[kv, s] = table[kv, block]


def attend_kernel(place, source, q_ref, g_ref, *refs, heads, fars, outs, head, shard_count):
    own, far = refs[:heads], refs[heads : heads + fars]
    table, total = refs[-2:]
    far_out = refs[-2 - outs : -2]
    o_ref, dq_ref, near_out = refs[-5 - outs : -2 - outs]
    step = pl.program_id(0)
    blocks_here = near_out.shape[1]

    @pl.when(step == 0)
    def _():
        fill_table(place, own, head, table)
        for part, c in parts_of(far, place, origin, shard_count):
            for kv in range(2):
                for s in range(CAP):
                    table[kv, blocks_here + c * CAP + s] = part[kv, s]
        total[...] = jnp.zeros_like(total)

    key_row = lax.broadcasted_iota(jnp.int32, (BLK, GROUP * BLK), 0)
    query_col = lax.broadcasted_iota(jnp.int32, (BLK, GROUP * BLK), 1) % BLK
    hidden = key_row > query_col
    for sub in range(STEP_BLOCKS):
        block = step * STEP_BLOCKS + sub
        rows = slice(sub * BLK, (sub + 1) * BLK)
        listed = [source[block * LIST + e] for e in range(LIST)]
        q = jnp.concatenate([q_ref[rows, g * HEAD_DIM : (g + 1) * HEAD_DIM] for g in range(GROUP)], axis=0)
        g_out = jnp.concatenate([g_ref[rows, g * HEAD_DIM : (g + 1) * HEAD_DIM] for g in range(GROUP)], axis=0)
        keys = jnp.concatenate([table[0, at] for at in listed], axis=0)
        values = jnp.concatenate([table[1, at] for at in listed], axis=0)
        scores = dot(keys, q, NT)
        parts = []
        for e in range(LIST):
            part = scores[e * BLK : (e + 1) * BLK]
            mask = hidden if e == 0 else hidden & (listed[e] == block)
            parts.append(jnp.where(mask, NEG_FILL, part))
        scores = jnp.concatenate(parts, axis=0)
        peak = jnp.max(scores, axis=0, keepdims=True)
        expo = jnp.exp2((scores - peak) * (SCALE * LOG2E))
        probs = expo * (1.0 / jnp.sum(expo, axis=0, keepdims=True))
        probs_low = probs.astype(jnp.bfloat16)
        dprob = dot(values, g_out, NT)
        delta = jnp.sum(probs * dprob, axis=0, keepdims=True)
        dscore = (probs * (dprob - delta)).astype(jnp.bfloat16)
        attended = dot(values, probs_low, TN).T.astype(jnp.bfloat16)
        dq = (dot(keys, dscore, TN) * SCALE).T.astype(jnp.bfloat16)
        for g in range(GROUP):
            cols = slice(g * HEAD_DIM, (g + 1) * HEAD_DIM)
            o_ref[rows, cols] = attended[g * BLK : (g + 1) * BLK]
            dq_ref[rows, cols] = dq[g * BLK : (g + 1) * BLK]
        dk = dot(dscore, q, NN)
        dv = dot(probs_low, g_out, NN)
        for e in range(LIST):
            total[0, listed[e]] += dk[e * BLK : (e + 1) * BLK]
            total[1, listed[e]] += dv[e * BLK : (e + 1) * BLK]

    @pl.when(step == pl.num_programs(0) - 1)
    def _():
        for kv, factor in ((0, SCALE), (1, 1.0)):
            near_out[kv] = total[kv, :blocks_here] * factor
            for out, c in parts_of(far_out, place, origin, shard_count):
                for s in range(CAP):
                    out[kv, s] = (total[kv, blocks_here + c * CAP + s] * factor).astype(jnp.bfloat16)


def gather_sum_kernel(place, asked, near, *refs, heads, shard_count):
    back, outs, total = refs[: -heads - 1], refs[-heads - 1 : -1], refs[-1]
    per_quarter = outs[0].shape[1] // BLK
    total[...] = near[...]
    for part, c in parts_of(back, place, partner, shard_count):
        for s in range(CAP):
            block = asked[c, s]
            for kv in range(2):
                total[kv, block] += part[kv, s].astype(jnp.float32)
    for r in range(heads):
        first = origin(place[1], r, heads) * per_quarter
        for kv in range(2):
            for j in range(per_quarter):
                outs[r][kv, j * BLK : (j + 1) * BLK, :] = total[kv, first + j].astype(jnp.bfloat16)


def whole(shape):
    return pl.BlockSpec(tuple(shape), lambda *_: (0,) * len(shape))


ANYWHERE = pl.BlockSpec(memory_space=pl.ANY)


def bf16(*shape):
    return jax.ShapeDtypeStruct(shape, jnp.bfloat16)


def call(kernel, scalars, arrays, out_shapes, scratch, name, any_in=False, any_out=False, limit=VMEM_LIMIT):
    return pl.pallas_call(
        kernel,
        grid_spec=pltpu.PrefetchScalarGridSpec(
            num_scalar_prefetch=len(scalars),
            grid=(1,),
            in_specs=[ANYWHERE if any_in else whole(x.shape) for x in arrays],
            out_specs=[ANYWHERE if any_out else whole(x.shape) for x in out_shapes],
            scratch_shapes=scratch,
        ),
        out_shape=out_shapes,
        compiler_params=params(limit),
        name=name,
    )(*scalars, *arrays)


def attend(place, source, queries, out_grad, own, far, out_shapes, head, earlier, shard_count):
    tokens_here, width = queries.shape
    blocks_here = tokens_here // BLK
    slots = blocks_here + shard_count * CAP
    tile = pl.BlockSpec((STEP_BLOCKS * BLK, GROUP * HEAD_DIM), lambda i, *_: (i, head))
    near_shape = (2, blocks_here, BLK, HEAD_DIM)
    arrays = [*own, *far]
    first = 4 + len(arrays)
    return pl.pallas_call(
        functools.partial(
            attend_kernel, heads=len(own), fars=len(far), outs=len(out_shapes), head=head, shard_count=shard_count
        ),
        grid_spec=pltpu.PrefetchScalarGridSpec(
            num_scalar_prefetch=2,
            grid=(blocks_here // STEP_BLOCKS,),
            in_specs=[tile, tile] + [whole(x.shape) for x in arrays] + [ANYWHERE] * len(earlier),
            out_specs=[tile, tile, whole(near_shape)] + [whole(x.shape) for x in out_shapes],
            scratch_shapes=[
                pltpu.VMEM((2, slots, BLK, HEAD_DIM), jnp.bfloat16),
                pltpu.VMEM((2, slots, BLK, HEAD_DIM), jnp.float32),
            ],
        ),
        out_shape=[bf16(tokens_here, width), bf16(tokens_here, width), jax.ShapeDtypeStruct(near_shape, jnp.float32)]
        + out_shapes,
        input_output_aliases={first: 0, first + 1: 1} if earlier else {},
        compiler_params=params(),
        cost_estimate=pl.CostEstimate(
            flops=12 * blocks_here * LIST * BLK * GROUP * BLK * HEAD_DIM,
            bytes_accessed=20 * 1024 * 1024,
            transcendentals=blocks_here * LIST * BLK * GROUP * BLK,
        ),
        name="attend",
    )(place, source, queries, out_grad, *arrays, *earlier)


def send(x, axis, count, r):
    return lax.ppermute(x, axis, [(i, partner(i, r, count)) for i in range(count)])


def send_back(x, axis, count, r):
    return lax.ppermute(x, axis, [(i, origin(i, r, count)) for i in range(count)])


def swap(x):
    return lax.all_to_all(x, "ctx", split_axis=0, concat_axis=0, tiled=True)


def requests_of(flat_ids, blocks_here, shard_index, shard_count):
    owner = flat_ids // blocks_here
    shards = jnp.arange(shard_count, dtype=jnp.int32)
    inner = jnp.arange(blocks_here, dtype=jnp.int32)
    every_block = jnp.arange(shard_count * blocks_here, dtype=jnp.int32)
    listed = jnp.any(flat_ids[:, None] == every_block[None, :], axis=0)
    grid = listed.reshape(shard_count, blocks_here) & (shards != shard_index)[:, None]
    rank = jnp.sum((grid[:, :, None] & (inner[:, None] < inner[None, :])[None]).astype(jnp.int32), axis=1)
    hit = grid[:, None] & (rank[:, None] == jnp.arange(128, dtype=jnp.int32)[None, :, None])
    requests = jnp.sum(jnp.where(hit, inner[None, None], 0), axis=2)
    same_owner = owner[:, None] == (every_block // blocks_here)[None, :]
    place_of = jnp.sum((same_owner & listed[None, :] & (every_block[None, :] < flat_ids[:, None])).astype(jnp.int32), axis=1)
    source = jnp.where(owner == shard_index, flat_ids % blocks_here, blocks_here + owner * CAP + place_of)
    return requests, source


def after(x, *others):
    return lax.optimization_barrier((x, *others))[0]


def per_device(queries, key_states, value_states, block_lists, out_grad):
    shard_index = lax.axis_index("ctx")
    shard_count = lax.axis_size("ctx")
    heads = lax.axis_size("head")
    blocks_here = queries.shape[0] // BLK
    quarter = key_states.shape[0]
    head_count = key_states.shape[1] // heads // HEAD_DIM
    place = jnp.stack([shard_index, lax.axis_index("head")]).astype(jnp.int32)

    pieces = call(
        split_kernel,
        [place],
        [key_states, value_states],
        [bf16(head_count, 2, quarter, HEAD_DIM)] * heads,
        [pltpu.SemaphoreType.DMA((2 * heads * head_count,))],
        "split",
        any_in=True,
        limit=VMEM_MOST,
    )
    own = [pieces[0]] + [send(pieces[r], "head", heads, r) for r in range(1, heads)]

    requests, source = requests_of(block_lists.reshape(-1), blocks_here, shard_index, shard_count)
    asked = swap(requests)

    one = (2, CAP, BLK, HEAD_DIM)
    by_step = [bf16(*one)] * (shard_count - 1)
    at_once = [bf16(shard_count, *one)]
    picked = call(
        functools.partial(pick_kernel, heads=heads, head_count=head_count, shard_count=shard_count),
        [place, asked],
        own,
        by_step + at_once * (head_count - 1),
        [pltpu.VMEM((2, blocks_here, BLK, HEAD_DIM), jnp.bfloat16)],
        "pick",
    )
    far = [[send(picked[r - 1], "ctx", shard_count, r) for r in range(1, shard_count)]]
    for x in picked[shard_count - 1 :]:
        far.append([swap(after(x, *far[-1]))])
    earlier, nears, backs = [], [], []
    for h in range(head_count):
        last = h == head_count - 1
        attended, query_grad, near, *far_grad = attend(
            place, source, queries, out_grad, own, far[h], by_step if last else at_once, h, earlier, shard_count
        )
        earlier = [attended, query_grad]
        nears.append(near)
        if last:
            backs.append([send_back(x, "ctx", shard_count, r) for r, x in enumerate(far_grad, 1)])
        else:
            backs.append([swap(after(far_grad[0], *far[h + 1]))])
    done = []
    for h in range(head_count):
        sums = call(
            functools.partial(gather_sum_kernel, heads=heads, shard_count=shard_count),
            [place, asked],
            [after(nears[h], nears[-1], *done[-1:]), *backs[h]],
            [bf16(2, quarter, HEAD_DIM)] * heads,
            [pltpu.VMEM((2, blocks_here, BLK, HEAD_DIM), jnp.float32)],
            "gather_sum",
        )
        done += [sums[0]] + [send_back(sums[r], "head", heads, r) for r in range(1, heads)]
    key_grad, value_grad = call(
        functools.partial(join_kernel, heads=heads),
        [place],
        done,
        [bf16(*key_states.shape)] * 2,
        [pltpu.SemaphoreType.DMA((2 * heads * head_count,))],
        "join",
        any_in=True,
        any_out=True,
    )
    return attended, query_grad, key_grad, value_grad


def solution(mesh):
    return jax.shard_map(
        per_device,
        mesh=mesh,
        in_specs=(
            P("ctx", "head"),
            P(("ctx", "head"), None),
            P(("ctx", "head"), None),
            P("ctx", None),
            P("ctx", "head"),
        ),
        out_specs=(
            P("ctx", "head"),
            P("ctx", "head"),
            P(("ctx", "head"), None),
            P(("ctx", "head"), None),
        ),
        check_vma=False,
    )
```

```python
import functools

import jax
import jax.numpy as jnp
from jax import lax
from jax.experimental import pallas as pl
from jax.experimental.pallas import tpu as pltpu
from jax.sharding import PartitionSpec as P

HEAD_DIM = 128
GROUP = 4
BLK = 64
LIST = 8
CAP = 3
STEP_BLOCKS = 2
NEG_FILL = -1e30
SCALE = HEAD_DIM ** (-0.5)
LOG2E = 1.4426950408889634
VMEM_LIMIT = 50 * 1024 * 1024
VMEM_MOST = 60 * 1024 * 1024

NT = (((1,), (1,)), ((), ()))
NN = (((1,), (0,)), ((), ()))
TN = (((0,), (0,)), ((), ()))


def dot(a, b, dims):
    return lax.dot_general(a, b, dims, preferred_element_type=jnp.float32)


def params(limit=VMEM_LIMIT):
    return pltpu.CompilerParams(vmem_limit_bytes=limit)


def partner(me, r, count):
    return me ^ r if count & (count - 1) == 0 else (me + r) % count


def origin(me, r, count):
    return me ^ r if count & (count - 1) == 0 else (me + count - r) % count


def head_columns(place, r, heads, h, head_count):
    col = (partner(place[1], r, heads) * head_count + h) * HEAD_DIM
    return pl.ds(pl.multiple_of(col, HEAD_DIM), HEAD_DIM)


def split_kernel(place, k_ref, v_ref, *refs):
    *outs, sem = refs
    heads, head_count = len(outs), outs[0].shape[0]
    copies = []
    for r, out in enumerate(outs):
        for h in range(head_count):
            cols = head_columns(place, r, heads, h, head_count)
            for kv, ref in enumerate((k_ref, v_ref)):
                at = (r * head_count + h) * 2 + kv
                copies.append(pltpu.make_async_copy(ref.at[:, cols], out.at[h, kv], sem.at[at]))
    for copy in copies:
        copy.start()
    for copy in copies:
        copy.wait()


def join_kernel(place, *refs, heads):
    *pieces, k_ref, v_ref, sem = refs
    head_count = len(pieces) // heads
    copies = []
    for at, piece in enumerate(pieces):
        cols = head_columns(place, at % heads, heads, at // heads, head_count)
        for kv, ref in enumerate((k_ref, v_ref)):
            copies.append(pltpu.make_async_copy(piece.at[kv], ref.at[:, cols], sem.at[2 * at + kv]))
    for copy in copies:
        copy.start()
    for copy in copies:
        copy.wait()


def fill_table(place, own, h, table):
    heads = len(own)
    per_quarter = own[0].shape[2] // BLK
    for r in range(heads):
        first = origin(place[1], r, heads) * per_quarter
        for kv in range(2):
            for j in range(per_quarter):
                table[kv, first + j] = own[r][h, kv, j * BLK : (j + 1) * BLK, :]


def pick(table, asked, there, out):
    for s in range(CAP):
        block = asked[there, s]
        for kv in range(2):
            out[kv, s] = table[kv, block]


def pick_kernel(place, asked, *refs, heads, shard_count):
    own, outs, table = refs[:heads], refs[heads:-1], refs[-1]
    fill_table(place, own, 0, table)
    for r, out in enumerate(outs, 1):
        pick(table, asked, partner(place[0], r, shard_count), out)


def attend_kernel(place, source, asked, q_ref, g_ref, *refs, heads, head, last, shard_count):
    steps = shard_count - 1
    own, far = refs[:heads], refs[heads : heads + steps]
    table, total = refs[-2:]
    outs = refs[-2 - steps : -2]
    o_ref, dq_ref, near_out = refs[-5 - steps : -2 - steps]
    step = pl.program_id(0)
    blocks_here = near_out.shape[1]

    @pl.when(step == 0)
    def _():
        fill_table(place, own, head, table)
        for r, part in enumerate(far, 1):
            first = blocks_here + origin(place[0], r, shard_count) * CAP
            for kv in range(2):
                for s in range(CAP):
                    table[kv, first + s] = part[kv, s]
        total[...] = jnp.zeros_like(total)

    key_row = lax.broadcasted_iota(jnp.int32, (BLK, GROUP * BLK), 0)
    query_col = lax.broadcasted_iota(jnp.int32, (BLK, GROUP * BLK), 1) % BLK
    hidden = key_row > query_col
    for sub in range(STEP_BLOCKS):
        block = step * STEP_BLOCKS + sub
        rows = slice(sub * BLK, (sub + 1) * BLK)
        listed = [source[block * LIST + e] for e in range(LIST)]
        q = jnp.concatenate([q_ref[rows, g * HEAD_DIM : (g + 1) * HEAD_DIM] for g in range(GROUP)], axis=0)
        g_out = jnp.concatenate([g_ref[rows, g * HEAD_DIM : (g + 1) * HEAD_DIM] for g in range(GROUP)], axis=0)
        keys = jnp.concatenate([table[0, at] for at in listed], axis=0)
        values = jnp.concatenate([table[1, at] for at in listed], axis=0)
        scores = dot(keys, q, NT)
        parts = []
        for e in range(LIST):
            part = scores[e * BLK : (e + 1) * BLK]
            mask = hidden if e == 0 else hidden & (listed[e] == block)
            parts.append(jnp.where(mask, NEG_FILL, part))
        scores = jnp.concatenate(parts, axis=0)
        peak = jnp.max(scores, axis=0, keepdims=True)
        expo = jnp.exp2((scores - peak) * (SCALE * LOG2E))
        probs = expo * (1.0 / jnp.sum(expo, axis=0, keepdims=True))
        probs_low = probs.astype(jnp.bfloat16)
        dprob = dot(values, g_out, NT)
        delta = jnp.sum(probs * dprob, axis=0, keepdims=True)
        dscore = (probs * (dprob - delta)).astype(jnp.bfloat16)
        attended = dot(values, probs_low, TN).T.astype(jnp.bfloat16)
        dq = (dot(keys, dscore, TN) * SCALE).T.astype(jnp.bfloat16)
        for g in range(GROUP):
            cols = slice(g * HEAD_DIM, (g + 1) * HEAD_DIM)
            o_ref[rows, cols] = attended[g * BLK : (g + 1) * BLK]
            dq_ref[rows, cols] = dq[g * BLK : (g + 1) * BLK]
        dk = dot(dscore, q, NN)
        dv = dot(probs_low, g_out, NN)
        for e in range(LIST):
            total[0, listed[e]] += dk[e * BLK : (e + 1) * BLK]
            total[1, listed[e]] += dv[e * BLK : (e + 1) * BLK]

    @pl.when(step == pl.num_programs(0) - 1)
    def _():
        for kv, factor in ((0, SCALE), (1, 1.0)):
            near_out[kv] = total[kv, :blocks_here] * factor
        if not last:
            fill_table(place, own, head + 1, table)
        for r, out in enumerate(outs, 1):
            there = partner(place[0], r, shard_count)

            @pl.when(there < place[0])
            def _():
                for kv, factor in ((0, SCALE), (1, 1.0)):
                    for s in range(CAP):
                        out[kv, s] = (total[kv, blocks_here + there * CAP + s] * factor).astype(jnp.bfloat16)

            @pl.when(there > place[0])
            def _():
                if last:
                    out[...] = jnp.zeros_like(out)
                else:
                    pick(table, asked, there, out)


def gather_sum_kernel(place, asked, near, *refs, heads, shard_count):
    back, outs, total = refs[: -heads - 1], refs[-heads - 1 : -1], refs[-1]
    per_quarter = outs[0].shape[1] // BLK
    total[...] = near[...]
    for r, part in enumerate(back, 1):
        there = origin(place[0], r, shard_count)

        @pl.when(there > place[0])
        def _():
            for s in range(CAP):
                block = asked[there, s]
                for kv in range(2):
                    total[kv, block] += part[kv, s].astype(jnp.float32)

    for r in range(heads):
        first = origin(place[1], r, heads) * per_quarter
        for kv in range(2):
            for j in range(per_quarter):
                outs[r][kv, j * BLK : (j + 1) * BLK, :] = total[kv, first + j].astype(jnp.bfloat16)


def whole(shape):
    return pl.BlockSpec(tuple(shape), lambda *_: (0,) * len(shape))


ANYWHERE = pl.BlockSpec(memory_space=pl.ANY)


def bf16(*shape):
    return jax.ShapeDtypeStruct(shape, jnp.bfloat16)


def call(kernel, scalars, arrays, out_shapes, scratch, name, any_in=False, any_out=False, limit=VMEM_LIMIT):
    return pl.pallas_call(
        kernel,
        grid_spec=pltpu.PrefetchScalarGridSpec(
            num_scalar_prefetch=len(scalars),
            grid=(1,),
            in_specs=[ANYWHERE if any_in else whole(x.shape) for x in arrays],
            out_specs=[ANYWHERE if any_out else whole(x.shape) for x in out_shapes],
            scratch_shapes=scratch,
        ),
        out_shape=out_shapes,
        compiler_params=params(limit),
        name=name,
    )(*scalars, *arrays)


def attend(place, source, asked, queries, out_grad, own, far, head, last, earlier, shard_count):
    tokens_here, width = queries.shape
    blocks_here = tokens_here // BLK
    slots = blocks_here + shard_count * CAP
    tile = pl.BlockSpec((STEP_BLOCKS * BLK, GROUP * HEAD_DIM), lambda i, *_: (i, head))
    near_shape = (2, blocks_here, BLK, HEAD_DIM)
    arrays = [*own, *far]
    first = 5 + len(arrays)
    out_shapes = [bf16(2, CAP, BLK, HEAD_DIM)] * (shard_count - 1)
    return pl.pallas_call(
        functools.partial(
            attend_kernel, heads=len(own), head=head, last=last, shard_count=shard_count
        ),
        grid_spec=pltpu.PrefetchScalarGridSpec(
            num_scalar_prefetch=3,
            grid=(blocks_here // STEP_BLOCKS,),
            in_specs=[tile, tile] + [whole(x.shape) for x in arrays] + [ANYWHERE] * len(earlier),
            out_specs=[tile, tile, whole(near_shape)] + [whole(x.shape) for x in out_shapes],
            scratch_shapes=[
                pltpu.VMEM((2, slots, BLK, HEAD_DIM), jnp.bfloat16),
                pltpu.VMEM((2, slots, BLK, HEAD_DIM), jnp.float32),
            ],
        ),
        out_shape=[bf16(tokens_here, width), bf16(tokens_here, width), jax.ShapeDtypeStruct(near_shape, jnp.float32)]
        + out_shapes,
        input_output_aliases={first: 0, first + 1: 1} if earlier else {},
        compiler_params=params(),
        cost_estimate=pl.CostEstimate(
            flops=12 * blocks_here * LIST * BLK * GROUP * BLK * HEAD_DIM,
            bytes_accessed=20 * 1024 * 1024,
            transcendentals=blocks_here * LIST * BLK * GROUP * BLK,
        ),
        name="attend",
    )(place, source, asked, queries, out_grad, *arrays, *earlier)


def send(x, axis, count, r):
    return lax.ppermute(x, axis, [(i, partner(i, r, count)) for i in range(count)])


def send_back(x, axis, count, r):
    return lax.ppermute(x, axis, [(i, origin(i, r, count)) for i in range(count)])


def requests_of(flat_ids, blocks_here, shard_index, shard_count):
    owner = flat_ids // blocks_here
    shards = jnp.arange(shard_count, dtype=jnp.int32)
    inner = jnp.arange(blocks_here, dtype=jnp.int32)
    every_block = jnp.arange(shard_count * blocks_here, dtype=jnp.int32)
    listed = jnp.any(flat_ids[:, None] == every_block[None, :], axis=0)
    grid = listed.reshape(shard_count, blocks_here) & (shards != shard_index)[:, None]
    rank = jnp.sum((grid[:, :, None] & (inner[:, None] < inner[None, :])[None]).astype(jnp.int32), axis=1)
    hit = grid[:, None] & (rank[:, None] == jnp.arange(128, dtype=jnp.int32)[None, :, None])
    requests = jnp.sum(jnp.where(hit, inner[None, None], 0), axis=2)
    same_owner = owner[:, None] == (every_block // blocks_here)[None, :]
    place_of = jnp.sum((same_owner & listed[None, :] & (every_block[None, :] < flat_ids[:, None])).astype(jnp.int32), axis=1)
    source = jnp.where(owner == shard_index, flat_ids % blocks_here, blocks_here + owner * CAP + place_of)
    return requests, source


def after(x, *others):
    return lax.optimization_barrier((x, *others))[0]


def per_device(queries, key_states, value_states, block_lists, out_grad):
    shard_index = lax.axis_index("ctx")
    shard_count = lax.axis_size("ctx")
    heads = lax.axis_size("head")
    blocks_here = queries.shape[0] // BLK
    quarter = key_states.shape[0]
    head_count = key_states.shape[1] // heads // HEAD_DIM
    place = jnp.stack([shard_index, lax.axis_index("head")]).astype(jnp.int32)

    pieces = call(
        split_kernel,
        [place],
        [key_states, value_states],
        [bf16(head_count, 2, quarter, HEAD_DIM)] * heads,
        [pltpu.SemaphoreType.DMA((2 * heads * head_count,))],
        "split",
        any_in=True,
        limit=VMEM_MOST,
    )
    own = [pieces[0]] + [send(pieces[r], "head", heads, r) for r in range(1, heads)]

    requests, source = requests_of(block_lists.reshape(-1), blocks_here, shard_index, shard_count)
    asked = lax.all_to_all(requests, "ctx", split_axis=0, concat_axis=0, tiled=True)

    def exchange(arrays):
        return [send(x, "ctx", shard_count, r) for r, x in enumerate(arrays, 1)]

    picked = call(
        functools.partial(pick_kernel, heads=heads, shard_count=shard_count),
        [place, asked],
        own,
        [bf16(2, CAP, BLK, HEAD_DIM)] * (shard_count - 1),
        [pltpu.VMEM((2, blocks_here, BLK, HEAD_DIM), jnp.bfloat16)],
        "pick",
    )
    come, earlier, nears, backs = exchange(picked), [], [], []
    for h in range(head_count):
        attended, query_grad, near, *go = attend(
            place, source, asked, queries, out_grad, own, come, h, h == head_count - 1, earlier, shard_count
        )
        earlier = [attended, query_grad]
        nears.append(near)
        come = exchange(go)
        backs.append(come)
    done = []
    for h in range(head_count):
        sums = call(
            functools.partial(gather_sum_kernel, heads=heads, shard_count=shard_count),
            [place, asked],
            [after(nears[h], nears[-1], *done[-1:]), *backs[h]],
            [bf16(2, quarter, HEAD_DIM)] * heads,
            [pltpu.VMEM((2, blocks_here, BLK, HEAD_DIM), jnp.float32)],
            "gather_sum",
        )
        done += [sums[0]] + [send_back(sums[r], "head", heads, r) for r in range(1, heads)]
    key_grad, value_grad = call(
        functools.partial(join_kernel, heads=heads),
        [place],
        done,
        [bf16(*key_states.shape)] * 2,
        [pltpu.SemaphoreType.DMA((2 * heads * head_count,))],
        "join",
        any_in=True,
        any_out=True,
    )
    return attended, query_grad, key_grad, value_grad


def solution(mesh):
    return jax.shard_map(
        per_device,
        mesh=mesh,
        in_specs=(
            P("ctx", "head"),
            P(("ctx", "head"), None),
            P(("ctx", "head"), None),
            P("ctx", None),
            P("ctx", "head"),
        ),
        out_specs=(
            P("ctx", "head"),
            P("ctx", "head"),
            P(("ctx", "head"), None),
            P(("ctx", "head"), None),
        ),
        check_vma=False,
    )
```

```python
import functools

import jax
import jax.numpy as jnp
from jax import lax
from jax.experimental import pallas as pl
from jax.experimental.pallas import tpu as pltpu
from jax.sharding import PartitionSpec as P

HEAD_DIM = 128
GROUP = 4
BLK = 64
LIST = 8
CAP = 3
STEP_BLOCKS = 4
TOGETHER = 2
NEG_FILL = -1e30
SCALE = HEAD_DIM ** (-0.5)
LOG2E = 1.4426950408889634
VMEM_LIMIT = 50 * 1024 * 1024
VMEM_MOST = 60 * 1024 * 1024

NT = (((1,), (1,)), ((), ()))
NN = (((1,), (0,)), ((), ()))
TN = (((0,), (0,)), ((), ()))


def dot(a, b, dims):
    return lax.dot_general(a, b, dims, preferred_element_type=jnp.float32)


def params(limit=VMEM_LIMIT):
    return pltpu.CompilerParams(vmem_limit_bytes=limit)


def partner(me, r, count):
    return me ^ r if count & (count - 1) == 0 else (me + r) % count


def origin(me, r, count):
    return me ^ r if count & (count - 1) == 0 else (me + count - r) % count


def steps_of(count):
    return [*range(count // 2, count), *range(1, count // 2)] if count > 1 else []


def head_columns(place, r, heads, h, head_count):
    col = (partner(place[1], r, heads) * head_count + h) * HEAD_DIM
    return pl.ds(pl.multiple_of(col, HEAD_DIM), HEAD_DIM)


def split_kernel(place, k_ref, v_ref, *refs):
    *outs, sem = refs
    heads, head_count = len(outs), outs[0].shape[0]
    copies = []
    for r, out in enumerate(outs):
        for h in range(head_count):
            cols = head_columns(place, r, heads, h, head_count)
            for kv, ref in enumerate((k_ref, v_ref)):
                at = (r * head_count + h) * 2 + kv
                copies.append(pltpu.make_async_copy(ref.at[:, cols], out.at[h, kv], sem.at[at]))
    for copy in copies:
        copy.start()
    for copy in copies:
        copy.wait()


def join_kernel(place, *refs, heads):
    *pieces, k_ref, v_ref, sem = refs
    head_count = len(pieces) // heads
    copies = []
    for at, piece in enumerate(pieces):
        cols = head_columns(place, at % heads, heads, at // heads, head_count)
        for kv, ref in enumerate((k_ref, v_ref)):
            copies.append(pltpu.make_async_copy(piece.at[kv], ref.at[:, cols], sem.at[2 * at + kv]))
    for copy in copies:
        copy.start()
    for copy in copies:
        copy.wait()


def fill_table(place, own, h, table):
    heads = len(own)
    per_quarter = own[0].shape[2] // BLK
    for r in range(heads):
        first = origin(place[1], r, heads) * per_quarter
        for kv in range(2):
            for j in range(per_quarter):
                table[kv, first + j] = own[r][h, kv, j * BLK : (j + 1) * BLK, :]


def pick(table, asked, there, out):
    for s in range(CAP):
        block = asked[there, s]
        for kv in range(2):
            out[kv, s] = table[kv, block]


def pick_kernel(place, asked, *refs, heads, shard_count):
    own, outs, table = refs[:heads], refs[heads:-1], refs[-1]
    fill_table(place, own, 0, table)
    for r, out in zip(steps_of(shard_count), outs):
        pick(table, asked, partner(place[0], r, shard_count), out)


def by_head(ref, b):
    rows = slice(b * BLK, (b + 1) * BLK)
    return jnp.concatenate([ref[rows, g * HEAD_DIM : (g + 1) * HEAD_DIM] for g in range(GROUP)], axis=0)


def by_row(ref, b, x):
    rows = slice(b * BLK, (b + 1) * BLK)
    for g in range(GROUP):
        ref[rows, g * HEAD_DIM : (g + 1) * HEAD_DIM] = x[g * BLK : (g + 1) * BLK]


def attend_kernel(place, source, asked, q_ref, g_ref, *refs, heads, head, last, shard_count):
    steps = shard_count - 1
    own, far = refs[:heads], refs[heads : heads + steps]
    table, total = refs[-2:]
    outs = refs[-2 - steps : -2]
    o_ref, dq_ref, near_out = refs[-5 - steps : -2 - steps]
    step = pl.program_id(0)
    blocks_here = near_out.shape[1]

    @pl.when(step == 0)
    def _():
        fill_table(place, own, head, table)
        for r, part in zip(steps_of(shard_count), far):
            first = blocks_here + origin(place[0], r, shard_count) * CAP
            for kv in range(2):
                for s in range(CAP):
                    table[kv, first + s] = part[kv, s]
        total[...] = jnp.zeros_like(total)

    key_row = lax.broadcasted_iota(jnp.int32, (BLK, GROUP * BLK), 0)
    query_col = lax.broadcasted_iota(jnp.int32, (BLK, GROUP * BLK), 1) % BLK
    hidden = key_row > query_col
    for first in range(0, STEP_BLOCKS, TOGETHER):
        subs = range(first, first + TOGETHER)
        listed = {b: [source[(step * STEP_BLOCKS + b) * LIST + e] for e in range(LIST)] for b in subs}
        q = {b: by_head(q_ref, b) for b in subs}
        g_out = {b: by_head(g_ref, b) for b in subs}
        keys = {b: jnp.concatenate([table[0, at] for at in listed[b]], axis=0) for b in subs}
        values = {b: jnp.concatenate([table[1, at] for at in listed[b]], axis=0) for b in subs}
        scores = {b: dot(keys[b], q[b], NT) for b in subs}
        dprob, probs, probs_low, dscore = {}, {}, {}, {}
        for b in subs:
            block = step * STEP_BLOCKS + b
            parts = []
            for e in range(LIST):
                mask = hidden if e == 0 else hidden & (listed[b][e] == block)
                parts.append(jnp.where(mask, NEG_FILL, scores[b][e * BLK : (e + 1) * BLK]))
            masked = jnp.concatenate(parts, axis=0)
            dprob[b] = dot(values[b], g_out[b], NT)
            peak = jnp.max(masked, axis=0, keepdims=True)
            expo = jnp.exp2((masked - peak) * (SCALE * LOG2E))
            probs[b] = expo * (1.0 / jnp.sum(expo, axis=0, keepdims=True))
            probs_low[b] = probs[b].astype(jnp.bfloat16)
        for b in subs:
            attended = dot(values[b], probs_low[b], TN).astype(jnp.bfloat16).T
            by_row(o_ref, b, attended)
            dv = dot(probs_low[b], g_out[b], NN)
            delta = jnp.sum(probs[b] * dprob[b], axis=0, keepdims=True)
            dscore[b] = (probs[b] * (dprob[b] - delta)).astype(jnp.bfloat16)
            for e in range(LIST):
                total[1, listed[b][e]] += dv[e * BLK : (e + 1) * BLK]
        for b in subs:
            dq = (dot(keys[b], dscore[b], TN) * SCALE).astype(jnp.bfloat16).T
            by_row(dq_ref, b, dq)
            dk = dot(dscore[b], q[b], NN)
            for e in range(LIST):
                total[0, listed[b][e]] += dk[e * BLK : (e + 1) * BLK]

    @pl.when(step == pl.num_programs(0) - 1)
    def _():
        for kv, factor in ((0, SCALE), (1, 1.0)):
            near_out[kv] = total[kv, :blocks_here] * factor
        if not last:
            fill_table(place, own, head + 1, table)
        for r, out in zip(steps_of(shard_count), outs):
            there = partner(place[0], r, shard_count)

            @pl.when(there < place[0])
            def _():
                for kv, factor in ((0, SCALE), (1, 1.0)):
                    for s in range(CAP):
                        out[kv, s] = (total[kv, blocks_here + there * CAP + s] * factor).astype(jnp.bfloat16)

            @pl.when(there > place[0])
            def _():
                if last:
                    out[...] = jnp.zeros_like(out)
                else:
                    pick(table, asked, there, out)


def gather_sum_kernel(place, asked, near, *refs, heads, shard_count):
    back, outs, total = refs[: -heads - 1], refs[-heads - 1 : -1], refs[-1]
    per_quarter = outs[0].shape[1] // BLK
    total[...] = near[...]
    for r, part in zip(steps_of(shard_count), back):
        there = origin(place[0], r, shard_count)

        @pl.when(there > place[0])
        def _():
            for s in range(CAP):
                block = asked[there, s]
                for kv in range(2):
                    total[kv, block] += part[kv, s].astype(jnp.float32)

    for r in range(heads):
        first = origin(place[1], r, heads) * per_quarter
        for kv in range(2):
            for j in range(per_quarter):
                outs[r][kv, j * BLK : (j + 1) * BLK, :] = total[kv, first + j].astype(jnp.bfloat16)


def whole(shape):
    return pl.BlockSpec(tuple(shape), lambda *_: (0,) * len(shape))


ANYWHERE = pl.BlockSpec(memory_space=pl.ANY)


def bf16(*shape):
    return jax.ShapeDtypeStruct(shape, jnp.bfloat16)


def call(kernel, scalars, arrays, out_shapes, scratch, name, any_in=False, any_out=False, limit=VMEM_LIMIT):
    return pl.pallas_call(
        kernel,
        grid_spec=pltpu.PrefetchScalarGridSpec(
            num_scalar_prefetch=len(scalars),
            grid=(1,),
            in_specs=[ANYWHERE if any_in else whole(x.shape) for x in arrays],
            out_specs=[ANYWHERE if any_out else whole(x.shape) for x in out_shapes],
            scratch_shapes=scratch,
        ),
        out_shape=out_shapes,
        compiler_params=params(limit),
        name=name,
    )(*scalars, *arrays)


def attend(place, source, asked, queries, out_grad, own, far, head, last, earlier, shard_count):
    tokens_here, width = queries.shape
    blocks_here = tokens_here // BLK
    slots = blocks_here + shard_count * CAP
    tile = pl.BlockSpec((STEP_BLOCKS * BLK, GROUP * HEAD_DIM), lambda i, *_: (i, head))
    near_shape = (2, blocks_here, BLK, HEAD_DIM)
    arrays = [*own, *far]
    first = 5 + len(arrays)
    out_shapes = [bf16(2, CAP, BLK, HEAD_DIM)] * (shard_count - 1)
    return pl.pallas_call(
        functools.partial(
            attend_kernel, heads=len(own), head=head, last=last, shard_count=shard_count
        ),
        grid_spec=pltpu.PrefetchScalarGridSpec(
            num_scalar_prefetch=3,
            grid=(blocks_here // STEP_BLOCKS,),
            in_specs=[tile, tile] + [whole(x.shape) for x in arrays] + [ANYWHERE] * len(earlier),
            out_specs=[tile, tile, whole(near_shape)] + [whole(x.shape) for x in out_shapes],
            scratch_shapes=[
                pltpu.VMEM((2, slots, BLK, HEAD_DIM), jnp.bfloat16),
                pltpu.VMEM((2, slots, BLK, HEAD_DIM), jnp.float32),
            ],
        ),
        out_shape=[bf16(tokens_here, width), bf16(tokens_here, width), jax.ShapeDtypeStruct(near_shape, jnp.float32)]
        + out_shapes,
        input_output_aliases={first: 0, first + 1: 1} if earlier else {},
        compiler_params=params(),
        cost_estimate=pl.CostEstimate(
            flops=12 * blocks_here * LIST * BLK * GROUP * BLK * HEAD_DIM,
            bytes_accessed=20 * 1024 * 1024,
            transcendentals=blocks_here * LIST * BLK * GROUP * BLK,
        ),
        name="attend",
    )(place, source, asked, queries, out_grad, *arrays, *earlier)


def send(x, axis, count, r):
    return lax.ppermute(x, axis, [(i, partner(i, r, count)) for i in range(count)])


def send_back(x, axis, count, r):
    return lax.ppermute(x, axis, [(i, origin(i, r, count)) for i in range(count)])


def requests_of(flat_ids, blocks_here, shard_index, shard_count):
    owner = flat_ids // blocks_here
    shards = jnp.arange(shard_count, dtype=jnp.int32)
    inner = jnp.arange(blocks_here, dtype=jnp.int32)
    every_block = jnp.arange(shard_count * blocks_here, dtype=jnp.int32)
    listed = jnp.any(flat_ids[:, None] == every_block[None, :], axis=0)
    grid = listed.reshape(shard_count, blocks_here) & (shards != shard_index)[:, None]
    rank = jnp.sum((grid[:, :, None] & (inner[:, None] < inner[None, :])[None]).astype(jnp.int32), axis=1)
    hit = grid[:, None] & (rank[:, None] == jnp.arange(128, dtype=jnp.int32)[None, :, None])
    requests = jnp.sum(jnp.where(hit, inner[None, None], 0), axis=2)
    same_owner = owner[:, None] == (every_block // blocks_here)[None, :]
    place_of = jnp.sum((same_owner & listed[None, :] & (every_block[None, :] < flat_ids[:, None])).astype(jnp.int32), axis=1)
    source = jnp.where(owner == shard_index, flat_ids % blocks_here, blocks_here + owner * CAP + place_of)
    return requests, source


def after(x, *others):
    return lax.optimization_barrier((x, *others))[0]


def per_device(queries, key_states, value_states, block_lists, out_grad):
    shard_index = lax.axis_index("ctx")
    shard_count = lax.axis_size("ctx")
    heads = lax.axis_size("head")
    blocks_here = queries.shape[0] // BLK
    quarter = key_states.shape[0]
    head_count = key_states.shape[1] // heads // HEAD_DIM
    place = jnp.stack([shard_index, lax.axis_index("head")]).astype(jnp.int32)

    pieces = call(
        split_kernel,
        [place],
        [key_states, value_states],
        [bf16(head_count, 2, quarter, HEAD_DIM)] * heads,
        [pltpu.SemaphoreType.DMA((2 * heads * head_count,))],
        "split",
        any_in=True,
        limit=VMEM_MOST,
    )
    own = [pieces[0]] + [send(pieces[r], "head", heads, r) for r in range(1, heads)]

    requests, source = requests_of(after(block_lists, pieces[0]).reshape(-1), blocks_here, shard_index, shard_count)
    asked = lax.all_to_all(requests, "ctx", split_axis=0, concat_axis=0, tiled=True)

    def exchange(arrays):
        return [send(x, "ctx", shard_count, r) for r, x in zip(steps_of(shard_count), arrays)]

    picked = call(
        functools.partial(pick_kernel, heads=heads, shard_count=shard_count),
        [place, asked],
        own,
        [bf16(2, CAP, BLK, HEAD_DIM)] * (shard_count - 1),
        [pltpu.VMEM((2, blocks_here, BLK, HEAD_DIM), jnp.bfloat16)],
        "pick",
    )
    come, earlier, nears, backs = exchange(picked), [], [], []
    for h in range(head_count):
        attended, query_grad, near, *go = attend(
            place, source, asked, queries, out_grad, own, come, h, h == head_count - 1, earlier, shard_count
        )
        earlier = [attended, query_grad]
        nears.append(near)
        come = exchange(go)
        backs.append(come)
    done = []
    for h in range(head_count):
        sums = call(
            functools.partial(gather_sum_kernel, heads=heads, shard_count=shard_count),
            [place, asked],
            [after(nears[h], nears[-1], *done[-1:]), *backs[h]],
            [bf16(2, quarter, HEAD_DIM)] * heads,
            [pltpu.VMEM((2, blocks_here, BLK, HEAD_DIM), jnp.float32)],
            "gather_sum",
        )
        done += [sums[0]] + [send_back(sums[r], "head", heads, r) for r in range(1, heads)]
    key_grad, value_grad = call(
        functools.partial(join_kernel, heads=heads),
        [place],
        done,
        [bf16(*key_states.shape)] * 2,
        [pltpu.SemaphoreType.DMA((2 * heads * head_count,))],
        "join",
        any_in=True,
        any_out=True,
    )
    return attended, query_grad, key_grad, value_grad


def solution(mesh):
    return jax.shard_map(
        per_device,
        mesh=mesh,
        in_specs=(
            P("ctx", "head"),
            P(("ctx", "head"), None),
            P(("ctx", "head"), None),
            P("ctx", None),
            P("ctx", "head"),
        ),
        out_specs=(
            P("ctx", "head"),
            P("ctx", "head"),
            P(("ctx", "head"), None),
            P(("ctx", "head"), None),
        ),
        check_vma=False,
    )
```

```python
import functools

import jax
import jax.numpy as jnp
from jax import lax
from jax.experimental import pallas as pl
from jax.experimental.pallas import tpu as pltpu
from jax.sharding import PartitionSpec as P

HEAD_DIM = 128
GROUP = 4
BLK = 64
LIST = 8
CAP = 3
STEP_BLOCKS = 4
TOGETHER = 4
NEG_FILL = -1e30
SCALE = HEAD_DIM ** (-0.5)
LOG2E = 1.4426950408889634
VMEM_LIMIT = 50 * 1024 * 1024
VMEM_MOST = 60 * 1024 * 1024

NT = (((1,), (1,)), ((), ()))
NN = (((1,), (0,)), ((), ()))
TN = (((0,), (0,)), ((), ()))


def dot(a, b, dims):
    return lax.dot_general(a, b, dims, preferred_element_type=jnp.float32)


def params(limit=VMEM_LIMIT):
    return pltpu.CompilerParams(vmem_limit_bytes=limit)


def partner(me, r, count):
    return me ^ r if count & (count - 1) == 0 else (me + r) % count


def origin(me, r, count):
    return me ^ r if count & (count - 1) == 0 else (me + count - r) % count


def steps_of(count):
    short = list(range(1, count // 2))
    return short[:2] + list(range(max(1, count // 2), count)) + short[2:]


def head_columns(place, r, heads, h, head_count):
    col = (partner(place[1], r, heads) * head_count + h) * HEAD_DIM
    return pl.ds(pl.multiple_of(col, HEAD_DIM), HEAD_DIM)


def split_kernel(place, k_ref, v_ref, *refs):
    *outs, sem = refs
    heads, head_count = len(outs), outs[0].shape[0]
    copies = []
    for r, out in enumerate(outs):
        for h in range(head_count):
            cols = head_columns(place, r, heads, h, head_count)
            for kv, ref in enumerate((k_ref, v_ref)):
                at = (r * head_count + h) * 2 + kv
                copies.append(pltpu.make_async_copy(ref.at[:, cols], out.at[h, kv], sem.at[at]))
    for copy in copies:
        copy.start()
    for copy in copies:
        copy.wait()


def join_kernel(place, *refs, heads):
    *pieces, k_ref, v_ref, sem = refs
    head_count = len(pieces) // heads
    copies = []
    for at, piece in enumerate(pieces):
        cols = head_columns(place, at % heads, heads, at // heads, head_count)
        for kv, ref in enumerate((k_ref, v_ref)):
            copies.append(pltpu.make_async_copy(piece.at[kv], ref.at[:, cols], sem.at[2 * at + kv]))
    for copy in copies:
        copy.start()
    for copy in copies:
        copy.wait()


def fill_table(place, own, h, table):
    heads = len(own)
    per_quarter = own[0].shape[2] // BLK
    for r in range(heads):
        first = origin(place[1], r, heads) * per_quarter
        for kv in range(2):
            for j in range(per_quarter):
                table[kv, first + j] = own[r][h, kv, j * BLK : (j + 1) * BLK, :]


def pick(table, asked, there, out):
    for s in range(CAP):
        block = asked[there, s]
        for kv in range(2):
            out[kv, s] = table[kv, block]


def pick_kernel(place, asked, *refs, heads, shard_count):
    own, outs, table = refs[:heads], refs[heads:-1], refs[-1]
    fill_table(place, own, 0, table)
    for r, out in zip(steps_of(shard_count), outs):
        pick(table, asked, partner(place[0], r, shard_count), out)


def by_head(ref, b):
    rows = slice(b * BLK, (b + 1) * BLK)
    return jnp.concatenate([ref[rows, g * HEAD_DIM : (g + 1) * HEAD_DIM] for g in range(GROUP)], axis=0)


def by_row(ref, b, x):
    rows = slice(b * BLK, (b + 1) * BLK)
    for g in range(GROUP):
        ref[rows, g * HEAD_DIM : (g + 1) * HEAD_DIM] = x[g * BLK : (g + 1) * BLK]


def attend_kernel(place, source, asked, q_ref, g_ref, *refs, heads, head, last, shard_count):
    steps = shard_count - 1
    own, far = refs[:heads], refs[heads : heads + steps]
    table, total = refs[-2:]
    outs = refs[-2 - steps : -2]
    o_ref, dq_ref, near_out = refs[-5 - steps : -2 - steps]
    step = pl.program_id(0)
    blocks_here = near_out.shape[1]

    @pl.when(step == 0)
    def _():
        fill_table(place, own, 0, table)
        for r, part in zip(steps_of(shard_count), far):
            first = blocks_here + origin(place[0], r, shard_count) * CAP
            for kv in range(2):
                for s in range(CAP):
                    table[kv, first + s] = part[kv, s]
        total[...] = jnp.zeros_like(total)

    key_row = lax.broadcasted_iota(jnp.int32, (BLK, GROUP * BLK), 0)
    query_col = lax.broadcasted_iota(jnp.int32, (BLK, GROUP * BLK), 1) % BLK
    hidden = key_row > query_col
    for first in range(0, STEP_BLOCKS, TOGETHER):
        subs = range(first, first + TOGETHER)
        listed = {b: [source[(step * STEP_BLOCKS + b) * LIST + e] for e in range(LIST)] for b in subs}
        q = {b: by_head(q_ref, b) for b in subs}
        g_out = {b: by_head(g_ref, b) for b in subs}
        keys = {b: jnp.concatenate([table[0, at] for at in listed[b]], axis=0) for b in subs}
        values = {b: jnp.concatenate([table[1, at] for at in listed[b]], axis=0) for b in subs}
        scores = {b: dot(keys[b], q[b], NT) for b in subs}
        dprob, probs, probs_low, dscore = {}, {}, {}, {}
        for b in subs:
            block = step * STEP_BLOCKS + b
            parts = []
            for e in range(LIST):
                mask = hidden if e == 0 else hidden & (listed[b][e] == block)
                parts.append(jnp.where(mask, NEG_FILL, scores[b][e * BLK : (e + 1) * BLK]))
            masked = jnp.concatenate(parts, axis=0)
            dprob[b] = dot(values[b], g_out[b], NT)
            peak = jnp.max(masked, axis=0, keepdims=True)
            expo = jnp.exp2((masked - peak) * (SCALE * LOG2E))
            probs[b] = expo * (1.0 / jnp.sum(expo, axis=0, keepdims=True))
            probs_low[b] = probs[b].astype(jnp.bfloat16)
        for b in subs:
            attended = dot(values[b], probs_low[b], TN).astype(jnp.bfloat16).T
            by_row(o_ref, b, attended)
            dv = dot(probs_low[b], g_out[b], NN)
            delta = jnp.sum(probs[b] * dprob[b], axis=0, keepdims=True)
            dscore[b] = (probs[b] * (dprob[b] - delta)).astype(jnp.bfloat16)
            for e in range(LIST):
                total[1, listed[b][e]] += dv[e * BLK : (e + 1) * BLK]
        for b in subs:
            dq = (dot(keys[b], dscore[b], TN) * SCALE).astype(jnp.bfloat16).T
            by_row(dq_ref, b, dq)
            dk = dot(dscore[b], q[b], NN)
            for e in range(LIST):
                total[0, listed[b][e]] += dk[e * BLK : (e + 1) * BLK]

    @pl.when(step == pl.num_programs(0) - 1)
    def _():
        for kv, factor in ((0, SCALE), (1, 1.0)):
            near_out[kv] = total[kv, :blocks_here] * factor
        if not last:
            fill_table(place, own, 1, table)
        for r, out in zip(steps_of(shard_count), outs):
            there = partner(place[0], r, shard_count)

            @pl.when(there < place[0])
            def _():
                for kv, factor in ((0, SCALE), (1, 1.0)):
                    for s in range(CAP):
                        out[kv, s] = (total[kv, blocks_here + there * CAP + s] * factor).astype(jnp.bfloat16)

            @pl.when(there > place[0])
            def _():
                if last:
                    out[...] = jnp.zeros_like(out)
                else:
                    pick(table, asked, there, out)


def gather_sum_kernel(place, asked, near, *refs, heads, shard_count):
    back, outs, total = refs[: -heads - 1], refs[-heads - 1 : -1], refs[-1]
    per_quarter = outs[0].shape[1] // BLK
    total[...] = near[...]
    for r, part in zip(steps_of(shard_count), back):
        there = origin(place[0], r, shard_count)

        @pl.when(there > place[0])
        def _():
            for s in range(CAP):
                block = asked[there, s]
                for kv in range(2):
                    total[kv, block] += part[kv, s].astype(jnp.float32)

    for r in range(heads):
        first = origin(place[1], r, heads) * per_quarter
        for kv in range(2):
            for j in range(per_quarter):
                outs[r][kv, j * BLK : (j + 1) * BLK, :] = total[kv, first + j].astype(jnp.bfloat16)


def whole(shape):
    return pl.BlockSpec(tuple(shape), lambda *_: (0,) * len(shape))


def heads_from(shape, head, count):
    return pl.BlockSpec((pl.Element(count), *(pl.Element(n) for n in shape[1:])), lambda *_: (head, *(0,) * (len(shape) - 1)))


ANYWHERE = pl.BlockSpec(memory_space=pl.ANY)


def bf16(*shape):
    return jax.ShapeDtypeStruct(shape, jnp.bfloat16)


def call(kernel, scalars, arrays, out_shapes, scratch, name, any_in=False, any_out=False, limit=VMEM_LIMIT):
    return pl.pallas_call(
        kernel,
        grid_spec=pltpu.PrefetchScalarGridSpec(
            num_scalar_prefetch=len(scalars),
            grid=(1,),
            in_specs=[ANYWHERE if any_in else whole(x.shape) for x in arrays],
            out_specs=[ANYWHERE if any_out else whole(x.shape) for x in out_shapes],
            scratch_shapes=scratch,
        ),
        out_shape=out_shapes,
        compiler_params=params(limit),
        name=name,
    )(*scalars, *arrays)


def attend(place, source, asked, queries, out_grad, own, far, head, last, earlier, shard_count):
    tokens_here, width = queries.shape
    blocks_here = tokens_here // BLK
    slots = blocks_here + shard_count * CAP
    tile = pl.BlockSpec((STEP_BLOCKS * BLK, GROUP * HEAD_DIM), lambda i, *_: (i, head))
    near_shape = (2, blocks_here, BLK, HEAD_DIM)
    arrays = [*own, *far]
    first = 5 + len(arrays)
    out_shapes = [bf16(2, CAP, BLK, HEAD_DIM)] * (shard_count - 1)
    return pl.pallas_call(
        functools.partial(
            attend_kernel, heads=len(own), head=head, last=last, shard_count=shard_count
        ),
        grid_spec=pltpu.PrefetchScalarGridSpec(
            num_scalar_prefetch=3,
            grid=(blocks_here // STEP_BLOCKS,),
            in_specs=[tile, tile]
            + [heads_from(x.shape, head, 1 if last else 2) for x in own]
            + [whole(x.shape) for x in far]
            + [ANYWHERE] * len(earlier),
            out_specs=[tile, tile, whole(near_shape)] + [whole(x.shape) for x in out_shapes],
            scratch_shapes=[
                pltpu.VMEM((2, slots, BLK, HEAD_DIM), jnp.bfloat16),
                pltpu.VMEM((2, slots, BLK, HEAD_DIM), jnp.float32),
            ],
        ),
        out_shape=[bf16(tokens_here, width), bf16(tokens_here, width), jax.ShapeDtypeStruct(near_shape, jnp.float32)]
        + out_shapes,
        input_output_aliases={first: 0, first + 1: 1} if earlier else {},
        compiler_params=params(),
        cost_estimate=pl.CostEstimate(
            flops=12 * blocks_here * LIST * BLK * GROUP * BLK * HEAD_DIM,
            bytes_accessed=20 * 1024 * 1024,
            transcendentals=blocks_here * LIST * BLK * GROUP * BLK,
        ),
        name="attend",
    )(place, source, asked, queries, out_grad, *arrays, *earlier)


def send(x, axis, count, r):
    return lax.ppermute(x, axis, [(i, partner(i, r, count)) for i in range(count)])


def send_back(x, axis, count, r):
    return lax.ppermute(x, axis, [(i, origin(i, r, count)) for i in range(count)])


def requests_of(flat_ids, blocks_here, shard_index, shard_count):
    owner = flat_ids // blocks_here
    shards = jnp.arange(shard_count, dtype=jnp.int32)
    inner = jnp.arange(blocks_here, dtype=jnp.int32)
    every_block = jnp.arange(shard_count * blocks_here, dtype=jnp.int32)
    listed = jnp.any(flat_ids[:, None] == every_block[None, :], axis=0)
    grid = listed.reshape(shard_count, blocks_here) & (shards != shard_index)[:, None]
    rank = jnp.sum((grid[:, :, None] & (inner[:, None] < inner[None, :])[None]).astype(jnp.int32), axis=1)
    hit = grid[:, None] & (rank[:, None] == jnp.arange(128, dtype=jnp.int32)[None, :, None])
    requests = jnp.sum(jnp.where(hit, inner[None, None], 0), axis=2)
    same_owner = owner[:, None] == (every_block // blocks_here)[None, :]
    place_of = jnp.sum((same_owner & listed[None, :] & (every_block[None, :] < flat_ids[:, None])).astype(jnp.int32), axis=1)
    source = jnp.where(owner == shard_index, flat_ids % blocks_here, blocks_here + owner * CAP + place_of)
    return requests, source


def after(x, *others):
    return lax.optimization_barrier((x, *others))[0]


def per_device(queries, key_states, value_states, block_lists, out_grad):
    shard_index = lax.axis_index("ctx")
    shard_count = lax.axis_size("ctx")
    heads = lax.axis_size("head")
    blocks_here = queries.shape[0] // BLK
    quarter = key_states.shape[0]
    head_count = key_states.shape[1] // heads // HEAD_DIM
    place = jnp.stack([shard_index, lax.axis_index("head")]).astype(jnp.int32)

    pieces = call(
        split_kernel,
        [place],
        [key_states, value_states],
        [bf16(head_count, 2, quarter, HEAD_DIM)] * heads,
        [pltpu.SemaphoreType.DMA((2 * heads * head_count,))],
        "split",
        any_in=True,
        limit=VMEM_MOST,
    )
    own = [pieces[0]] + [send(pieces[r], "head", heads, r) for r in range(1, heads)]

    requests, source = requests_of(after(block_lists, *own[1:2]).reshape(-1), blocks_here, shard_index, shard_count)
    asked = lax.all_to_all(requests, "ctx", split_axis=0, concat_axis=0, tiled=True)

    def exchange(arrays):
        return [send(x, "ctx", shard_count, r) for r, x in zip(steps_of(shard_count), arrays)]

    picked = call(
        functools.partial(pick_kernel, heads=heads, shard_count=shard_count),
        [place, asked],
        own,
        [bf16(2, CAP, BLK, HEAD_DIM)] * (shard_count - 1),
        [pltpu.VMEM((2, blocks_here, BLK, HEAD_DIM), jnp.bfloat16)],
        "pick",
    )
    come, earlier, nears, backs = exchange(picked), [], [], []
    for h in range(head_count):
        attended, query_grad, near, *go = attend(
            place, source, asked, queries, out_grad, own, come, h, h == head_count - 1, earlier, shard_count
        )
        earlier = [attended, query_grad]
        nears.append(near)
        come = exchange(go)
        backs.append(come)
    done = []
    for h in range(head_count):
        sums = call(
            functools.partial(gather_sum_kernel, heads=heads, shard_count=shard_count),
            [place, asked],
            [after(nears[h], nears[-1], *done[-1:]), *backs[h]],
            [bf16(2, quarter, HEAD_DIM)] * heads,
            [pltpu.VMEM((2, blocks_here, BLK, HEAD_DIM), jnp.float32)],
            "gather_sum",
        )
        done += [sums[0]] + [send_back(sums[r], "head", heads, r) for r in range(1, heads)]
    key_grad, value_grad = call(
        functools.partial(join_kernel, heads=heads),
        [place],
        done,
        [bf16(*key_states.shape)] * 2,
        [pltpu.SemaphoreType.DMA((2 * heads * head_count,))],
        "join",
        any_in=True,
        any_out=True,
    )
    return attended, query_grad, key_grad, value_grad


def solution(mesh):
    return jax.shard_map(
        per_device,
        mesh=mesh,
        in_specs=(
            P("ctx", "head"),
            P(("ctx", "head"), None),
            P(("ctx", "head"), None),
            P("ctx", None),
            P("ctx", "head"),
        ),
        out_specs=(
            P("ctx", "head"),
            P("ctx", "head"),
            P(("ctx", "head"), None),
            P(("ctx", "head"), None),
        ),
        check_vma=False,
    )
```

```python
import functools

import jax
import jax.numpy as jnp
from jax import lax
from jax.experimental import pallas as pl
from jax.experimental.pallas import tpu as pltpu
from jax.sharding import PartitionSpec as P

HEAD_DIM = 128
GROUP = 4
BLK = 64
LIST = 8
CAP = 3
STEP_BLOCKS = 4
TOGETHER = 4
NEG_FILL = -1e30
SCALE = HEAD_DIM ** (-0.5)
LOG2E = 1.4426950408889634
VMEM_LIMIT = 50 * 1024 * 1024
VMEM_MOST = 60 * 1024 * 1024

NT = (((1,), (1,)), ((), ()))
NN = (((1,), (0,)), ((), ()))
TN = (((0,), (0,)), ((), ()))


def dot(a, b, dims):
    return lax.dot_general(a, b, dims, preferred_element_type=jnp.float32)


def params(limit=VMEM_LIMIT):
    return pltpu.CompilerParams(vmem_limit_bytes=limit)


def partner(me, r, count):
    return me ^ r if count & (count - 1) == 0 else (me + r) % count


def origin(me, r, count):
    return me ^ r if count & (count - 1) == 0 else (me + count - r) % count


def steps_of(count):
    short = list(range(1, count // 2))
    return short[:2] + list(range(max(1, count // 2), count)) + short[2:]


def head_columns(place, r, heads, h, head_count):
    col = (partner(place[1], r, heads) * head_count + h) * HEAD_DIM
    return pl.ds(pl.multiple_of(col, HEAD_DIM), HEAD_DIM)


def split_kernel(place, k_ref, v_ref, *refs):
    *outs, sem = refs
    heads, head_count = len(outs), outs[0].shape[0]
    copies = []
    for r, out in enumerate(outs):
        for h in range(head_count):
            cols = head_columns(place, r, heads, h, head_count)
            for kv, ref in enumerate((k_ref, v_ref)):
                at = (r * head_count + h) * 2 + kv
                copies.append(pltpu.make_async_copy(ref.at[:, cols], out.at[h, kv], sem.at[at]))
    for copy in copies:
        copy.start()
    for copy in copies:
        copy.wait()


def join_kernel(place, *refs, heads):
    *pieces, k_ref, v_ref, sem = refs
    head_count = len(pieces) // heads
    copies = []
    for at, piece in enumerate(pieces):
        cols = head_columns(place, at % heads, heads, at // heads, head_count)
        for kv, ref in enumerate((k_ref, v_ref)):
            copies.append(pltpu.make_async_copy(piece.at[kv], ref.at[:, cols], sem.at[2 * at + kv]))
    for copy in copies:
        copy.start()
    for copy in copies:
        copy.wait()


def fill_table(place, own, h, table):
    heads = len(own)
    per_quarter = own[0].shape[2] // BLK
    for r in range(heads):
        first = origin(place[1], r, heads) * per_quarter
        for kv in range(2):
            for j in range(per_quarter):
                table[kv, first + j] = own[r][h, kv, j * BLK : (j + 1) * BLK, :]


def pick(table, asked, there, out):
    for s in range(CAP):
        block = asked[there, s]
        for kv in range(2):
            out[kv, s] = table[kv, block]


def pick_kernel(place, asked, *refs, heads, steps, head, shard_count):
    own, outs, table = refs[:heads], refs[heads:-1], refs[-1]
    fill_table(place, own, head, table)
    for r, out in zip(steps, outs):
        pick(table, asked, partner(place[0], r, shard_count), out)


def by_head(ref, b):
    rows = slice(b * BLK, (b + 1) * BLK)
    return jnp.concatenate([ref[rows, g * HEAD_DIM : (g + 1) * HEAD_DIM] for g in range(GROUP)], axis=0)


def by_row(ref, b, x):
    rows = slice(b * BLK, (b + 1) * BLK)
    for g in range(GROUP):
        ref[rows, g * HEAD_DIM : (g + 1) * HEAD_DIM] = x[g * BLK : (g + 1) * BLK]


def attend_kernel(place, source, asked, q_ref, g_ref, *refs, heads, head, last, shard_count):
    steps = shard_count - 1
    own, far = refs[:heads], refs[heads : heads + steps]
    table, total = refs[-2:]
    outs = refs[-2 - steps : -2]
    o_ref, dq_ref, near_out = refs[-5 - steps : -2 - steps]
    step = pl.program_id(0)
    blocks_here = near_out.shape[1]

    @pl.when(step == 0)
    def _():
        fill_table(place, own, 0, table)
        for r, part in zip(steps_of(shard_count), far):
            first = blocks_here + origin(place[0], r, shard_count) * CAP
            for kv in range(2):
                for s in range(CAP):
                    table[kv, first + s] = part[kv, s]
        total[...] = jnp.zeros_like(total)

    key_row = lax.broadcasted_iota(jnp.int32, (BLK, GROUP * BLK), 0)
    query_col = lax.broadcasted_iota(jnp.int32, (BLK, GROUP * BLK), 1) % BLK
    hidden = key_row > query_col
    for first in range(0, STEP_BLOCKS, TOGETHER):
        subs = range(first, first + TOGETHER)
        listed = {b: [source[(step * STEP_BLOCKS + b) * LIST + e] for e in range(LIST)] for b in subs}
        q = {b: by_head(q_ref, b) for b in subs}
        g_out = {b: by_head(g_ref, b) for b in subs}
        keys = {b: jnp.concatenate([table[0, at] for at in listed[b]], axis=0) for b in subs}
        values = {b: jnp.concatenate([table[1, at] for at in listed[b]], axis=0) for b in subs}
        scores = {b: dot(keys[b], q[b], NT) for b in subs}
        dprob, probs, probs_low, dscore = {}, {}, {}, {}
        for b in subs:
            block = step * STEP_BLOCKS + b
            parts = []
            for e in range(LIST):
                mask = hidden if e == 0 else hidden & (listed[b][e] == block)
                parts.append(jnp.where(mask, NEG_FILL, scores[b][e * BLK : (e + 1) * BLK]))
            masked = jnp.concatenate(parts, axis=0)
            dprob[b] = dot(values[b], g_out[b], NT)
            peak = jnp.max(masked, axis=0, keepdims=True)
            expo = jnp.exp2((masked - peak) * (SCALE * LOG2E))
            probs[b] = expo * (1.0 / jnp.sum(expo, axis=0, keepdims=True))
            probs_low[b] = probs[b].astype(jnp.bfloat16)
        for b in subs:
            attended = dot(values[b], probs_low[b], TN).astype(jnp.bfloat16).T
            by_row(o_ref, b, attended)
            dv = dot(probs_low[b], g_out[b], NN)
            delta = jnp.sum(probs[b] * dprob[b], axis=0, keepdims=True)
            dscore[b] = (probs[b] * (dprob[b] - delta)).astype(jnp.bfloat16)
            for e in range(LIST):
                total[1, listed[b][e]] += dv[e * BLK : (e + 1) * BLK]
        for b in subs:
            dq = (dot(keys[b], dscore[b], TN) * SCALE).astype(jnp.bfloat16).T
            by_row(dq_ref, b, dq)
            dk = dot(dscore[b], q[b], NN)
            for e in range(LIST):
                total[0, listed[b][e]] += dk[e * BLK : (e + 1) * BLK]

    @pl.when(step == pl.num_programs(0) - 1)
    def _():
        for kv, factor in ((0, SCALE), (1, 1.0)):
            near_out[kv] = total[kv, :blocks_here] * factor
        if not last:
            fill_table(place, own, 1, table)
        for r, out in zip(steps_of(shard_count), outs):
            there = partner(place[0], r, shard_count)

            @pl.when(there < place[0])
            def _():
                for kv, factor in ((0, SCALE), (1, 1.0)):
                    for s in range(CAP):
                        out[kv, s] = (total[kv, blocks_here + there * CAP + s] * factor).astype(jnp.bfloat16)

            @pl.when(there > place[0])
            def _():
                if last or r >= shard_count // 2:
                    out[...] = jnp.zeros_like(out)
                else:
                    pick(table, asked, there, out)


def gather_sum_kernel(place, asked, near, *refs, heads, shard_count):
    back, outs, total = refs[: -heads - 1], refs[-heads - 1 : -1], refs[-1]
    per_quarter = outs[0].shape[1] // BLK
    total[...] = near[...]
    for r, part in zip(steps_of(shard_count), back):
        there = origin(place[0], r, shard_count)

        @pl.when(there > place[0])
        def _():
            for s in range(CAP):
                block = asked[there, s]
                for kv in range(2):
                    total[kv, block] += part[kv, s].astype(jnp.float32)

    for r in range(heads):
        first = origin(place[1], r, heads) * per_quarter
        for kv in range(2):
            for j in range(per_quarter):
                outs[r][kv, j * BLK : (j + 1) * BLK, :] = total[kv, first + j].astype(jnp.bfloat16)


def whole(shape):
    return pl.BlockSpec(tuple(shape), lambda *_: (0,) * len(shape))


def heads_from(shape, head, count):
    return pl.BlockSpec((pl.Element(count), *(pl.Element(n) for n in shape[1:])), lambda *_: (head, *(0,) * (len(shape) - 1)))


ANYWHERE = pl.BlockSpec(memory_space=pl.ANY)


def bf16(*shape):
    return jax.ShapeDtypeStruct(shape, jnp.bfloat16)


def call(kernel, scalars, arrays, out_shapes, scratch, name, any_in=False, any_out=False, limit=VMEM_LIMIT):
    return pl.pallas_call(
        kernel,
        grid_spec=pltpu.PrefetchScalarGridSpec(
            num_scalar_prefetch=len(scalars),
            grid=(1,),
            in_specs=[ANYWHERE if any_in else whole(x.shape) for x in arrays],
            out_specs=[ANYWHERE if any_out else whole(x.shape) for x in out_shapes],
            scratch_shapes=scratch,
        ),
        out_shape=out_shapes,
        compiler_params=params(limit),
        name=name,
    )(*scalars, *arrays)


def attend(place, source, asked, queries, out_grad, own, far, head, last, earlier, shard_count):
    tokens_here, width = queries.shape
    blocks_here = tokens_here // BLK
    slots = blocks_here + shard_count * CAP
    tile = pl.BlockSpec((STEP_BLOCKS * BLK, GROUP * HEAD_DIM), lambda i, *_: (i, head))
    near_shape = (2, blocks_here, BLK, HEAD_DIM)
    arrays = [*own, *far]
    first = 5 + len(arrays)
    out_shapes = [bf16(2, CAP, BLK, HEAD_DIM)] * (shard_count - 1)
    return pl.pallas_call(
        functools.partial(
            attend_kernel, heads=len(own), head=head, last=last, shard_count=shard_count
        ),
        grid_spec=pltpu.PrefetchScalarGridSpec(
            num_scalar_prefetch=3,
            grid=(blocks_here // STEP_BLOCKS,),
            in_specs=[tile, tile]
            + [heads_from(x.shape, head, 1 if last else 2) for x in own]
            + [whole(x.shape) for x in far]
            + [ANYWHERE] * len(earlier),
            out_specs=[tile, tile, whole(near_shape)] + [whole(x.shape) for x in out_shapes],
            scratch_shapes=[
                pltpu.VMEM((2, slots, BLK, HEAD_DIM), jnp.bfloat16),
                pltpu.VMEM((2, slots, BLK, HEAD_DIM), jnp.float32),
            ],
        ),
        out_shape=[bf16(tokens_here, width), bf16(tokens_here, width), jax.ShapeDtypeStruct(near_shape, jnp.float32)]
        + out_shapes,
        input_output_aliases={first: 0, first + 1: 1} if earlier else {},
        compiler_params=params(),
        cost_estimate=pl.CostEstimate(
            flops=12 * blocks_here * LIST * BLK * GROUP * BLK * HEAD_DIM,
            bytes_accessed=20 * 1024 * 1024,
            transcendentals=blocks_here * LIST * BLK * GROUP * BLK,
        ),
        name="attend",
    )(place, source, asked, queries, out_grad, *arrays, *earlier)


def send(x, axis, count, r):
    return lax.ppermute(x, axis, [(i, partner(i, r, count)) for i in range(count)])


def send_back(x, axis, count, r):
    return lax.ppermute(x, axis, [(i, origin(i, r, count)) for i in range(count)])


def requests_of(flat_ids, blocks_here, shard_index, shard_count):
    owner = flat_ids // blocks_here
    shards = jnp.arange(shard_count, dtype=jnp.int32)
    inner = jnp.arange(blocks_here, dtype=jnp.int32)
    every_block = jnp.arange(shard_count * blocks_here, dtype=jnp.int32)
    listed = jnp.any(flat_ids[:, None] == every_block[None, :], axis=0)
    grid = listed.reshape(shard_count, blocks_here) & (shards != shard_index)[:, None]
    rank = jnp.sum((grid[:, :, None] & (inner[:, None] < inner[None, :])[None]).astype(jnp.int32), axis=1)
    hit = grid[:, None] & (rank[:, None] == jnp.arange(128, dtype=jnp.int32)[None, :, None])
    requests = jnp.sum(jnp.where(hit, inner[None, None], 0), axis=2)
    same_owner = owner[:, None] == (every_block // blocks_here)[None, :]
    place_of = jnp.sum((same_owner & listed[None, :] & (every_block[None, :] < flat_ids[:, None])).astype(jnp.int32), axis=1)
    source = jnp.where(owner == shard_index, flat_ids % blocks_here, blocks_here + owner * CAP + place_of)
    return requests, source


def after(x, *others):
    return lax.optimization_barrier((x, *others))[0]


def per_device(queries, key_states, value_states, block_lists, out_grad):
    shard_index = lax.axis_index("ctx")
    shard_count = lax.axis_size("ctx")
    heads = lax.axis_size("head")
    blocks_here = queries.shape[0] // BLK
    quarter = key_states.shape[0]
    head_count = key_states.shape[1] // heads // HEAD_DIM
    place = jnp.stack([shard_index, lax.axis_index("head")]).astype(jnp.int32)

    pieces = call(
        split_kernel,
        [place],
        [key_states, value_states],
        [bf16(head_count, 2, quarter, HEAD_DIM)] * heads,
        [pltpu.SemaphoreType.DMA((2 * heads * head_count,))],
        "split",
        any_in=True,
        limit=VMEM_MOST,
    )
    own = [pieces[0]] + [send(pieces[r], "head", heads, r) for r in range(1, heads)]

    requests, source = requests_of(after(block_lists, *own[1:2]).reshape(-1), blocks_here, shard_index, shard_count)
    asked = lax.all_to_all(requests, "ctx", split_axis=0, concat_axis=0, tiled=True)

    steps = steps_of(shard_count)
    wide = [r for r in steps if r >= shard_count // 2]

    def exchange(arrays):
        return {r: send(x, "ctx", shard_count, r) for r, x in arrays}

    def picked(head, steps):
        arrays = call(
            functools.partial(pick_kernel, heads=heads, steps=steps, head=head, shard_count=shard_count),
            [place, asked],
            own,
            [bf16(2, CAP, BLK, HEAD_DIM)] * len(steps),
            [pltpu.VMEM((2, blocks_here, BLK, HEAD_DIM), jnp.bfloat16)],
            "pick",
        )
        return list(zip(steps, arrays))

    come, earlier, nears, backs = exchange(picked(0, steps)), [], [], []
    for h in range(head_count):
        last = h == head_count - 1
        ahead = {}
        if not last:
            ahead = exchange([(r, after(x, *come.values())) for r, x in picked(h + 1, wide)])
        attended, query_grad, near, *go = attend(
            place, source, asked, queries, out_grad, own, [come[r] for r in steps], h, last, earlier, shard_count
        )
        earlier = [attended, query_grad]
        nears.append(near)
        back = exchange(zip(steps, go))
        backs.append([back[r] for r in steps])
        come = {**back, **ahead}
    done = []
    for h in range(head_count):
        sums = call(
            functools.partial(gather_sum_kernel, heads=heads, shard_count=shard_count),
            [place, asked],
            [after(nears[h], nears[-1], *done[-1:]), *backs[h]],
            [bf16(2, quarter, HEAD_DIM)] * heads,
            [pltpu.VMEM((2, blocks_here, BLK, HEAD_DIM), jnp.float32)],
            "gather_sum",
        )
        done += [sums[0]] + [send_back(sums[r], "head", heads, r) for r in range(1, heads)]
    key_grad, value_grad = call(
        functools.partial(join_kernel, heads=heads),
        [place],
        done,
        [bf16(*key_states.shape)] * 2,
        [pltpu.SemaphoreType.DMA((2 * heads * head_count,))],
        "join",
        any_in=True,
        any_out=True,
    )
    return attended, query_grad, key_grad, value_grad


def solution(mesh):
    return jax.shard_map(
        per_device,
        mesh=mesh,
        in_specs=(
            P("ctx", "head"),
            P(("ctx", "head"), None),
            P(("ctx", "head"), None),
            P("ctx", None),
            P("ctx", "head"),
        ),
        out_specs=(
            P("ctx", "head"),
            P("ctx", "head"),
            P(("ctx", "head"), None),
            P(("ctx", "head"), None),
        ),
        check_vma=False,
    )
```

```python
import functools

import jax
import jax.numpy as jnp
from jax import lax
from jax.experimental import pallas as pl
from jax.experimental.pallas import tpu as pltpu
from jax.sharding import PartitionSpec as P

HEAD_DIM = 128
GROUP = 4
BLK = 64
LIST = 8
CAP = 3
STEP_BLOCKS = 4
TOGETHER = 4
NEG_FILL = -1e30
SCALE = HEAD_DIM ** (-0.5)
LOG2E = 1.4426950408889634
VMEM_LIMIT = 50 * 1024 * 1024
VMEM_MOST = 60 * 1024 * 1024

NT = (((1,), (1,)), ((), ()))
NN = (((1,), (0,)), ((), ()))
TN = (((0,), (0,)), ((), ()))


def dot(a, b, dims):
    return lax.dot_general(a, b, dims, preferred_element_type=jnp.float32)


def params(limit=VMEM_LIMIT):
    return pltpu.CompilerParams(vmem_limit_bytes=limit)


def partner(me, r, count):
    return me ^ r if count & (count - 1) == 0 else (me + r) % count


def origin(me, r, count):
    return me ^ r if count & (count - 1) == 0 else (me + count - r) % count


def steps_of(count):
    short = list(range(1, count // 2))
    return short[:2] + list(range(max(1, count // 2), count)) + short[2:]


def near_steps(count):
    return range(1, count // 2)


def head_columns(place, r, heads, h, head_count):
    col = (partner(place[1], r, heads) * head_count + h) * HEAD_DIM
    return pl.ds(pl.multiple_of(col, HEAD_DIM), HEAD_DIM)


def split_kernel(place, k_ref, v_ref, *refs):
    *outs, sem = refs
    heads, head_count = len(outs), outs[0].shape[0]
    copies = []
    for r, out in enumerate(outs):
        for h in range(head_count):
            cols = head_columns(place, r, heads, h, head_count)
            for kv, ref in enumerate((k_ref, v_ref)):
                at = (r * head_count + h) * 2 + kv
                copies.append(pltpu.make_async_copy(ref.at[:, cols], out.at[h, kv], sem.at[at]))
    for copy in copies:
        copy.start()
    for copy in copies:
        copy.wait()


def join_kernel(place, *refs, heads):
    *pieces, k_ref, v_ref, sem = refs
    head_count = len(pieces) // heads
    copies = []
    for at, piece in enumerate(pieces):
        cols = head_columns(place, at % heads, heads, at // heads, head_count)
        for kv, ref in enumerate((k_ref, v_ref)):
            copies.append(pltpu.make_async_copy(piece.at[kv], ref.at[:, cols], sem.at[2 * at + kv]))
    for copy in copies:
        copy.start()
    for copy in copies:
        copy.wait()


def fill_table(place, own, h, table):
    heads = len(own)
    per_quarter = own[0].shape[2] // BLK
    for r in range(heads):
        first = origin(place[1], r, heads) * per_quarter
        for kv in range(2):
            for j in range(per_quarter):
                table[kv, first + j] = own[r][h, kv, j * BLK : (j + 1) * BLK, :]


def pick(table, asked, there, out):
    for s in range(CAP):
        block = asked[there, s]
        for kv in range(2):
            out[kv, s] = table[kv, block]


def pick_kernel(place, asked, *refs, heads, steps, head, shard_count):
    own, outs, table = refs[:heads], refs[heads:-1], refs[-1]
    for h in range(own[0].shape[0]):
        mine = [(r, out if len(out.shape) == 4 else out.at[h]) for r, out in zip(steps, outs)
                if h == head or len(out.shape) == 5]
        if mine:
            fill_table(place, own, h, table)
        for r, out in mine:
            pick(table, asked, partner(place[0], r, shard_count), out)


def by_head(ref, b):
    rows = slice(b * BLK, (b + 1) * BLK)
    return jnp.concatenate([ref[rows, g * HEAD_DIM : (g + 1) * HEAD_DIM] for g in range(GROUP)], axis=0)


def by_row(ref, b, x):
    rows = slice(b * BLK, (b + 1) * BLK)
    for g in range(GROUP):
        ref[rows, g * HEAD_DIM : (g + 1) * HEAD_DIM] = x[g * BLK : (g + 1) * BLK]


def attend_kernel(place, source, q_ref, g_ref, *refs, heads, head, kept, shard_count):
    steps = shard_count - 1
    own, far = refs[:heads], refs[heads : heads + steps]
    near_grads = refs[heads + steps : heads + steps + kept]
    table, total = refs[-2:]
    outs = refs[-2 - steps : -2]
    o_ref, dq_ref, near_out = refs[-5 - steps : -2 - steps]
    step = pl.program_id(0)
    blocks_here = near_out.shape[1]

    @pl.when(step == 0)
    def _():
        fill_table(place, own, 0, table)
        for r, part in zip(steps_of(shard_count), far):
            first = blocks_here + origin(place[0], r, shard_count) * CAP
            part = part.at[head] if len(part.shape) == 5 else part
            for kv in range(2):
                for s in range(CAP):
                    table[kv, first + s] = part[kv, s]
        total[...] = jnp.zeros_like(total)

    key_row = lax.broadcasted_iota(jnp.int32, (BLK, GROUP * BLK), 0)
    query_col = lax.broadcasted_iota(jnp.int32, (BLK, GROUP * BLK), 1) % BLK
    hidden = key_row > query_col
    for first in range(0, STEP_BLOCKS, TOGETHER):
        subs = range(first, first + TOGETHER)
        listed = {b: [source[(step * STEP_BLOCKS + b) * LIST + e] for e in range(LIST)] for b in subs}
        q = {b: by_head(q_ref, b) for b in subs}
        g_out = {b: by_head(g_ref, b) for b in subs}
        keys = {b: jnp.concatenate([table[0, at] for at in listed[b]], axis=0) for b in subs}
        values = {b: jnp.concatenate([table[1, at] for at in listed[b]], axis=0) for b in subs}
        scores = {b: dot(keys[b], q[b], NT) for b in subs}
        dprob, probs, probs_low, dscore = {}, {}, {}, {}
        for b in subs:
            block = step * STEP_BLOCKS + b
            parts = []
            for e in range(LIST):
                mask = hidden if e == 0 else hidden & (listed[b][e] == block)
                parts.append(jnp.where(mask, NEG_FILL, scores[b][e * BLK : (e + 1) * BLK]))
            masked = jnp.concatenate(parts, axis=0)
            dprob[b] = dot(values[b], g_out[b], NT)
            peak = jnp.max(masked, axis=0, keepdims=True)
            expo = jnp.exp2((masked - peak) * (SCALE * LOG2E))
            probs[b] = expo * (1.0 / jnp.sum(expo, axis=0, keepdims=True))
            probs_low[b] = probs[b].astype(jnp.bfloat16)
        for b in subs:
            attended = dot(values[b], probs_low[b], TN).astype(jnp.bfloat16).T
            by_row(o_ref, b, attended)
            dv = dot(probs_low[b], g_out[b], NN)
            delta = jnp.sum(probs[b] * dprob[b], axis=0, keepdims=True)
            dscore[b] = (probs[b] * (dprob[b] - delta)).astype(jnp.bfloat16)
            for e in range(LIST):
                total[1, listed[b][e]] += dv[e * BLK : (e + 1) * BLK]
        for b in subs:
            dq = (dot(keys[b], dscore[b], TN) * SCALE).astype(jnp.bfloat16).T
            by_row(dq_ref, b, dq)
            dk = dot(dscore[b], q[b], NN)
            for e in range(LIST):
                total[0, listed[b][e]] += dk[e * BLK : (e + 1) * BLK]

    @pl.when(step == pl.num_programs(0) - 1)
    def _():
        for kv, factor in ((0, SCALE), (1, 1.0)):
            near_out[kv] = total[kv, :blocks_here] * factor
        kept_refs = list(near_grads)
        for r, out in zip(steps_of(shard_count), outs):
            there = partner(place[0], r, shard_count)
            if len(out.shape) == 5:
                if head:
                    out[:head] = kept_refs.pop(0)[...]
                out = out.at[head]

            @pl.when(there < place[0])
            def _():
                for kv, factor in ((0, SCALE), (1, 1.0)):
                    for s in range(CAP):
                        out[kv, s] = (total[kv, blocks_here + there * CAP + s] * factor).astype(jnp.bfloat16)

            @pl.when(there > place[0])
            def _():
                out[...] = jnp.zeros_like(out)


def gather_sum_kernel(place, asked, near, *refs, heads, head, shard_count):
    back, outs, total = refs[: -heads - 1], refs[-heads - 1 : -1], refs[-1]
    per_quarter = outs[0].shape[1] // BLK
    total[...] = near[...]
    for r, part in zip(steps_of(shard_count), back):
        there = origin(place[0], r, shard_count)
        part = part.at[head] if len(part.shape) == 5 else part

        @pl.when(there > place[0])
        def _():
            for s in range(CAP):
                block = asked[there, s]
                for kv in range(2):
                    total[kv, block] += part[kv, s].astype(jnp.float32)

    for r in range(heads):
        first = origin(place[1], r, heads) * per_quarter
        for kv in range(2):
            for j in range(per_quarter):
                outs[r][kv, j * BLK : (j + 1) * BLK, :] = total[kv, first + j].astype(jnp.bfloat16)


def whole(shape):
    return pl.BlockSpec(tuple(shape), lambda *_: (0,) * len(shape))


def heads_from(shape, head, count):
    return pl.BlockSpec((pl.Element(count), *(pl.Element(n) for n in shape[1:])), lambda *_: (head, *(0,) * (len(shape) - 1)))


ANYWHERE = pl.BlockSpec(memory_space=pl.ANY)


def bf16(*shape):
    return jax.ShapeDtypeStruct(shape, jnp.bfloat16)


def call(kernel, scalars, arrays, out_shapes, scratch, name, any_in=False, any_out=False, limit=VMEM_LIMIT):
    return pl.pallas_call(
        kernel,
        grid_spec=pltpu.PrefetchScalarGridSpec(
            num_scalar_prefetch=len(scalars),
            grid=(1,),
            in_specs=[ANYWHERE if any_in else whole(x.shape) for x in arrays],
            out_specs=[ANYWHERE if any_out else whole(x.shape) for x in out_shapes],
            scratch_shapes=scratch,
        ),
        out_shape=out_shapes,
        compiler_params=params(limit),
        name=name,
    )(*scalars, *arrays)


def attend(place, source, queries, out_grad, own, far, near_grads, head, earlier, shard_count):
    tokens_here, width = queries.shape
    blocks_here = tokens_here // BLK
    slots = blocks_here + shard_count * CAP
    tile = pl.BlockSpec((STEP_BLOCKS * BLK, GROUP * HEAD_DIM), lambda i, *_: (i, head))
    near_shape = (2, blocks_here, BLK, HEAD_DIM)
    arrays = [*own, *far, *near_grads]
    first = 4 + len(arrays)
    one = (2, CAP, BLK, HEAD_DIM)
    out_shapes = [bf16(head + 1, *one) if r in near_steps(shard_count) else bf16(*one) for r in steps_of(shard_count)]
    return pl.pallas_call(
        functools.partial(
            attend_kernel, heads=len(own), head=head, kept=len(near_grads), shard_count=shard_count
        ),
        grid_spec=pltpu.PrefetchScalarGridSpec(
            num_scalar_prefetch=2,
            grid=(blocks_here // STEP_BLOCKS,),
            in_specs=[tile, tile]
            + [heads_from(x.shape, head, 1) for x in own]
            + [whole(x.shape) for x in [*far, *near_grads]]
            + [ANYWHERE] * len(earlier),
            out_specs=[tile, tile, whole(near_shape)] + [whole(x.shape) for x in out_shapes],
            scratch_shapes=[
                pltpu.VMEM((2, slots, BLK, HEAD_DIM), jnp.bfloat16),
                pltpu.VMEM((2, slots, BLK, HEAD_DIM), jnp.float32),
            ],
        ),
        out_shape=[bf16(tokens_here, width), bf16(tokens_here, width), jax.ShapeDtypeStruct(near_shape, jnp.float32)]
        + out_shapes,
        input_output_aliases={first: 0, first + 1: 1} if earlier else {},
        compiler_params=params(),
        cost_estimate=pl.CostEstimate(
            flops=12 * blocks_here * LIST * BLK * GROUP * BLK * HEAD_DIM,
            bytes_accessed=20 * 1024 * 1024,
            transcendentals=blocks_here * LIST * BLK * GROUP * BLK,
        ),
        name="attend",
    )(place, source, queries, out_grad, *arrays, *earlier)


def send(x, axis, count, r):
    return lax.ppermute(x, axis, [(i, partner(i, r, count)) for i in range(count)])


def send_back(x, axis, count, r):
    return lax.ppermute(x, axis, [(i, origin(i, r, count)) for i in range(count)])


def requests_of(flat_ids, blocks_here, shard_index, shard_count):
    owner = flat_ids // blocks_here
    shards = jnp.arange(shard_count, dtype=jnp.int32)
    inner = jnp.arange(blocks_here, dtype=jnp.int32)
    every_block = jnp.arange(shard_count * blocks_here, dtype=jnp.int32)
    listed = jnp.any(flat_ids[:, None] == every_block[None, :], axis=0)
    grid = listed.reshape(shard_count, blocks_here) & (shards != shard_index)[:, None]
    rank = jnp.sum((grid[:, :, None] & (inner[:, None] < inner[None, :])[None]).astype(jnp.int32), axis=1)
    hit = grid[:, None] & (rank[:, None] == jnp.arange(128, dtype=jnp.int32)[None, :, None])
    requests = jnp.sum(jnp.where(hit, inner[None, None], 0), axis=2)
    same_owner = owner[:, None] == (every_block // blocks_here)[None, :]
    place_of = jnp.sum((same_owner & listed[None, :] & (every_block[None, :] < flat_ids[:, None])).astype(jnp.int32), axis=1)
    source = jnp.where(owner == shard_index, flat_ids % blocks_here, blocks_here + owner * CAP + place_of)
    return requests, source


def after(x, *others):
    return lax.optimization_barrier((x, *others))[0]


def per_device(queries, key_states, value_states, block_lists, out_grad):
    shard_index = lax.axis_index("ctx")
    shard_count = lax.axis_size("ctx")
    heads = lax.axis_size("head")
    blocks_here = queries.shape[0] // BLK
    quarter = key_states.shape[0]
    head_count = key_states.shape[1] // heads // HEAD_DIM
    place = jnp.stack([shard_index, lax.axis_index("head")]).astype(jnp.int32)

    pieces = call(
        split_kernel,
        [place],
        [key_states, value_states],
        [bf16(head_count, 2, quarter, HEAD_DIM)] * heads,
        [pltpu.SemaphoreType.DMA((2 * heads * head_count,))],
        "split",
        any_in=True,
        limit=VMEM_MOST,
    )
    own = [pieces[0]] + [send(pieces[r], "head", heads, r) for r in range(1, heads)]

    requests, source = requests_of(after(block_lists, *own[1:2]).reshape(-1), blocks_here, shard_index, shard_count)
    asked = lax.all_to_all(requests, "ctx", split_axis=0, concat_axis=0, tiled=True)

    steps = steps_of(shard_count)
    near = [r for r in steps if r in near_steps(shard_count)]
    wide = [r for r in steps if r not in near]
    one = (2, CAP, BLK, HEAD_DIM)

    def exchange(arrays):
        return {r: send(x, "ctx", shard_count, r) for r, x in arrays}

    def picked(head, steps):
        arrays = call(
            functools.partial(pick_kernel, heads=heads, steps=steps, head=head, shard_count=shard_count),
            [place, asked],
            own,
            [bf16(head_count, *one) if r in near else bf16(*one) for r in steps],
            [pltpu.VMEM((2, blocks_here, BLK, HEAD_DIM), jnp.bfloat16)],
            "pick",
        )
        return list(zip(steps, arrays))

    come, near_grads, earlier, nears, backs = exchange(picked(0, steps)), [], [], [], []
    for h in range(head_count):
        ahead = {}
        if h + 1 < head_count:
            ahead = exchange([(r, after(x, *[come[n] for n in near[:2]])) for r, x in picked(h + 1, wide)])
        attended, query_grad, local, *go = attend(
            place, source, queries, out_grad, own, [come[r] for r in steps], near_grads, h, earlier, shard_count
        )
        go = dict(zip(steps, go))
        earlier, near_grads = [attended, query_grad], [go[r] for r in near]
        nears.append(local)
        if h + 1 == head_count:
            sent = [x for back in backs for x in back.values()]
            near_back = exchange([(r, after(go[r], *sent)) for r in near])
        backs.append(exchange([(r, go[r]) for r in wide]))
        come = {**come, **ahead}
    backs = [[{**near_back, **back}[r] for r in steps] for back in backs]
    done = []
    for h in range(head_count):
        sums = call(
            functools.partial(gather_sum_kernel, heads=heads, head=h, shard_count=shard_count),
            [place, asked],
            [after(nears[h], *[backs[-1][steps.index(r)] for r in wide[: len(wide) // 2]], *done[-1:]), *backs[h]],
            [bf16(2, quarter, HEAD_DIM)] * heads,
            [pltpu.VMEM((2, blocks_here, BLK, HEAD_DIM), jnp.float32)],
            "gather_sum",
        )
        done += [sums[0]] + [send_back(sums[r], "head", heads, r) for r in range(1, heads)]
    key_grad, value_grad = call(
        functools.partial(join_kernel, heads=heads),
        [place],
        done,
        [bf16(*key_states.shape)] * 2,
        [pltpu.SemaphoreType.DMA((2 * heads * head_count,))],
        "join",
        any_in=True,
        any_out=True,
    )
    return attended, query_grad, key_grad, value_grad


def solution(mesh):
    return jax.shard_map(
        per_device,
        mesh=mesh,
        in_specs=(
            P("ctx", "head"),
            P(("ctx", "head"), None),
            P(("ctx", "head"), None),
            P("ctx", None),
            P("ctx", "head"),
        ),
        out_specs=(
            P("ctx", "head"),
            P("ctx", "head"),
            P(("ctx", "head"), None),
            P(("ctx", "head"), None),
        ),
        check_vma=False,
    )
```

```python
import functools

import jax
import jax.numpy as jnp
from jax import lax
from jax.experimental import pallas as pl
from jax.experimental.pallas import tpu as pltpu
from jax.sharding import PartitionSpec as P

HEAD_DIM = 128
GROUP = 4
BLK = 64
LIST = 8
CAP = 3
STEP_BLOCKS = 4
SPLIT_STEPS = 4
TOGETHER = 4
NEG_FILL = -1e30
SCALE = HEAD_DIM ** (-0.5)
LOG2E = 1.4426950408889634
VMEM_LIMIT = 50 * 1024 * 1024
VMEM_MOST = 60 * 1024 * 1024

NT = (((1,), (1,)), ((), ()))
NN = (((1,), (0,)), ((), ()))
TN = (((0,), (0,)), ((), ()))


def dot(a, b, dims):
    return lax.dot_general(a, b, dims, preferred_element_type=jnp.float32)


def params(limit=VMEM_LIMIT):
    return pltpu.CompilerParams(vmem_limit_bytes=limit)


def partner(me, r, count):
    return me ^ r if count & (count - 1) == 0 else (me + r) % count


def origin(me, r, count):
    return me ^ r if count & (count - 1) == 0 else (me + count - r) % count


def steps_of(count):
    short = list(range(1, count // 2))
    return short[:2] + list(range(max(1, count // 2), count)) + short[2:]


def head_columns(place, r, heads, h, head_count):
    col = (partner(place[1], r, heads) * head_count + h) * HEAD_DIM
    return pl.ds(pl.multiple_of(col, HEAD_DIM), HEAD_DIM)


def split_kernel(place, k_ref, v_ref, *outs):
    heads, head_count = len(outs), outs[0].shape[0]
    for r, out in enumerate(outs):
        for h in range(head_count):
            cols = head_columns(place, r, heads, h, head_count)
            out[h, 0] = k_ref[:, cols]
            out[h, 1] = v_ref[:, cols]


def join_kernel(place, *refs, heads):
    *pieces, k_ref, v_ref, sem = refs
    head_count = len(pieces) // heads
    copies = []
    for at, piece in enumerate(pieces):
        cols = head_columns(place, at % heads, heads, at // heads, head_count)
        for kv, ref in enumerate((k_ref, v_ref)):
            copies.append(pltpu.make_async_copy(piece.at[kv], ref.at[:, cols], sem.at[2 * at + kv]))
    for copy in copies:
        copy.start()
    for copy in copies:
        copy.wait()


def fill_table(place, own, h, table):
    heads = len(own)
    per_quarter = own[0].shape[2] // BLK
    for r in range(heads):
        first = origin(place[1], r, heads) * per_quarter
        for kv in range(2):
            for j in range(per_quarter):
                table[kv, first + j] = own[r][h, kv, j * BLK : (j + 1) * BLK, :]


def pick(table, asked, there, out):
    for s in range(CAP):
        block = asked[there, s]
        for kv in range(2):
            out[kv, s] = table[kv, block]


def pick_kernel(place, asked, *refs, heads, steps, head, shard_count):
    own, outs, table = refs[:heads], refs[heads:-1], refs[-1]
    fill_table(place, own, head, table)
    for r, out in zip(steps, outs):
        pick(table, asked, partner(place[0], r, shard_count), out)


def by_head(ref, b):
    rows = slice(b * BLK, (b + 1) * BLK)
    return jnp.concatenate([ref[rows, g * HEAD_DIM : (g + 1) * HEAD_DIM] for g in range(GROUP)], axis=0)


def by_row(ref, b, x):
    rows = slice(b * BLK, (b + 1) * BLK)
    for g in range(GROUP):
        ref[rows, g * HEAD_DIM : (g + 1) * HEAD_DIM] = x[g * BLK : (g + 1) * BLK]


def attend_kernel(place, source, asked, q_ref, g_ref, *refs, heads, head, last, shard_count):
    steps = shard_count - 1
    own, far = refs[:heads], refs[heads : heads + steps]
    table, total = refs[-2:]
    outs = refs[-2 - steps : -2]
    o_ref, dq_ref, near_out = refs[-5 - steps : -2 - steps]
    step = pl.program_id(0)
    blocks_here = near_out.shape[1]

    @pl.when(step == 0)
    def _():
        fill_table(place, own, 0, table)
        for r, part in zip(steps_of(shard_count), far):
            first = blocks_here + origin(place[0], r, shard_count) * CAP
            for kv in range(2):
                for s in range(CAP):
                    table[kv, first + s] = part[kv, s]
        total[...] = jnp.zeros_like(total)

    key_row = lax.broadcasted_iota(jnp.int32, (BLK, GROUP * BLK), 0)
    query_col = lax.broadcasted_iota(jnp.int32, (BLK, GROUP * BLK), 1) % BLK
    hidden = key_row > query_col
    for first in range(0, STEP_BLOCKS, TOGETHER):
        subs = range(first, first + TOGETHER)
        listed = {b: [source[(step * STEP_BLOCKS + b) * LIST + e] for e in range(LIST)] for b in subs}
        q = {b: by_head(q_ref, b) for b in subs}
        g_out = {b: by_head(g_ref, b) for b in subs}
        keys = {b: jnp.concatenate([table[0, at] for at in listed[b]], axis=0) for b in subs}
        values = {b: jnp.concatenate([table[1, at] for at in listed[b]], axis=0) for b in subs}
        scores = {b: dot(keys[b], q[b], NT) for b in subs}
        dprob, probs, probs_low, dscore = {}, {}, {}, {}
        for b in subs:
            block = step * STEP_BLOCKS + b
            parts = []
            for e in range(LIST):
                mask = hidden if e == 0 else hidden & (listed[b][e] == block)
                parts.append(jnp.where(mask, NEG_FILL, scores[b][e * BLK : (e + 1) * BLK]))
            masked = jnp.concatenate(parts, axis=0)
            dprob[b] = dot(values[b], g_out[b], NT)
            peak = jnp.max(masked, axis=0, keepdims=True)
            expo = jnp.exp2((masked - peak) * (SCALE * LOG2E))
            probs[b] = expo * (1.0 / jnp.sum(expo, axis=0, keepdims=True))
            probs_low[b] = probs[b].astype(jnp.bfloat16)
        for b in subs:
            attended = dot(values[b], probs_low[b], TN).astype(jnp.bfloat16).T
            by_row(o_ref, b, attended)
            dv = dot(probs_low[b], g_out[b], NN)
            delta = jnp.sum(probs[b] * dprob[b], axis=0, keepdims=True)
            dscore[b] = (probs[b] * (dprob[b] - delta)).astype(jnp.bfloat16)
            for e in range(LIST):
                total[1, listed[b][e]] += dv[e * BLK : (e + 1) * BLK]
        for b in subs:
            dq = (dot(keys[b], dscore[b], TN) * SCALE).astype(jnp.bfloat16).T
            by_row(dq_ref, b, dq)
            dk = dot(dscore[b], q[b], NN)
            for e in range(LIST):
                total[0, listed[b][e]] += dk[e * BLK : (e + 1) * BLK]

    @pl.when(step == pl.num_programs(0) - 1)
    def _():
        for kv, factor in ((0, SCALE), (1, 1.0)):
            near_out[kv] = total[kv, :blocks_here] * factor
        if not last:
            fill_table(place, own, 1, table)
        for r, out in zip(steps_of(shard_count), outs):
            there = partner(place[0], r, shard_count)

            @pl.when(there < place[0])
            def _():
                for kv, factor in ((0, SCALE), (1, 1.0)):
                    for s in range(CAP):
                        out[kv, s] = (total[kv, blocks_here + there * CAP + s] * factor).astype(jnp.bfloat16)

            @pl.when(there > place[0])
            def _():
                if last or r >= shard_count // 2:
                    out[...] = jnp.zeros_like(out)
                else:
                    pick(table, asked, there, out)


def gather_sum_kernel(place, asked, near, *refs, heads, shard_count):
    back, outs, total = refs[: -heads - 1], refs[-heads - 1 : -1], refs[-1]
    per_quarter = outs[0].shape[1] // BLK
    total[...] = near[...]
    for r, part in zip(steps_of(shard_count), back):
        there = origin(place[0], r, shard_count)

        @pl.when(there > place[0])
        def _():
            for s in range(CAP):
                block = asked[there, s]
                for kv in range(2):
                    total[kv, block] += part[kv, s].astype(jnp.float32)

    for r in range(heads):
        first = origin(place[1], r, heads) * per_quarter
        for kv in range(2):
            for j in range(per_quarter):
                outs[r][kv, j * BLK : (j + 1) * BLK, :] = total[kv, first + j].astype(jnp.bfloat16)


def whole(shape):
    return pl.BlockSpec(tuple(shape), lambda *_: (0,) * len(shape))


def heads_from(shape, head, count):
    return pl.BlockSpec((pl.Element(count), *(pl.Element(n) for n in shape[1:])), lambda *_: (head, *(0,) * (len(shape) - 1)))


ANYWHERE = pl.BlockSpec(memory_space=pl.ANY)


def bf16(*shape):
    return jax.ShapeDtypeStruct(shape, jnp.bfloat16)


def call(kernel, scalars, arrays, out_shapes, scratch, name, any_in=False, any_out=False, limit=VMEM_LIMIT):
    return pl.pallas_call(
        kernel,
        grid_spec=pltpu.PrefetchScalarGridSpec(
            num_scalar_prefetch=len(scalars),
            grid=(1,),
            in_specs=[ANYWHERE if any_in else whole(x.shape) for x in arrays],
            out_specs=[ANYWHERE if any_out else whole(x.shape) for x in out_shapes],
            scratch_shapes=scratch,
        ),
        out_shape=out_shapes,
        compiler_params=params(limit),
        name=name,
    )(*scalars, *arrays)


def split(place, key_states, value_states, heads, head_count):
    quarter, width = key_states.shape
    rows = quarter // SPLIT_STEPS
    return pl.pallas_call(
        split_kernel,
        grid_spec=pltpu.PrefetchScalarGridSpec(
            num_scalar_prefetch=1,
            grid=(SPLIT_STEPS,),
            in_specs=[pl.BlockSpec((rows, width), lambda i, *_: (i, 0))] * 2,
            out_specs=[pl.BlockSpec((head_count, 2, rows, HEAD_DIM), lambda i, *_: (0, 0, i, 0))] * heads,
        ),
        out_shape=[bf16(head_count, 2, quarter, HEAD_DIM)] * heads,
        compiler_params=params(VMEM_MOST),
        name="split",
    )(place, key_states, value_states)


def attend(place, source, asked, queries, out_grad, own, far, head, last, earlier, shard_count):
    tokens_here, width = queries.shape
    blocks_here = tokens_here // BLK
    slots = blocks_here + shard_count * CAP
    tile = pl.BlockSpec((STEP_BLOCKS * BLK, GROUP * HEAD_DIM), lambda i, *_: (i, head))
    near_shape = (2, blocks_here, BLK, HEAD_DIM)
    arrays = [*own, *far]
    first = 5 + len(arrays)
    out_shapes = [bf16(2, CAP, BLK, HEAD_DIM)] * (shard_count - 1)
    return pl.pallas_call(
        functools.partial(
            attend_kernel, heads=len(own), head=head, last=last, shard_count=shard_count
        ),
        grid_spec=pltpu.PrefetchScalarGridSpec(
            num_scalar_prefetch=3,
            grid=(blocks_here // STEP_BLOCKS,),
            in_specs=[tile, tile]
            + [heads_from(x.shape, head, 1 if last else 2) for x in own]
            + [whole(x.shape) for x in far]
            + [ANYWHERE] * len(earlier),
            out_specs=[tile, tile, whole(near_shape)] + [whole(x.shape) for x in out_shapes],
            scratch_shapes=[
                pltpu.VMEM((2, slots, BLK, HEAD_DIM), jnp.bfloat16),
                pltpu.VMEM((2, slots, BLK, HEAD_DIM), jnp.float32),
            ],
        ),
        out_shape=[bf16(tokens_here, width), bf16(tokens_here, width), jax.ShapeDtypeStruct(near_shape, jnp.float32)]
        + out_shapes,
        input_output_aliases={first: 0, first + 1: 1} if earlier else {},
        compiler_params=params(),
        cost_estimate=pl.CostEstimate(
            flops=12 * blocks_here * LIST * BLK * GROUP * BLK * HEAD_DIM,
            bytes_accessed=20 * 1024 * 1024,
            transcendentals=blocks_here * LIST * BLK * GROUP * BLK,
        ),
        name="attend",
    )(place, source, asked, queries, out_grad, *arrays, *earlier)


def send(x, axis, count, r):
    return lax.ppermute(x, axis, [(i, partner(i, r, count)) for i in range(count)])


def send_back(x, axis, count, r):
    return lax.ppermute(x, axis, [(i, origin(i, r, count)) for i in range(count)])


def requests_of(flat_ids, blocks_here, shard_index, shard_count):
    owner = flat_ids // blocks_here
    shards = jnp.arange(shard_count, dtype=jnp.int32)
    inner = jnp.arange(blocks_here, dtype=jnp.int32)
    every_block = jnp.arange(shard_count * blocks_here, dtype=jnp.int32)
    listed = jnp.any(flat_ids[:, None] == every_block[None, :], axis=0)
    grid = listed.reshape(shard_count, blocks_here) & (shards != shard_index)[:, None]
    rank = jnp.sum((grid[:, :, None] & (inner[:, None] < inner[None, :])[None]).astype(jnp.int32), axis=1)
    hit = grid[:, None] & (rank[:, None] == jnp.arange(128, dtype=jnp.int32)[None, :, None])
    requests = jnp.sum(jnp.where(hit, inner[None, None], 0), axis=2)
    same_owner = owner[:, None] == (every_block // blocks_here)[None, :]
    place_of = jnp.sum((same_owner & listed[None, :] & (every_block[None, :] < flat_ids[:, None])).astype(jnp.int32), axis=1)
    source = jnp.where(owner == shard_index, flat_ids % blocks_here, blocks_here + owner * CAP + place_of)
    return requests, source


def after(x, *others):
    return lax.optimization_barrier((x, *others))[0]


def per_device(queries, key_states, value_states, block_lists, out_grad):
    shard_index = lax.axis_index("ctx")
    shard_count = lax.axis_size("ctx")
    heads = lax.axis_size("head")
    blocks_here = queries.shape[0] // BLK
    quarter = key_states.shape[0]
    head_count = key_states.shape[1] // heads // HEAD_DIM
    place = jnp.stack([shard_index, lax.axis_index("head")]).astype(jnp.int32)

    pieces = split(place, key_states, value_states, heads, head_count)
    own = [pieces[0]] + [send(pieces[r], "head", heads, r) for r in range(1, heads)]

    requests, source = requests_of(after(block_lists, *own[1:2]).reshape(-1), blocks_here, shard_index, shard_count)
    asked = lax.all_to_all(requests, "ctx", split_axis=0, concat_axis=0, tiled=True)

    steps = steps_of(shard_count)
    wide = [r for r in steps if r >= shard_count // 2]

    def exchange(arrays):
        return {r: send(x, "ctx", shard_count, r) for r, x in arrays}

    def picked(head, steps):
        arrays = call(
            functools.partial(pick_kernel, heads=heads, steps=steps, head=head, shard_count=shard_count),
            [place, asked],
            own,
            [bf16(2, CAP, BLK, HEAD_DIM)] * len(steps),
            [pltpu.VMEM((2, blocks_here, BLK, HEAD_DIM), jnp.bfloat16)],
            "pick",
        )
        return list(zip(steps, arrays))

    come, earlier, nears, backs = exchange(picked(0, steps)), [], [], []
    for h in range(head_count):
        last = h == head_count - 1
        ahead = {}
        if not last:
            ahead = exchange([(r, after(x, *[come[n] for n in steps[:3]])) for r, x in picked(h + 1, wide)])
        attended, query_grad, near, *go = attend(
            place, source, asked, queries, out_grad, own, [come[r] for r in steps], h, last, earlier, shard_count
        )
        earlier = [attended, query_grad]
        nears.append(near)
        back = exchange(zip(steps, go))
        backs.append([back[r] for r in steps])
        come = {**back, **ahead}
    done = []
    for h in range(head_count):
        sums = call(
            functools.partial(gather_sum_kernel, heads=heads, shard_count=shard_count),
            [place, asked],
            [after(nears[h], nears[-1], *done[-1:]), *backs[h]],
            [bf16(2, quarter, HEAD_DIM)] * heads,
            [pltpu.VMEM((2, blocks_here, BLK, HEAD_DIM), jnp.float32)],
            "gather_sum",
        )
        done += [sums[0]] + [send_back(sums[r], "head", heads, r) for r in range(1, heads)]
    key_grad, value_grad = call(
        functools.partial(join_kernel, heads=heads),
        [place],
        done,
        [bf16(*key_states.shape)] * 2,
        [pltpu.SemaphoreType.DMA((2 * heads * head_count,))],
        "join",
        any_in=True,
        any_out=True,
    )
    return attended, query_grad, key_grad, value_grad


def solution(mesh):
    return jax.shard_map(
        per_device,
        mesh=mesh,
        in_specs=(
            P("ctx", "head"),
            P(("ctx", "head"), None),
            P(("ctx", "head"), None),
            P("ctx", None),
            P("ctx", "head"),
        ),
        out_specs=(
            P("ctx", "head"),
            P("ctx", "head"),
            P(("ctx", "head"), None),
            P(("ctx", "head"), None),
        ),
        check_vma=False,
    )
```

```python
import functools

import jax
import jax.numpy as jnp
from jax import lax
from jax.experimental import pallas as pl
from jax.experimental.pallas import tpu as pltpu
from jax.sharding import PartitionSpec as P

HEAD_DIM = 128
GROUP = 4
BLK = 64
LIST = 8
CAP = 3
STEP_BLOCKS = 4
TOGETHER = 4
NEG_FILL = -1e30
SCALE = HEAD_DIM ** (-0.5)
LOG2E = 1.4426950408889634
VMEM_LIMIT = 50 * 1024 * 1024
VMEM_MOST = 60 * 1024 * 1024

NT = (((1,), (1,)), ((), ()))
NN = (((1,), (0,)), ((), ()))
TN = (((0,), (0,)), ((), ()))


def dot(a, b, dims):
    return lax.dot_general(a, b, dims, preferred_element_type=jnp.float32)


def params(limit=VMEM_LIMIT):
    return pltpu.CompilerParams(vmem_limit_bytes=limit)


def partner(me, r, count):
    return me ^ r if count & (count - 1) == 0 else (me + r) % count


def origin(me, r, count):
    return me ^ r if count & (count - 1) == 0 else (me + count - r) % count


def steps_of(count):
    short = list(range(1, count // 2))
    return short[:2] + list(range(max(1, count // 2), count)) + short[2:]


def head_columns(place, r, heads, h, head_count):
    col = (partner(place[1], r, heads) * head_count + h) * HEAD_DIM
    return pl.ds(pl.multiple_of(col, HEAD_DIM), HEAD_DIM)


def split_kernel(place, k_ref, v_ref, *refs):
    *outs, sem = refs
    heads, head_count = len(outs), outs[0].shape[0]
    copies = []
    for r, out in enumerate(outs):
        for h in range(head_count):
            cols = head_columns(place, r, heads, h, head_count)
            for kv, ref in enumerate((k_ref, v_ref)):
                at = (r * head_count + h) * 2 + kv
                copies.append(pltpu.make_async_copy(ref.at[:, cols], out.at[h, kv], sem.at[at]))
    for copy in copies:
        copy.start()
    for copy in copies:
        copy.wait()


def join_kernel(place, *refs, heads):
    *pieces, k_ref, v_ref, sem = refs
    head_count = len(pieces) // heads
    copies = []
    for at, piece in enumerate(pieces):
        cols = head_columns(place, at % heads, heads, at // heads, head_count)
        for kv, ref in enumerate((k_ref, v_ref)):
            copies.append(pltpu.make_async_copy(piece.at[kv], ref.at[:, cols], sem.at[2 * at + kv]))
    for copy in copies:
        copy.start()
    for copy in copies:
        copy.wait()


def fill_table(place, own, h, table):
    heads = len(own)
    per_quarter = own[0].shape[2] // BLK
    for r in range(heads):
        first = origin(place[1], r, heads) * per_quarter
        for kv in range(2):
            for j in range(per_quarter):
                table[kv, first + j] = own[r][h, kv, j * BLK : (j + 1) * BLK, :]


def pick(table, asked, there, out):
    for s in range(CAP):
        block = asked[there, s]
        for kv in range(2):
            out[kv, s] = table[kv, block]


def pick_kernel(place, asked, *refs, heads, steps, head, shard_count):
    own, outs, table = refs[:heads], refs[heads:-1], refs[-1]
    fill_table(place, own, head, table)
    for r, out in zip(steps, outs):
        pick(table, asked, partner(place[0], r, shard_count), out)


def by_head(ref, b):
    rows = slice(b * BLK, (b + 1) * BLK)
    return jnp.concatenate([ref[rows, g * HEAD_DIM : (g + 1) * HEAD_DIM] for g in range(GROUP)], axis=0)


def by_row(ref, b, x):
    rows = slice(b * BLK, (b + 1) * BLK)
    for g in range(GROUP):
        ref[rows, g * HEAD_DIM : (g + 1) * HEAD_DIM] = x[g * BLK : (g + 1) * BLK]


def attend_kernel(place, source, asked, q_ref, g_ref, *refs, heads, head, last, shard_count):
    steps = shard_count - 1
    own, far = refs[:heads], refs[heads : heads + steps]
    table, total = refs[-2:]
    outs = refs[-2 - steps : -2]
    o_ref, dq_ref, near_out = refs[-5 - steps : -2 - steps]
    step = pl.program_id(0)
    blocks_here = near_out.shape[1]

    @pl.when(step == 0)
    def _():
        fill_table(place, own, 0, table)
        for r, part in zip(steps_of(shard_count), far):
            first = blocks_here + origin(place[0], r, shard_count) * CAP
            for kv in range(2):
                for s in range(CAP):
                    table[kv, first + s] = part[kv, s]
        total[...] = jnp.zeros_like(total)

    key_row = lax.broadcasted_iota(jnp.int32, (BLK, GROUP * BLK), 0)
    query_col = lax.broadcasted_iota(jnp.int32, (BLK, GROUP * BLK), 1) % BLK
    hidden = key_row > query_col
    for first in range(0, STEP_BLOCKS, TOGETHER):
        subs = range(first, first + TOGETHER)
        listed = {b: [source[(step * STEP_BLOCKS + b) * LIST + e] for e in range(LIST)] for b in subs}
        q = {b: by_head(q_ref, b) for b in subs}
        g_out = {b: by_head(g_ref, b) for b in subs}
        keys = {b: jnp.concatenate([table[0, at] for at in listed[b]], axis=0) for b in subs}
        values = {b: jnp.concatenate([table[1, at] for at in listed[b]], axis=0) for b in subs}
        scores = {b: dot(keys[b], q[b], NT) for b in subs}
        dprob, probs, probs_low, dscore = {}, {}, {}, {}
        for b in subs:
            block = step * STEP_BLOCKS + b
            parts = []
            for e in range(LIST):
                mask = hidden if e == 0 else hidden & (listed[b][e] == block)
                parts.append(jnp.where(mask, NEG_FILL, scores[b][e * BLK : (e + 1) * BLK]))
            masked = jnp.concatenate(parts, axis=0)
            dprob[b] = dot(values[b], g_out[b], NT)
            peak = jnp.max(masked, axis=0, keepdims=True)
            expo = jnp.exp2((masked - peak) * (SCALE * LOG2E))
            probs[b] = expo * (1.0 / jnp.sum(expo, axis=0, keepdims=True))
            probs_low[b] = probs[b].astype(jnp.bfloat16)
        for b in subs:
            attended = dot(values[b], probs_low[b], TN).astype(jnp.bfloat16).T
            by_row(o_ref, b, attended)
            dv = dot(probs_low[b], g_out[b], NN)
            delta = jnp.sum(probs[b] * dprob[b], axis=0, keepdims=True)
            dscore[b] = (probs[b] * (dprob[b] - delta)).astype(jnp.bfloat16)
            for e in range(LIST):
                total[1, listed[b][e]] += dv[e * BLK : (e + 1) * BLK]
        for b in subs:
            dq = (dot(keys[b], dscore[b], TN) * SCALE).astype(jnp.bfloat16).T
            by_row(dq_ref, b, dq)
            dk = dot(dscore[b], q[b], NN)
            for e in range(LIST):
                total[0, listed[b][e]] += dk[e * BLK : (e + 1) * BLK]

    @pl.when(step == pl.num_programs(0) - 1)
    def _():
        for kv, factor in ((0, SCALE), (1, 1.0)):
            near_out[kv] = (total[kv, :blocks_here] * factor).astype(jnp.bfloat16)
        if not last:
            fill_table(place, own, 1, table)
        for r, out in zip(steps_of(shard_count), outs):
            there = partner(place[0], r, shard_count)

            @pl.when(there < place[0])
            def _():
                for kv, factor in ((0, SCALE), (1, 1.0)):
                    for s in range(CAP):
                        out[kv, s] = (total[kv, blocks_here + there * CAP + s] * factor).astype(jnp.bfloat16)

            @pl.when(there > place[0])
            def _():
                if last or r >= shard_count // 2:
                    out[...] = jnp.zeros_like(out)
                else:
                    pick(table, asked, there, out)


def gather_sum_kernel(place, asked, near, *refs, heads, shard_count):
    back, outs, total = refs[: -heads - 1], refs[-heads - 1 : -1], refs[-1]
    per_quarter = outs[0].shape[1] // BLK
    total[...] = near[...].astype(jnp.float32)
    for r, part in zip(steps_of(shard_count), back):
        there = origin(place[0], r, shard_count)

        @pl.when(there > place[0])
        def _():
            for s in range(CAP):
                block = asked[there, s]
                for kv in range(2):
                    total[kv, block] += part[kv, s].astype(jnp.float32)

    for r in range(heads):
        first = origin(place[1], r, heads) * per_quarter
        for kv in range(2):
            for j in range(per_quarter):
                outs[r][kv, j * BLK : (j + 1) * BLK, :] = total[kv, first + j].astype(jnp.bfloat16)


def whole(shape):
    return pl.BlockSpec(tuple(shape), lambda *_: (0,) * len(shape))


def heads_from(shape, head, count):
    return pl.BlockSpec((pl.Element(count), *(pl.Element(n) for n in shape[1:])), lambda *_: (head, *(0,) * (len(shape) - 1)))


ANYWHERE = pl.BlockSpec(memory_space=pl.ANY)


def bf16(*shape):
    return jax.ShapeDtypeStruct(shape, jnp.bfloat16)


def call(kernel, scalars, arrays, out_shapes, scratch, name, any_in=False, any_out=False, limit=VMEM_LIMIT):
    return pl.pallas_call(
        kernel,
        grid_spec=pltpu.PrefetchScalarGridSpec(
            num_scalar_prefetch=len(scalars),
            grid=(1,),
            in_specs=[ANYWHERE if any_in else whole(x.shape) for x in arrays],
            out_specs=[ANYWHERE if any_out else whole(x.shape) for x in out_shapes],
            scratch_shapes=scratch,
        ),
        out_shape=out_shapes,
        compiler_params=params(limit),
        name=name,
    )(*scalars, *arrays)


def attend(place, source, asked, queries, out_grad, own, far, head, last, earlier, shard_count):
    tokens_here, width = queries.shape
    blocks_here = tokens_here // BLK
    slots = blocks_here + shard_count * CAP
    tile = pl.BlockSpec((STEP_BLOCKS * BLK, GROUP * HEAD_DIM), lambda i, *_: (i, head))
    near_shape = (2, blocks_here, BLK, HEAD_DIM)
    arrays = [*own, *far]
    first = 5 + len(arrays)
    out_shapes = [bf16(2, CAP, BLK, HEAD_DIM)] * (shard_count - 1)
    return pl.pallas_call(
        functools.partial(
            attend_kernel, heads=len(own), head=head, last=last, shard_count=shard_count
        ),
        grid_spec=pltpu.PrefetchScalarGridSpec(
            num_scalar_prefetch=3,
            grid=(blocks_here // STEP_BLOCKS,),
            in_specs=[tile, tile]
            + [heads_from(x.shape, head, 1 if last else 2) for x in own]
            + [whole(x.shape) for x in far]
            + [ANYWHERE] * len(earlier),
            out_specs=[tile, tile, whole(near_shape)] + [whole(x.shape) for x in out_shapes],
            scratch_shapes=[
                pltpu.VMEM((2, slots, BLK, HEAD_DIM), jnp.bfloat16),
                pltpu.VMEM((2, slots, BLK, HEAD_DIM), jnp.float32),
            ],
        ),
        out_shape=[bf16(tokens_here, width), bf16(tokens_here, width), bf16(*near_shape)]
        + out_shapes,
        input_output_aliases={first: 0, first + 1: 1} if earlier else {},
        compiler_params=params(),
        cost_estimate=pl.CostEstimate(
            flops=12 * blocks_here * LIST * BLK * GROUP * BLK * HEAD_DIM,
            bytes_accessed=20 * 1024 * 1024,
            transcendentals=blocks_here * LIST * BLK * GROUP * BLK,
        ),
        name="attend",
    )(place, source, asked, queries, out_grad, *arrays, *earlier)


def send(x, axis, count, r):
    return lax.ppermute(x, axis, [(i, partner(i, r, count)) for i in range(count)])


def send_back(x, axis, count, r):
    return lax.ppermute(x, axis, [(i, origin(i, r, count)) for i in range(count)])


def requests_of(flat_ids, blocks_here, shard_index, shard_count):
    owner = flat_ids // blocks_here
    shards = jnp.arange(shard_count, dtype=jnp.int32)
    inner = jnp.arange(blocks_here, dtype=jnp.int32)
    every_block = jnp.arange(shard_count * blocks_here, dtype=jnp.int32)
    listed = jnp.any(flat_ids[:, None] == every_block[None, :], axis=0)
    grid = listed.reshape(shard_count, blocks_here) & (shards != shard_index)[:, None]
    rank = jnp.sum((grid[:, :, None] & (inner[:, None] < inner[None, :])[None]).astype(jnp.int32), axis=1)
    hit = grid[:, None] & (rank[:, None] == jnp.arange(128, dtype=jnp.int32)[None, :, None])
    requests = jnp.sum(jnp.where(hit, inner[None, None], 0), axis=2)
    same_owner = owner[:, None] == (every_block // blocks_here)[None, :]
    place_of = jnp.sum((same_owner & listed[None, :] & (every_block[None, :] < flat_ids[:, None])).astype(jnp.int32), axis=1)
    source = jnp.where(owner == shard_index, flat_ids % blocks_here, blocks_here + owner * CAP + place_of)
    return requests, source


def after(x, *others):
    return lax.optimization_barrier((x, *others))[0]


def per_device(queries, key_states, value_states, block_lists, out_grad):
    shard_index = lax.axis_index("ctx")
    shard_count = lax.axis_size("ctx")
    heads = lax.axis_size("head")
    blocks_here = queries.shape[0] // BLK
    quarter = key_states.shape[0]
    head_count = key_states.shape[1] // heads // HEAD_DIM
    place = jnp.stack([shard_index, lax.axis_index("head")]).astype(jnp.int32)

    pieces = call(
        split_kernel,
        [place],
        [key_states, value_states],
        [bf16(head_count, 2, quarter, HEAD_DIM)] * heads,
        [pltpu.SemaphoreType.DMA((2 * heads * head_count,))],
        "split",
        any_in=True,
        limit=VMEM_MOST,
    )
    own = [pieces[0]] + [send(pieces[r], "head", heads, r) for r in range(1, heads)]

    requests, source = requests_of(after(block_lists, *own[1:2]).reshape(-1), blocks_here, shard_index, shard_count)
    asked = lax.all_to_all(requests, "ctx", split_axis=0, concat_axis=0, tiled=True)

    steps = steps_of(shard_count)
    wide = [r for r in steps if r >= shard_count // 2]

    def exchange(arrays):
        return {r: send(x, "ctx", shard_count, r) for r, x in arrays}

    def picked(head, steps):
        arrays = call(
            functools.partial(pick_kernel, heads=heads, steps=steps, head=head, shard_count=shard_count),
            [place, asked],
            own,
            [bf16(2, CAP, BLK, HEAD_DIM)] * len(steps),
            [pltpu.VMEM((2, blocks_here, BLK, HEAD_DIM), jnp.bfloat16)],
            "pick",
        )
        return list(zip(steps, arrays))

    come, earlier, nears, backs = exchange(picked(0, steps)), [], [], []
    for h in range(head_count):
        last = h == head_count - 1
        ahead = {}
        if not last:
            ahead = exchange([(r, after(x, *come.values())) for r, x in picked(h + 1, wide)])
        attended, query_grad, near, *go = attend(
            place, source, asked, queries, out_grad, own, [come[r] for r in steps], h, last, earlier, shard_count
        )
        earlier = [attended, query_grad]
        nears.append(near)
        back = exchange(zip(steps, go))
        backs.append([back[r] for r in steps])
        come = {**back, **ahead}
    done = []
    for h in range(head_count):
        sums = call(
            functools.partial(gather_sum_kernel, heads=heads, shard_count=shard_count),
            [place, asked],
            [after(nears[h], nears[-1], *done[-1:]), *backs[h]],
            [bf16(2, quarter, HEAD_DIM)] * heads,
            [pltpu.VMEM((2, blocks_here, BLK, HEAD_DIM), jnp.float32)],
            "gather_sum",
        )
        done += [sums[0]] + [send_back(sums[r], "head", heads, r) for r in range(1, heads)]
    key_grad, value_grad = call(
        functools.partial(join_kernel, heads=heads),
        [place],
        done,
        [bf16(*key_states.shape)] * 2,
        [pltpu.SemaphoreType.DMA((2 * heads * head_count,))],
        "join",
        any_in=True,
        any_out=True,
    )
    return attended, query_grad, key_grad, value_grad


def solution(mesh):
    return jax.shard_map(
        per_device,
        mesh=mesh,
        in_specs=(
            P("ctx", "head"),
            P(("ctx", "head"), None),
            P(("ctx", "head"), None),
            P("ctx", None),
            P("ctx", "head"),
        ),
        out_specs=(
            P("ctx", "head"),
            P("ctx", "head"),
            P(("ctx", "head"), None),
            P(("ctx", "head"), None),
        ),
        check_vma=False,
    )
```

```python
import functools

import jax
import jax.numpy as jnp
from jax import lax
from jax.experimental import pallas as pl
from jax.experimental.pallas import tpu as pltpu
from jax.sharding import PartitionSpec as P

HEAD_DIM = 128
GROUP = 4
BLK = 64
LIST = 8
CAP = 3
STEP_BLOCKS = 4
TOGETHER = 4
NEG_FILL = -1e30
SCALE = HEAD_DIM ** (-0.5)
LOG2E = 1.4426950408889634
VMEM_LIMIT = 50 * 1024 * 1024
VMEM_MOST = 60 * 1024 * 1024

NT = (((1,), (1,)), ((), ()))
NN = (((1,), (0,)), ((), ()))
TN = (((0,), (0,)), ((), ()))


def dot(a, b, dims):
    return lax.dot_general(a, b, dims, preferred_element_type=jnp.float32)


def params(limit=VMEM_LIMIT):
    return pltpu.CompilerParams(vmem_limit_bytes=limit)


def partner(me, r, count):
    return me ^ r if count & (count - 1) == 0 else (me + r) % count


def origin(me, r, count):
    return me ^ r if count & (count - 1) == 0 else (me + count - r) % count


def steps_of(count):
    short = list(range(1, count // 2))
    return short[:2] + list(range(max(1, count // 2), count)) + short[2:]


def head_columns(place, r, heads, h, head_count):
    col = (partner(place[1], r, heads) * head_count + h) * HEAD_DIM
    return pl.ds(pl.multiple_of(col, HEAD_DIM), HEAD_DIM)


def split_kernel(place, k_ref, v_ref, *refs):
    *outs, sem = refs
    heads, head_count = len(outs), outs[0].shape[0]
    copies = []
    for r, out in enumerate(outs):
        for h in range(head_count):
            cols = head_columns(place, r, heads, h, head_count)
            for kv, ref in enumerate((k_ref, v_ref)):
                at = (r * head_count + h) * 2 + kv
                copies.append(pltpu.make_async_copy(ref.at[:, cols], out.at[h, kv], sem.at[at]))
    for copy in copies:
        copy.start()
    for copy in copies:
        copy.wait()


def join_kernel(place, *refs, heads):
    *pieces, k_ref, v_ref, sem = refs
    head_count = len(pieces) // heads
    copies = []
    for at, piece in enumerate(pieces):
        cols = head_columns(place, at % heads, heads, at // heads, head_count)
        for kv, ref in enumerate((k_ref, v_ref)):
            copies.append(pltpu.make_async_copy(piece.at[kv], ref.at[:, cols], sem.at[2 * at + kv]))
    for copy in copies:
        copy.start()
    for copy in copies:
        copy.wait()


def fill_table(place, own, h, table):
    heads = len(own)
    per_quarter = own[0].shape[2] // BLK
    for r in range(heads):
        first = origin(place[1], r, heads) * per_quarter
        for kv in range(2):
            for j in range(per_quarter):
                table[kv, first + j] = own[r][h, kv, j * BLK : (j + 1) * BLK, :]


def pick(table, asked, there, out):
    for s in range(CAP):
        block = asked[there, s]
        for kv in range(2):
            out[kv, s] = table[kv, block]


def pick_kernel(place, asked, *refs, heads, steps, head, shard_count):
    own, outs, table = refs[:heads], refs[heads:-1], refs[-1]
    fill_table(place, own, head, table)
    for r, out in zip(steps, outs):
        pick(table, asked, partner(place[0], r, shard_count), out)


def by_head(ref, b):
    rows = slice(b * BLK, (b + 1) * BLK)
    return jnp.concatenate([ref[rows, g * HEAD_DIM : (g + 1) * HEAD_DIM] for g in range(GROUP)], axis=0)


def by_row(ref, b, x):
    rows = slice(b * BLK, (b + 1) * BLK)
    for g in range(GROUP):
        ref[rows, g * HEAD_DIM : (g + 1) * HEAD_DIM] = x[g * BLK : (g + 1) * BLK]


def attend_kernel(place, source, asked, q_ref, g_ref, *refs, heads, head, last, shard_count):
    steps = shard_count - 1
    own, far = refs[:heads], refs[heads : heads + steps]
    table, total = refs[-2:]
    outs = refs[-2 - steps : -2]
    o_ref, dq_ref, near_out = refs[-5 - steps : -2 - steps]
    step = pl.program_id(0)
    blocks_here = near_out.shape[1]

    @pl.when(step == 0)
    def _():
        fill_table(place, own, 0, table)
        for r, part in zip(steps_of(shard_count), far):
            first = blocks_here + origin(place[0], r, shard_count) * CAP
            for kv in range(2):
                for s in range(CAP):
                    table[kv, first + s] = part[kv, s]
        total[...] = jnp.zeros_like(total)

    key_row = lax.broadcasted_iota(jnp.int32, (BLK, GROUP * BLK), 0)
    query_col = lax.broadcasted_iota(jnp.int32, (BLK, GROUP * BLK), 1) % BLK
    hidden = key_row > query_col
    for first in range(0, STEP_BLOCKS, TOGETHER):
        subs = range(first, first + TOGETHER)
        listed = {b: [source[(step * STEP_BLOCKS + b) * LIST + e] for e in range(LIST)] for b in subs}
        q = {b: by_head(q_ref, b) for b in subs}
        g_out = {b: by_head(g_ref, b) for b in subs}
        keys = {b: jnp.concatenate([table[0, at] for at in listed[b]], axis=0) for b in subs}
        values = {b: jnp.concatenate([table[1, at] for at in listed[b]], axis=0) for b in subs}
        scores = {b: dot(keys[b], q[b], NT) for b in subs}
        dprob, probs, probs_low, dscore = {}, {}, {}, {}
        for b in subs:
            block = step * STEP_BLOCKS + b
            parts = []
            for e in range(LIST):
                mask = hidden if e == 0 else hidden & (listed[b][e] == block)
                parts.append(jnp.where(mask, NEG_FILL, scores[b][e * BLK : (e + 1) * BLK]))
            masked = jnp.concatenate(parts, axis=0)
            dprob[b] = dot(values[b], g_out[b], NT)
            peak = jnp.max(masked, axis=0, keepdims=True)
            expo = jnp.exp2((masked - peak) * (SCALE * LOG2E))
            probs[b] = expo * (1.0 / jnp.sum(expo, axis=0, keepdims=True))
            probs_low[b] = probs[b].astype(jnp.bfloat16)
        for b in subs:
            attended = dot(probs_low[b], values[b], TN).astype(jnp.bfloat16)
            by_row(o_ref, b, attended)
            dv = dot(probs_low[b], g_out[b], NN)
            delta = jnp.sum(probs[b] * dprob[b], axis=0, keepdims=True)
            dscore[b] = (probs[b] * (dprob[b] - delta)).astype(jnp.bfloat16)
            for e in range(LIST):
                total[1, listed[b][e]] += dv[e * BLK : (e + 1) * BLK]
        for b in subs:
            dq = (dot(dscore[b], keys[b], TN) * SCALE).astype(jnp.bfloat16)
            by_row(dq_ref, b, dq)
            dk = dot(dscore[b], q[b], NN)
            for e in range(LIST):
                total[0, listed[b][e]] += dk[e * BLK : (e + 1) * BLK]

    @pl.when(step == pl.num_programs(0) - 1)
    def _():
        for kv, factor in ((0, SCALE), (1, 1.0)):
            near_out[kv] = (total[kv, :blocks_here] * factor).astype(jnp.bfloat16)
        if not last:
            fill_table(place, own, 1, table)
        for r, out in zip(steps_of(shard_count), outs):
            there = partner(place[0], r, shard_count)

            @pl.when(there < place[0])
            def _():
                for kv, factor in ((0, SCALE), (1, 1.0)):
                    for s in range(CAP):
                        out[kv, s] = (total[kv, blocks_here + there * CAP + s] * factor).astype(jnp.bfloat16)

            @pl.when(there > place[0])
            def _():
                if last or r >= shard_count // 2:
                    out[...] = jnp.zeros_like(out)
                else:
                    pick(table, asked, there, out)


def gather_sum_kernel(place, asked, near, *refs, heads, shard_count):
    back, outs, total = refs[: -heads - 1], refs[-heads - 1 : -1], refs[-1]
    per_quarter = outs[0].shape[1] // BLK
    total[...] = near[...].astype(jnp.float32)
    for r, part in zip(steps_of(shard_count), back):
        there = origin(place[0], r, shard_count)

        @pl.when(there > place[0])
        def _():
            for s in range(CAP):
                block = asked[there, s]
                for kv in range(2):
                    total[kv, block] += part[kv, s].astype(jnp.float32)

    for r in range(heads):
        first = origin(place[1], r, heads) * per_quarter
        for kv in range(2):
            for j in range(per_quarter):
                outs[r][kv, j * BLK : (j + 1) * BLK, :] = total[kv, first + j].astype(jnp.bfloat16)


def whole(shape):
    return pl.BlockSpec(tuple(shape), lambda *_: (0,) * len(shape))


def heads_from(shape, head, count):
    return pl.BlockSpec((pl.Element(count), *(pl.Element(n) for n in shape[1:])), lambda *_: (head, *(0,) * (len(shape) - 1)))


ANYWHERE = pl.BlockSpec(memory_space=pl.ANY)


def bf16(*shape):
    return jax.ShapeDtypeStruct(shape, jnp.bfloat16)


def call(kernel, scalars, arrays, out_shapes, scratch, name, any_in=False, any_out=False, limit=VMEM_LIMIT):
    return pl.pallas_call(
        kernel,
        grid_spec=pltpu.PrefetchScalarGridSpec(
            num_scalar_prefetch=len(scalars),
            grid=(1,),
            in_specs=[ANYWHERE if any_in else whole(x.shape) for x in arrays],
            out_specs=[ANYWHERE if any_out else whole(x.shape) for x in out_shapes],
            scratch_shapes=scratch,
        ),
        out_shape=out_shapes,
        compiler_params=params(limit),
        name=name,
    )(*scalars, *arrays)


def attend(place, source, asked, queries, out_grad, own, far, head, last, earlier, shard_count):
    tokens_here, width = queries.shape
    blocks_here = tokens_here // BLK
    slots = blocks_here + shard_count * CAP
    tile = pl.BlockSpec((STEP_BLOCKS * BLK, GROUP * HEAD_DIM), lambda i, *_: (i, head))
    near_shape = (2, blocks_here, BLK, HEAD_DIM)
    arrays = [*own, *far]
    first = 5 + len(arrays)
    out_shapes = [bf16(2, CAP, BLK, HEAD_DIM)] * (shard_count - 1)
    return pl.pallas_call(
        functools.partial(
            attend_kernel, heads=len(own), head=head, last=last, shard_count=shard_count
        ),
        grid_spec=pltpu.PrefetchScalarGridSpec(
            num_scalar_prefetch=3,
            grid=(blocks_here // STEP_BLOCKS,),
            in_specs=[tile, tile]
            + [heads_from(x.shape, head, 1 if last else 2) for x in own]
            + [whole(x.shape) for x in far]
            + [ANYWHERE] * len(earlier),
            out_specs=[tile, tile, whole(near_shape)] + [whole(x.shape) for x in out_shapes],
            scratch_shapes=[
                pltpu.VMEM((2, slots, BLK, HEAD_DIM), jnp.bfloat16),
                pltpu.VMEM((2, slots, BLK, HEAD_DIM), jnp.float32),
            ],
        ),
        out_shape=[bf16(tokens_here, width), bf16(tokens_here, width), bf16(*near_shape)]
        + out_shapes,
        input_output_aliases={first: 0, first + 1: 1} if earlier else {},
        compiler_params=params(),
        cost_estimate=pl.CostEstimate(
            flops=12 * blocks_here * LIST * BLK * GROUP * BLK * HEAD_DIM,
            bytes_accessed=20 * 1024 * 1024,
            transcendentals=blocks_here * LIST * BLK * GROUP * BLK,
        ),
        name="attend",
    )(place, source, asked, queries, out_grad, *arrays, *earlier)


def send(x, axis, count, r):
    return lax.ppermute(x, axis, [(i, partner(i, r, count)) for i in range(count)])


def send_back(x, axis, count, r):
    return lax.ppermute(x, axis, [(i, origin(i, r, count)) for i in range(count)])


def requests_of(flat_ids, blocks_here, shard_index, shard_count):
    owner = flat_ids // blocks_here
    shards = jnp.arange(shard_count, dtype=jnp.int32)
    inner = jnp.arange(blocks_here, dtype=jnp.int32)
    every_block = jnp.arange(shard_count * blocks_here, dtype=jnp.int32)
    listed = jnp.any(flat_ids[:, None] == every_block[None, :], axis=0)
    grid = listed.reshape(shard_count, blocks_here) & (shards != shard_index)[:, None]
    rank = jnp.sum((grid[:, :, None] & (inner[:, None] < inner[None, :])[None]).astype(jnp.int32), axis=1)
    hit = grid[:, None] & (rank[:, None] == jnp.arange(128, dtype=jnp.int32)[None, :, None])
    requests = jnp.sum(jnp.where(hit, inner[None, None], 0), axis=2)
    same_owner = owner[:, None] == (every_block // blocks_here)[None, :]
    place_of = jnp.sum((same_owner & listed[None, :] & (every_block[None, :] < flat_ids[:, None])).astype(jnp.int32), axis=1)
    source = jnp.where(owner == shard_index, flat_ids % blocks_here, blocks_here + owner * CAP + place_of)
    return requests, source


def after(x, *others):
    return lax.optimization_barrier((x, *others))[0]


def per_device(queries, key_states, value_states, block_lists, out_grad):
    shard_index = lax.axis_index("ctx")
    shard_count = lax.axis_size("ctx")
    heads = lax.axis_size("head")
    blocks_here = queries.shape[0] // BLK
    quarter = key_states.shape[0]
    head_count = key_states.shape[1] // heads // HEAD_DIM
    place = jnp.stack([shard_index, lax.axis_index("head")]).astype(jnp.int32)

    pieces = call(
        split_kernel,
        [place],
        [key_states, value_states],
        [bf16(head_count, 2, quarter, HEAD_DIM)] * heads,
        [pltpu.SemaphoreType.DMA((2 * heads * head_count,))],
        "split",
        any_in=True,
        limit=VMEM_MOST,
    )
    own = [pieces[0]] + [send(pieces[r], "head", heads, r) for r in range(1, heads)]

    requests, source = requests_of(after(block_lists, *own[1:2]).reshape(-1), blocks_here, shard_index, shard_count)
    asked = lax.all_to_all(requests, "ctx", split_axis=0, concat_axis=0, tiled=True)

    steps = steps_of(shard_count)
    wide = [r for r in steps if r >= shard_count // 2]

    def exchange(arrays):
        return {r: send(x, "ctx", shard_count, r) for r, x in arrays}

    def picked(head, steps):
        arrays = call(
            functools.partial(pick_kernel, heads=heads, steps=steps, head=head, shard_count=shard_count),
            [place, asked],
            own,
            [bf16(2, CAP, BLK, HEAD_DIM)] * len(steps),
            [pltpu.VMEM((2, blocks_here, BLK, HEAD_DIM), jnp.bfloat16)],
            "pick",
        )
        return list(zip(steps, arrays))

    come, earlier, nears, backs = exchange(picked(0, steps)), [], [], []
    for h in range(head_count):
        last = h == head_count - 1
        ahead = {}
        if not last:
            ahead = exchange([(r, after(x, *come.values())) for r, x in picked(h + 1, wide)])
        attended, query_grad, near, *go = attend(
            place, source, asked, queries, out_grad, own, [come[r] for r in steps], h, last, earlier, shard_count
        )
        earlier = [attended, query_grad]
        nears.append(near)
        back = exchange(zip(steps, go))
        backs.append([back[r] for r in steps])
        come = {**back, **ahead}
    done = []
    for h in range(head_count):
        sums = call(
            functools.partial(gather_sum_kernel, heads=heads, shard_count=shard_count),
            [place, asked],
            [after(nears[h], nears[-1], *done[-1:]), *backs[h]],
            [bf16(2, quarter, HEAD_DIM)] * heads,
            [pltpu.VMEM((2, blocks_here, BLK, HEAD_DIM), jnp.float32)],
            "gather_sum",
        )
        done += [sums[0]] + [send_back(sums[r], "head", heads, r) for r in range(1, heads)]
    key_grad, value_grad = call(
        functools.partial(join_kernel, heads=heads),
        [place],
        done,
        [bf16(*key_states.shape)] * 2,
        [pltpu.SemaphoreType.DMA((2 * heads * head_count,))],
        "join",
        any_in=True,
        any_out=True,
    )
    return attended, query_grad, key_grad, value_grad


def solution(mesh):
    return jax.shard_map(
        per_device,
        mesh=mesh,
        in_specs=(
            P("ctx", "head"),
            P(("ctx", "head"), None),
            P(("ctx", "head"), None),
            P("ctx", None),
            P("ctx", "head"),
        ),
        out_specs=(
            P("ctx", "head"),
            P("ctx", "head"),
            P(("ctx", "head"), None),
            P(("ctx", "head"), None),
        ),
        check_vma=False,
    )
```

```python
import functools

import jax
import jax.numpy as jnp
from jax import lax
from jax.experimental import pallas as pl
from jax.experimental.pallas import tpu as pltpu
from jax.sharding import PartitionSpec as P

HEAD_DIM = 128
GROUP = 4
BLK = 64
LIST = 8
CAP = 3
STEP_BLOCKS = 4
TOGETHER = 4
NEG_FILL = -1e30
SCALE = HEAD_DIM ** (-0.5)
LOG2E = 1.4426950408889634
VMEM_LIMIT = 50 * 1024 * 1024
VMEM_MOST = 60 * 1024 * 1024

NT = (((1,), (1,)), ((), ()))
NN = (((1,), (0,)), ((), ()))
TN = (((0,), (0,)), ((), ()))


def dot(a, b, dims):
    return lax.dot_general(a, b, dims, preferred_element_type=jnp.float32)


def params(limit=VMEM_LIMIT):
    return pltpu.CompilerParams(vmem_limit_bytes=limit)


def partner(me, r, count):
    return me ^ r if count & (count - 1) == 0 else (me + r) % count


def origin(me, r, count):
    return me ^ r if count & (count - 1) == 0 else (me + count - r) % count


def steps_of(count):
    short = list(range(1, count // 2))
    return short[:2] + list(range(max(1, count // 2), count)) + short[2:]


def head_columns(place, r, heads, h, head_count):
    col = (partner(place[1], r, heads) * head_count + h) * HEAD_DIM
    return pl.ds(pl.multiple_of(col, HEAD_DIM), HEAD_DIM)


def split_kernel(place, k_ref, v_ref, *refs):
    *outs, sem = refs
    heads, head_count = len(outs), outs[0].shape[0]
    copies = []
    for r, out in enumerate(outs):
        for h in range(head_count):
            cols = head_columns(place, r, heads, h, head_count)
            for kv, ref in enumerate((k_ref, v_ref)):
                at = (r * head_count + h) * 2 + kv
                copies.append(pltpu.make_async_copy(ref.at[:, cols], out.at[h, kv], sem.at[at]))
    for copy in copies:
        copy.start()
    for copy in copies:
        copy.wait()


def join_kernel(place, *refs, heads):
    *pieces, k_ref, v_ref, sem = refs
    head_count = len(pieces) // heads
    copies = []
    for at, piece in enumerate(pieces):
        cols = head_columns(place, at % heads, heads, at // heads, head_count)
        for kv, ref in enumerate((k_ref, v_ref)):
            copies.append(pltpu.make_async_copy(piece.at[kv], ref.at[:, cols], sem.at[2 * at + kv]))
    for copy in copies:
        copy.start()
    for copy in copies:
        copy.wait()


def fill_table(place, own, h, table):
    heads = len(own)
    per_quarter = own[0].shape[2] // BLK
    for r in range(heads):
        first = origin(place[1], r, heads) * per_quarter
        for kv in range(2):
            for j in range(per_quarter):
                table[kv, first + j] = own[r][h, kv, j * BLK : (j + 1) * BLK, :]


def pick(table, asked, there, out):
    for s in range(CAP):
        block = asked[there, s]
        for kv in range(2):
            out[kv, s] = table[kv, block]


def pick_kernel(place, asked, *refs, heads, steps, head, shard_count):
    own, outs, table = refs[:heads], refs[heads:-1], refs[-1]
    fill_table(place, own, head, table)
    for r, out in zip(steps, outs):
        pick(table, asked, partner(place[0], r, shard_count), out)


def by_head(ref, b):
    rows = slice(b * BLK, (b + 1) * BLK)
    return jnp.concatenate([ref[rows, g * HEAD_DIM : (g + 1) * HEAD_DIM] for g in range(GROUP)], axis=0)


def beside(turned, kv, listed):
    left = lax.broadcasted_iota(jnp.int32, (HEAD_DIM, 2 * BLK), 1) < BLK
    pairs = zip(listed[::2], listed[1::2])
    return jnp.concatenate([jnp.where(left, turned[kv, a], turned[kv, b]) for a, b in pairs], axis=1)


def by_row(ref, b, x):
    rows = slice(b * BLK, (b + 1) * BLK)
    for g in range(GROUP):
        ref[rows, g * HEAD_DIM : (g + 1) * HEAD_DIM] = x[g * BLK : (g + 1) * BLK]


def attend_kernel(place, source, asked, q_ref, g_ref, *refs, heads, head, last, shard_count):
    steps = shard_count - 1
    own, far = refs[:heads], refs[heads : heads + steps]
    table, turned, total = refs[-3:]
    outs = refs[-3 - steps : -3]
    o_ref, dq_ref, near_out = refs[-6 - steps : -3 - steps]
    step = pl.program_id(0)
    blocks_here = near_out.shape[1]

    @pl.when(step == 0)
    def _():
        fill_table(place, own, 0, table)
        for r, part in zip(steps_of(shard_count), far):
            first = blocks_here + origin(place[0], r, shard_count) * CAP
            for kv in range(2):
                for s in range(CAP):
                    table[kv, first + s] = part[kv, s]
        for kv in range(2):
            for slot in range(table.shape[1]):
                block = table[kv, slot].T
                turned[kv, slot] = jnp.concatenate([block, block], axis=1)
        total[...] = jnp.zeros_like(total)

    key_row = lax.broadcasted_iota(jnp.int32, (BLK, GROUP * BLK), 0)
    query_col = lax.broadcasted_iota(jnp.int32, (BLK, GROUP * BLK), 1) % BLK
    hidden = key_row > query_col
    for first in range(0, STEP_BLOCKS, TOGETHER):
        subs = range(first, first + TOGETHER)
        listed = {b: [source[(step * STEP_BLOCKS + b) * LIST + e] for e in range(LIST)] for b in subs}
        q = {b: by_head(q_ref, b) for b in subs}
        g_out = {b: by_head(g_ref, b) for b in subs}
        keys = {b: jnp.concatenate([table[0, at] for at in listed[b]], axis=0) for b in subs}
        values = {b: jnp.concatenate([table[1, at] for at in listed[b]], axis=0) for b in subs}
        scores = {b: dot(keys[b], q[b], NT) for b in subs}
        dprob, probs, probs_low, dscore = {}, {}, {}, {}
        for b in subs:
            block = step * STEP_BLOCKS + b
            parts = []
            for e in range(LIST):
                mask = hidden if e == 0 else hidden & (listed[b][e] == block)
                parts.append(jnp.where(mask, NEG_FILL, scores[b][e * BLK : (e + 1) * BLK]))
            masked = jnp.concatenate(parts, axis=0)
            dprob[b] = dot(values[b], g_out[b], NT)
            peak = jnp.max(masked, axis=0, keepdims=True)
            expo = jnp.exp2((masked - peak) * (SCALE * LOG2E))
            probs[b] = expo * (1.0 / jnp.sum(expo, axis=0, keepdims=True))
            probs_low[b] = probs[b].astype(jnp.bfloat16)
        for b in subs:
            attended = dot(beside(turned, 1, listed[b]), probs_low[b], NN).astype(jnp.bfloat16).T
            by_row(o_ref, b, attended)
            dv = dot(probs_low[b], g_out[b], NN)
            delta = jnp.sum(probs[b] * dprob[b], axis=0, keepdims=True)
            dscore[b] = (probs[b] * (dprob[b] - delta)).astype(jnp.bfloat16)
            for e in range(LIST):
                total[1, listed[b][e]] += dv[e * BLK : (e + 1) * BLK]
        for b in subs:
            dq = (dot(beside(turned, 0, listed[b]), dscore[b], NN) * SCALE).astype(jnp.bfloat16).T
            by_row(dq_ref, b, dq)
            dk = dot(dscore[b], q[b], NN)
            for e in range(LIST):
                total[0, listed[b][e]] += dk[e * BLK : (e + 1) * BLK]

    @pl.when(step == pl.num_programs(0) - 1)
    def _():
        for kv, factor in ((0, SCALE), (1, 1.0)):
            near_out[kv] = (total[kv, :blocks_here] * factor).astype(jnp.bfloat16)
        if not last:
            fill_table(place, own, 1, table)
        for r, out in zip(steps_of(shard_count), outs):
            there = partner(place[0], r, shard_count)

            @pl.when(there < place[0])
            def _():
                for kv, factor in ((0, SCALE), (1, 1.0)):
                    for s in range(CAP):
                        out[kv, s] = (total[kv, blocks_here + there * CAP + s] * factor).astype(jnp.bfloat16)

            @pl.when(there > place[0])
            def _():
                if last or r >= shard_count // 2:
                    out[...] = jnp.zeros_like(out)
                else:
                    pick(table, asked, there, out)


def gather_sum_kernel(place, asked, near, *refs, heads, shard_count):
    back, outs, total = refs[: -heads - 1], refs[-heads - 1 : -1], refs[-1]
    per_quarter = outs[0].shape[1] // BLK
    total[...] = near[...].astype(jnp.float32)
    for r, part in zip(steps_of(shard_count), back):
        there = origin(place[0], r, shard_count)

        @pl.when(there > place[0])
        def _():
            for s in range(CAP):
                block = asked[there, s]
                for kv in range(2):
                    total[kv, block] += part[kv, s].astype(jnp.float32)

    for r in range(heads):
        first = origin(place[1], r, heads) * per_quarter
        for kv in range(2):
            for j in range(per_quarter):
                outs[r][kv, j * BLK : (j + 1) * BLK, :] = total[kv, first + j].astype(jnp.bfloat16)


def whole(shape):
    return pl.BlockSpec(tuple(shape), lambda *_: (0,) * len(shape))


def heads_from(shape, head, count):
    return pl.BlockSpec((pl.Element(count), *(pl.Element(n) for n in shape[1:])), lambda *_: (head, *(0,) * (len(shape) - 1)))


ANYWHERE = pl.BlockSpec(memory_space=pl.ANY)


def bf16(*shape):
    return jax.ShapeDtypeStruct(shape, jnp.bfloat16)


def call(kernel, scalars, arrays, out_shapes, scratch, name, any_in=False, any_out=False, limit=VMEM_LIMIT):
    return pl.pallas_call(
        kernel,
        grid_spec=pltpu.PrefetchScalarGridSpec(
            num_scalar_prefetch=len(scalars),
            grid=(1,),
            in_specs=[ANYWHERE if any_in else whole(x.shape) for x in arrays],
            out_specs=[ANYWHERE if any_out else whole(x.shape) for x in out_shapes],
            scratch_shapes=scratch,
        ),
        out_shape=out_shapes,
        compiler_params=params(limit),
        name=name,
    )(*scalars, *arrays)


def attend(place, source, asked, queries, out_grad, own, far, head, last, earlier, shard_count):
    tokens_here, width = queries.shape
    blocks_here = tokens_here // BLK
    slots = blocks_here + shard_count * CAP
    tile = pl.BlockSpec((STEP_BLOCKS * BLK, GROUP * HEAD_DIM), lambda i, *_: (i, head))
    near_shape = (2, blocks_here, BLK, HEAD_DIM)
    arrays = [*own, *far]
    first = 5 + len(arrays)
    out_shapes = [bf16(2, CAP, BLK, HEAD_DIM)] * (shard_count - 1)
    return pl.pallas_call(
        functools.partial(
            attend_kernel, heads=len(own), head=head, last=last, shard_count=shard_count
        ),
        grid_spec=pltpu.PrefetchScalarGridSpec(
            num_scalar_prefetch=3,
            grid=(blocks_here // STEP_BLOCKS,),
            in_specs=[tile, tile]
            + [heads_from(x.shape, head, 1 if last else 2) for x in own]
            + [whole(x.shape) for x in far]
            + [ANYWHERE] * len(earlier),
            out_specs=[tile, tile, whole(near_shape)] + [whole(x.shape) for x in out_shapes],
            scratch_shapes=[
                pltpu.VMEM((2, slots, BLK, HEAD_DIM), jnp.bfloat16),
                pltpu.VMEM((2, slots, HEAD_DIM, 2 * BLK), jnp.bfloat16),
                pltpu.VMEM((2, slots, BLK, HEAD_DIM), jnp.float32),
            ],
        ),
        out_shape=[bf16(tokens_here, width), bf16(tokens_here, width), bf16(*near_shape)]
        + out_shapes,
        input_output_aliases={first: 0, first + 1: 1} if earlier else {},
        compiler_params=params(),
        cost_estimate=pl.CostEstimate(
            flops=12 * blocks_here * LIST * BLK * GROUP * BLK * HEAD_DIM,
            bytes_accessed=20 * 1024 * 1024,
            transcendentals=blocks_here * LIST * BLK * GROUP * BLK,
        ),
        name="attend",
    )(place, source, asked, queries, out_grad, *arrays, *earlier)


def send(x, axis, count, r):
    return lax.ppermute(x, axis, [(i, partner(i, r, count)) for i in range(count)])


def send_back(x, axis, count, r):
    return lax.ppermute(x, axis, [(i, origin(i, r, count)) for i in range(count)])


def requests_of(flat_ids, blocks_here, shard_index, shard_count):
    owner = flat_ids // blocks_here
    shards = jnp.arange(shard_count, dtype=jnp.int32)
    inner = jnp.arange(blocks_here, dtype=jnp.int32)
    every_block = jnp.arange(shard_count * blocks_here, dtype=jnp.int32)
    listed = jnp.any(flat_ids[:, None] == every_block[None, :], axis=0)
    grid = listed.reshape(shard_count, blocks_here) & (shards != shard_index)[:, None]
    rank = jnp.sum((grid[:, :, None] & (inner[:, None] < inner[None, :])[None]).astype(jnp.int32), axis=1)
    hit = grid[:, None] & (rank[:, None] == jnp.arange(128, dtype=jnp.int32)[None, :, None])
    requests = jnp.sum(jnp.where(hit, inner[None, None], 0), axis=2)
    same_owner = owner[:, None] == (every_block // blocks_here)[None, :]
    place_of = jnp.sum((same_owner & listed[None, :] & (every_block[None, :] < flat_ids[:, None])).astype(jnp.int32), axis=1)
    source = jnp.where(owner == shard_index, flat_ids % blocks_here, blocks_here + owner * CAP + place_of)
    return requests, source


def after(x, *others):
    return lax.optimization_barrier((x, *others))[0]


def per_device(queries, key_states, value_states, block_lists, out_grad):
    shard_index = lax.axis_index("ctx")
    shard_count = lax.axis_size("ctx")
    heads = lax.axis_size("head")
    blocks_here = queries.shape[0] // BLK
    quarter = key_states.shape[0]
    head_count = key_states.shape[1] // heads // HEAD_DIM
    place = jnp.stack([shard_index, lax.axis_index("head")]).astype(jnp.int32)

    pieces = call(
        split_kernel,
        [place],
        [key_states, value_states],
        [bf16(head_count, 2, quarter, HEAD_DIM)] * heads,
        [pltpu.SemaphoreType.DMA((2 * heads * head_count,))],
        "split",
        any_in=True,
        limit=VMEM_MOST,
    )
    own = [pieces[0]] + [send(pieces[r], "head", heads, r) for r in range(1, heads)]

    requests, source = requests_of(after(block_lists, *own[1:2]).reshape(-1), blocks_here, shard_index, shard_count)
    asked = lax.all_to_all(requests, "ctx", split_axis=0, concat_axis=0, tiled=True)

    steps = steps_of(shard_count)
    wide = [r for r in steps if r >= shard_count // 2]

    def exchange(arrays):
        return {r: send(x, "ctx", shard_count, r) for r, x in arrays}

    def picked(head, steps):
        arrays = call(
            functools.partial(pick_kernel, heads=heads, steps=steps, head=head, shard_count=shard_count),
            [place, asked],
            own,
            [bf16(2, CAP, BLK, HEAD_DIM)] * len(steps),
            [pltpu.VMEM((2, blocks_here, BLK, HEAD_DIM), jnp.bfloat16)],
            "pick",
        )
        return list(zip(steps, arrays))

    come, earlier, nears, backs = exchange(picked(0, steps)), [], [], []
    for h in range(head_count):
        last = h == head_count - 1
        ahead = {}
        if not last:
            ahead = exchange([(r, after(x, *come.values())) for r, x in picked(h + 1, wide)])
        attended, query_grad, near, *go = attend(
            place, source, asked, queries, out_grad, own, [come[r] for r in steps], h, last, earlier, shard_count
        )
        earlier = [attended, query_grad]
        nears.append(near)
        back = exchange(zip(steps, go))
        backs.append([back[r] for r in steps])
        come = {**back, **ahead}
    done = []
    for h in range(head_count):
        sums = call(
            functools.partial(gather_sum_kernel, heads=heads, shard_count=shard_count),
            [place, asked],
            [after(nears[h], nears[-1], *done[-1:]), *backs[h]],
            [bf16(2, quarter, HEAD_DIM)] * heads,
            [pltpu.VMEM((2, blocks_here, BLK, HEAD_DIM), jnp.float32)],
            "gather_sum",
        )
        done += [sums[0]] + [send_back(sums[r], "head", heads, r) for r in range(1, heads)]
    key_grad, value_grad = call(
        functools.partial(join_kernel, heads=heads),
        [place],
        done,
        [bf16(*key_states.shape)] * 2,
        [pltpu.SemaphoreType.DMA((2 * heads * head_count,))],
        "join",
        any_in=True,
        any_out=True,
    )
    return attended, query_grad, key_grad, value_grad


def solution(mesh):
    return jax.shard_map(
        per_device,
        mesh=mesh,
        in_specs=(
            P("ctx", "head"),
            P(("ctx", "head"), None),
            P(("ctx", "head"), None),
            P("ctx", None),
            P("ctx", "head"),
        ),
        out_specs=(
            P("ctx", "head"),
            P("ctx", "head"),
            P(("ctx", "head"), None),
            P(("ctx", "head"), None),
        ),
        check_vma=False,
    )
```
